32 devices in a mesh: emb: 16 (over z, y, x), bal: 2 (over core).
Axes of the slice: x: 2, y: 2, z: 4, core: 2. Of those that a mesh axis runs over, the one named last changes fastest.
Arguments:
- item_ids: int32 [2, 4096, 4], P('bal'), may hold values from 0 to 1023
- seq_lengths: int32 [2, 16, 2], P(None, 'emb'), may hold values from 1 to 128, as said below
- surplus_slot: int32 [2, 16], P(None, 'emb'), may hold values from 0 to 1
- helper_map: int32 [2, 16], P(None, 'emb'), may hold values from 0 to 1, as said below
- embed_tables: bfloat16 [16, 1024, 128], P('emb'), may hold values from -3 to 3
- weight_in: bfloat16 [512, 2048], P('bal'), may hold values from -0.25 to 0.25
- weight_out: bfloat16 [512, 512], P('bal'), may hold values from -0.25 to 0.25
- cotangent: bfloat16 [2, 4096, 512], P('bal', 'emb'), may hold values from -6 to 6
Outputs:
- layer_out: bfloat16 [2, 4096, 512], P('bal', 'emb')
- table_grad: float32 [16, 1024, 128], P('emb', 'bal')
- grad_in: float32 [512, 2048], P('bal')
- grad_out: float32 [512, 512], P('bal')
The draws below stay inside these ranges and needn't reach their ends.
Inputs may be any that keep to these rules, and one draw needn't show every extreme that they name: `seq_lengths`: some slot has 128 live events. Each column helper_map[:, e] is a permutation of the bal indices.
All inputs are finite; a program needn't handle non-finite values.
Results may differ from the reference program's by a relative error of at most 0.014.
Values may be sent and summed in bfloat16 or wider, within the bound.
No kernel may reach another device: no remote copies, remote signals or barrier semaphores. Data moves between devices by JAX's collectives and lax.ppermute only.
A program may use at most 64 MiB of HBM per device.

```python
import math
import jax
import jax.numpy as jnp
import numpy as np
from jax import lax

D = 512
HEADS = 8
F1 = 2048
COLS = 128
TABLES = 4
DISTINCT = 1024
SLOT = 128
NSEQ = 2
ROWS_DEV = 256
EMB_ROWS = 4096
EVENTS = 8192
N_EMB = 16
N_BAL = 2


def draw_seq_lengths(key, part):
    base_key = jax.random.fold_in(key, 101)
    first_key, second_key = jax.random.split(base_key)
    drawn = jax.random.randint(first_key, (N_BAL * N_EMB * NSEQ,), 0, SLOT, dtype=jnp.int32)
    lengths = 1 + drawn * drawn // SLOT
    position = jax.random.randint(second_key, (), 0, N_BAL * N_EMB * NSEQ, dtype=jnp.int32)
    lengths = lengths.at[position].set(SLOT)
    return lengths.reshape(N_BAL, N_EMB, NSEQ).astype(jnp.int32)


def draw_helper_map(key, part):
    base_key = jax.random.fold_in(key, 202)
    column_keys = jax.random.split(base_key, N_EMB)
    orders = jax.vmap(lambda column_key: jax.random.permutation(column_key, N_BAL))(column_keys)
    return jnp.transpose(orders).astype(jnp.int32)


def touch_ends(entries, rng, least, high):
    shape = entries.shape
    index_at = [jax.random.randint(jax.random.fold_in(rng, axis), (), 0, shape[axis]) for axis in range(len(shape))]
    entries = entries.at[tuple(index_at)].set(least)
    longest = shape.index(max(shape))
    index_at[longest] = (index_at[longest] + 1) % shape[longest]
    return entries.at[tuple(index_at)].set(high)


def block_scale(stream_key, dims, cuts, least, top_value):
    level, own = 1.0, jax.random.fold_in(stream_key, 6)
    for dim, parts in cuts:
        draws = jnp.exp(jax.random.uniform(jax.random.fold_in(own, dim), (parts,), jnp.float32, least / len(cuts), top_value / len(cuts)))
        level = level * jnp.repeat(draws, dims[dim] // parts).reshape([-1 if axis == dim else 1 for axis in range(len(dims))])
    return level


def rank_bounds(count, skew):
    portions = [(1 << 20) // math.isqrt(standing ** skew) + 1 for standing in range(1, count + 1)]
    spread = 1 + sum(portions) // (1 << 30)
    return np.cumsum(np.array([max(1, weight // spread) for weight in portions]))


def skewed_ids(rng, shape, amount, slope):
    grid = rank_bounds(amount, slope)
    lot = jax.random.randint(jax.random.fold_in(rng, 1), shape, 0, int(grid[amount - 1]))
    rank = jnp.searchsorted(jnp.asarray(grid, jnp.int32), lot, side="right")
    return jax.random.permutation(jax.random.fold_in(rng, 2), amount)[rank].astype(jnp.int32)


def bell_draw(key, shape, spread, reach, shards=(), held_as=jnp.bfloat16):
    loudness = block_scale(key, shape, shards, -0.22, 0.18) if shards else 1.0
    result = jax.random.normal(key, shape, jnp.float32) * spread * loudness
    return jnp.minimum(jnp.maximum(result, -reach), reach).astype(held_as)


def setup_inputs(seed: int = 0) -> dict:
    key_list = jax.random.split(jax.random.key(seed), 9)
    return {
        "item_ids": touch_ends(skewed_ids(key_list[0], (N_BAL, EMB_ROWS, TABLES), DISTINCT, 1), jax.random.fold_in(key_list[0], 3), 0, DISTINCT - 1).astype(jnp.int32),
        "seq_lengths": draw_seq_lengths(jax.random.fold_in(key_list[8], 71), 0),
        "surplus_slot": touch_ends(jax.random.randint(key_list[2], (N_BAL, N_EMB), 0, NSEQ), jax.random.fold_in(key_list[2], 1), 0, NSEQ - 1).astype(jnp.int32),
        "helper_map": draw_helper_map(jax.random.fold_in(key_list[8], 71), 0),
        "embed_tables": bell_draw(key_list[4], (N_EMB, DISTINCT, COLS), (TABLES ** -0.5), 3.0, ((0, 16),)),
        "weight_in": bell_draw(key_list[5], (D, F1), D ** -0.5, 0.25, ((0, 2),)),
        "weight_out": bell_draw(key_list[6], (D, D), D ** -0.5, 0.25, ((0, 2),)),
        "cotangent": bell_draw(key_list[7], (N_BAL, EMB_ROWS, D), 1.0, 6.0, ((0, 2), (1, 16))),
    }


EPS = 1e-05

def silu_grad(argument):
    logistic = jax.nn.sigmoid(argument)
    return logistic * (1.0 + argument * (1.0 - logistic))

def seq_mask(lengths, row_count, slot_rows):
    position = jnp.arange(row_count, dtype=jnp.int32)
    slot_of = position // slot_rows
    within = position - slot_of * slot_rows
    slot_ids = jnp.arange(lengths.shape[0], dtype=jnp.int32)
    row_length = lax.optimization_barrier(jnp.sum(jnp.where(slot_of[:, None] == slot_ids[None, :], lengths[None, :], 0), axis=1))
    same_slot = slot_of[:, None] == slot_of[None, :]
    causal = position[None, :] <= position[:, None]
    live = within[:, None] < row_length[:, None]
    return jnp.where(same_slot & causal & live, 1.0, 0.0).astype(jnp.float32)

def normalize(values):
    average = lax.optimization_barrier(jnp.mean(values, axis=1, keepdims=True))
    centred = values - average
    inverse = lax.rsqrt(lax.optimization_barrier(jnp.mean(centred * centred, axis=1, keepdims=True)) + EPS)
    return (centred * inverse, inverse)

def norm_back(incoming, normed, inverse):
    first = lax.optimization_barrier(jnp.mean(incoming, axis=1, keepdims=True))
    second = lax.optimization_barrier(jnp.mean(incoming * normed, axis=1, keepdims=True))
    return inverse * (incoming - first - normed * second)

def head_slices(heads_input, head_index, head_width, model_width):
    head_values = lax.dynamic_slice_in_dim(heads_input, head_index * head_width, head_width, 1)
    head_query = lax.dynamic_slice_in_dim(heads_input, model_width + head_index * head_width, head_width, 1)
    head_keys = lax.dynamic_slice_in_dim(heads_input, 2 * model_width + head_index * head_width, head_width, 1)
    return (head_values, head_query, head_keys)

def head_forward(heads_input, allowed, head_index, head_width, model_width, seq_bound):
    head_values, head_query, head_keys = head_slices(heads_input, head_index, head_width, model_width)
    scores = jnp.dot(head_query, head_keys.T, preferred_element_type=jnp.float32) * head_width ** (-0.5)
    silu_weights = (jax.nn.silu(scores) * allowed / seq_bound).astype(jnp.bfloat16)
    return jnp.dot(silu_weights, head_values, preferred_element_type=jnp.float32)

def head_backward(heads_input, allowed, grad_attended, head_index, head_width, model_width, seq_bound):
    head_values, head_query, head_keys = head_slices(heads_input, head_index, head_width, model_width)
    score_scale = head_width ** (-0.5)
    scores = jnp.dot(head_query, head_keys.T, preferred_element_type=jnp.float32) * score_scale
    silu_weights = (jax.nn.silu(scores) * allowed / seq_bound).astype(jnp.bfloat16)
    grad_head = lax.dynamic_slice_in_dim(grad_attended, head_index * head_width, head_width, 1)
    grad_weights = jnp.dot(grad_head, head_values.T, preferred_element_type=jnp.float32)
    grad_values = jnp.dot(silu_weights.T, grad_head, preferred_element_type=jnp.float32)
    grad_scores = (grad_weights * allowed / seq_bound * silu_grad(scores)).astype(jnp.bfloat16)
    grad_query = jnp.dot(grad_scores, head_keys, preferred_element_type=jnp.float32) * score_scale
    grad_keys = jnp.dot(grad_scores.T, head_query, preferred_element_type=jnp.float32) * score_scale
    return (grad_values, grad_query, grad_keys)

def join_heads(stacked):
    head_count, row_count, head_width = stacked.shape
    return jnp.transpose(stacked, (1, 0, 2)).reshape(row_count, head_count * head_width)

def layer_forward(inputs, lengths, weight_in, weight_out, head_count, slot_rows):
    row_count, model_width = inputs.shape
    head_width = model_width // head_count
    seq_bound = slot_rows
    allowed = seq_mask(lengths, row_count, slot_rows)
    normed_in, in_inverse = normalize(inputs.astype(jnp.float32))
    normed_half = normed_in.astype(jnp.bfloat16)
    projected = jnp.dot(normed_half, weight_in, preferred_element_type=jnp.float32)
    activated = jax.nn.silu(projected)
    gate_rows = activated[:, :model_width]
    heads_input = activated[:, model_width:].astype(jnp.bfloat16)
    head_ids = jnp.arange(head_count, dtype=jnp.int32)
    attended = lax.map(lambda head_index: head_forward(heads_input, allowed, head_index, head_width, model_width, seq_bound), head_ids)
    normed_out, out_inverse = normalize(join_heads(attended))
    mixed_rows = (normed_out * gate_rows).astype(jnp.bfloat16)
    forward_out = (inputs.astype(jnp.float32) + jnp.dot(mixed_rows, weight_out, preferred_element_type=jnp.float32)).astype(jnp.bfloat16)
    stored = (allowed, normed_in, in_inverse, normed_half, projected, gate_rows, heads_input, normed_out, out_inverse, mixed_rows)
    return (forward_out, stored)

def layer_backward(stored, cotangent, weight_in, weight_out, head_count, slot_rows):
    allowed, normed_in, in_inverse, normed_half, projected, gate_rows, heads_input, normed_out, out_inverse, mixed_rows = stored
    row_count, model_width = normed_in.shape
    head_width = model_width // head_count
    seq_bound = slot_rows
    partial_out = jnp.dot(mixed_rows.T, cotangent, preferred_element_type=jnp.float32)
    grad_mixed = jnp.dot(cotangent, weight_out.T, preferred_element_type=jnp.float32)
    grad_gate = grad_mixed * normed_out
    grad_attended = norm_back(grad_mixed * gate_rows, normed_out, out_inverse).astype(jnp.bfloat16)
    head_ids = jnp.arange(head_count, dtype=jnp.int32)
    head_grads = lax.map(lambda head_index: head_backward(heads_input, allowed, grad_attended, head_index, head_width, model_width, seq_bound), head_ids)
    grad_heads = jnp.concatenate([join_heads(head_grads[0]), join_heads(head_grads[1]), join_heads(head_grads[2])], axis=1)
    grad_projected = (jnp.concatenate([grad_gate, grad_heads], axis=1) * silu_grad(projected)).astype(jnp.bfloat16)
    partial_in = jnp.dot(normed_half.T, grad_projected, preferred_element_type=jnp.float32)
    grad_normed = jnp.dot(grad_projected, weight_in.T, preferred_element_type=jnp.float32)
    grad_rows = (cotangent.astype(jnp.float32) + norm_back(grad_normed, normed_in, in_inverse)).astype(jnp.bfloat16)
    return (grad_rows, partial_in, partial_out)

def reference(item_ids, seq_lengths, surplus_slot, helper_map, embed_tables, weight_in, weight_out, cotangent):
    group_count = D // COLS
    full_tables = jnp.transpose(embed_tables.reshape(TABLES, group_count, DISTINCT, COLS), (0, 2, 1, 3)).reshape(TABLES, DISTINCT, D)
    flat_ids = item_ids.reshape(-1, TABLES)
    summed = jnp.zeros((flat_ids.shape[0], D), jnp.float32)
    for table_index in range(TABLES):
        summed = summed + full_tables[table_index][flat_ids[:, table_index]].astype(jnp.float32)
    embedded = summed.astype(jnp.bfloat16).reshape(N_BAL, N_EMB, NSEQ, SLOT, D)
    bal_ids = jnp.arange(N_BAL, dtype=jnp.int32)
    emb_ids = jnp.arange(N_EMB, dtype=jnp.int32)[None, :]
    source = lax.optimization_barrier(jnp.sum(jnp.where(helper_map[:, None, :] == bal_ids[None, :, None], bal_ids[:, None, None], 0), axis=0)).astype(jnp.int32)
    source_slot = surplus_slot[source, emb_ids]
    arrived = embedded[source, emb_ids, source_slot]
    slot_ids = jnp.arange(NSEQ, dtype=jnp.int32)
    replaced = slot_ids[None, None, :] == surplus_slot[:, :, None]
    proc_rows = jnp.where(replaced[:, :, :, None, None], arrived[:, :, None], embedded)
    proc_lengths = jnp.where(replaced, seq_lengths[source, emb_ids, source_slot][:, :, None], seq_lengths)
    blocks = N_BAL * N_EMB
    input_blocks = proc_rows.reshape(blocks, ROWS_DEV, D)
    cot_blocks = cotangent.reshape(blocks, ROWS_DEV, D)
    length_blocks = proc_lengths.reshape(blocks, NSEQ)

    def accumulate(totals, pieces):
        rows_here, cot_here, lengths_here = pieces
        forward_out, stored = layer_forward(rows_here, lengths_here, weight_in, weight_out, HEADS, SLOT)
        grad_rows, partial_in, partial_out = layer_backward(stored, cot_here, weight_in, weight_out, HEADS, SLOT)
        rounded_in = lax.optimization_barrier(partial_in.astype(jnp.bfloat16)).astype(jnp.float32)
        rounded_out = lax.optimization_barrier(partial_out.astype(jnp.bfloat16)).astype(jnp.float32)
        return ((totals[0] + rounded_in, totals[1] + rounded_out), (forward_out, grad_rows))
    start = (jnp.zeros((D, 4 * D), jnp.float32), jnp.zeros((D, D), jnp.float32))
    totals, outputs = lax.scan(accumulate, start, (input_blocks, cot_blocks, length_blocks))
    layer_out = outputs[0].reshape(N_BAL, EMB_ROWS, D)
    grad_proc = outputs[1].reshape(N_BAL, N_EMB, NSEQ, SLOT, D)
    helper_slot = surplus_slot[helper_map, emb_ids]
    came_back = grad_proc[helper_map, emb_ids, helper_slot]
    anchor_grads = jnp.where(replaced[:, :, :, None, None], came_back[:, :, None], grad_proc).reshape(-1, D)
    table_list = []
    for table_index in range(TABLES):
        table_list.append(jnp.zeros((DISTINCT, D), jnp.float32).at[flat_ids[:, table_index]].add(anchor_grads.astype(jnp.float32)))
    stacked = jnp.stack(table_list)
    table_scale = (DISTINCT / (N_BAL * EMB_ROWS)) ** 0.5
    table_grad = jnp.transpose(stacked.reshape(TABLES, DISTINCT, group_count, COLS), (0, 2, 1, 3)).reshape(N_EMB, DISTINCT, COLS) * table_scale
    grad_scale = EVENTS ** (-0.5)
    return (layer_out, table_grad, totals[0] * grad_scale, totals[1] * grad_scale)
```

```python
import functools

import jax
import jax.numpy as jnp
from jax import lax
from jax.experimental import pallas as pl
from jax.experimental.pallas import tpu as pltpu
from jax.sharding import PartitionSpec as P

HEADS = 8
EPS = 1e-05
LANES = 128
TILE_ROWS = 16
ROOM = 48 * 1024 * 1024

VMEM = pl.BlockSpec(memory_space=pltpu.VMEM)
SMEM = pl.BlockSpec(memory_space=pltpu.SMEM)
f32 = jnp.float32
bf16 = jnp.bfloat16


def matmul(left, right):
    return lax.dot_general(left, right, (((1,), (0,)), ((), ())), preferred_element_type=f32)


def matmul_nt(left, right):
    return lax.dot_general(left, right, (((1,), (1,)), ((), ())), preferred_element_type=f32)


def matmul_tn(left, right):
    return lax.dot_general(left, right, (((0,), (0,)), ((), ())), preferred_element_type=f32)


def sigmoid(value):
    return 0.5 * jnp.tanh(0.5 * value) + 0.5


def bal_swap(value, step, count):
    return lax.ppermute(value, "bal", [(i, i ^ step) for i in range(count)])


def emb_swap(value, step, count):
    return lax.ppermute(value, "emb", [(i, i ^ step) for i in range(count)])


def lookup_kernel(tables, groups, bals, pos_ref, *refs):
    ids_refs = refs[:groups]
    piece_refs = refs[groups : groups + 1 + (tables - 1) * bals]
    out_refs = refs[groups + 1 + (tables - 1) * bals :]
    bal = pos_ref[0]
    table_here = pos_ref[1]
    own_ref = piece_refs[0]
    distinct = own_ref.shape[0]
    part = distinct // bals
    rows = ids_refs[0].shape[2]
    lane = lax.broadcasted_iota(jnp.int32, (LANES, LANES), 1)
    for group in range(groups):
        for first in range(0, rows, LANES):
            total = jnp.zeros((LANES, own_ref.shape[1]), f32)
            for step in range(tables):
                row = ids_refs[group][table_here ^ step, :, first : first + LANES]
                column = jnp.transpose(jnp.broadcast_to(row, (LANES, LANES)))
                if step == 0:
                    pieces = [(own_ref, 0, distinct)]
                else:
                    base = 1 + (step - 1) * bals
                    pieces = [
                        (piece_refs[base + turn], (bal ^ turn) * part, part)
                        for turn in range(bals)
                    ]
                for ref, start, height in pieces:
                    shifted = column - start
                    hot = jnp.concatenate(
                        [
                            jnp.where(shifted == lane + at, 1.0, 0.0).astype(bf16)
                            for at in range(0, height, LANES)
                        ],
                        axis=1,
                    )
                    total = total + matmul(hot, ref[...])
            out_refs[group][first : first + LANES, :] = total.astype(bf16)


def scatter_kernel(tables, groups, bals, pos_ref, *refs):
    ids_refs = refs[:groups]
    grad_refs = refs[groups : 2 * groups]
    out_refs = refs[2 * groups :]
    bal = pos_ref[0]
    table_here = pos_ref[1]
    part = out_refs[0].shape[1]
    rows = ids_refs[0].shape[2]
    height = min(part, 256)
    iota = lax.broadcasted_iota(jnp.int32, (height, rows), 0)
    grads = jnp.concatenate([ref[...] for ref in grad_refs], axis=0)
    for step in range(tables):
        id_rows = [ref[table_here ^ step] for ref in ids_refs]
        for turn in range(bals):
            for at in range(0, part, height):
                start = (bal ^ turn) * part + at
                hot = jnp.concatenate(
                    [jnp.where(iota == row - start, 1.0, 0.0).astype(bf16) for row in id_rows],
                    axis=1,
                )
                out_refs[turn][step, at : at + height, :] = matmul(hot, grads).astype(bf16)


def norm(values):
    average = jnp.mean(values, axis=1, keepdims=True)
    centred = values - average
    inverse = lax.rsqrt(jnp.mean(centred * centred, axis=1, keepdims=True) + EPS)
    return centred * inverse, inverse


def norm_back(incoming, normed, inverse):
    first = jnp.mean(incoming, axis=1, keepdims=True)
    second = jnp.mean(incoming * normed, axis=1, keepdims=True)
    return inverse * (incoming - first - normed * second)


def layer_kernel(groups, bals, chunked, pos_ref, seq_ref, surplus_ref, helper_ref, *refs):
    refs = list(refs)
    take = lambda count: [refs.pop(0) for _ in range(count)]
    piece_refs = take(groups)
    in_refs = take(bals)
    out_refs = take(bals)
    (cot_ref,) = take(1)
    (layer_ref,) = take(1)
    grad_refs = take(groups)
    part_in_refs = take(bals)
    part_out_refs = take(bals)
    (x_ref, w_in, w_out, nt_ref, mt_ref, weights_ref, slope_ref, gate_ref, heads_ref, dsilu_ref, grads_ref) = refs

    bal = pos_ref[0]
    table_here = pos_ref[1]
    group_here = pos_ref[2]
    rows, width = cot_ref.shape
    slots = seq_ref.shape[1]
    slot_rows = rows // slots
    head_width = width // HEADS
    score_scale = head_width**-0.5
    piece = piece_refs[0].shape[1]

    for step in range(groups):
        x_ref[group_here ^ step] = piece_refs[step][...]
    part = in_refs[0].shape[0]
    for turn in range(bals):
        at = pl.ds(pl.multiple_of((bal ^ turn) * part, part), part)
        w_in[at, :] = in_refs[turn][...]
        w_out[at, :] = out_refs[turn][...]

    source = jnp.int32(0)
    for index in range(bals):
        source = source + jnp.where(helper_ref[index, 0] == bal, index, 0)
    my_slot = surplus_ref[bal, 0]
    moved = seq_ref[source, surplus_ref[source, 0]]
    lengths = [jnp.where(my_slot == slot, moved, seq_ref[bal, slot]) for slot in range(slots)]

    x = jnp.concatenate([x_ref[group] for group in range(groups)], axis=1).astype(f32)
    normed_in, in_inverse = norm(x)
    nt_ref[...] = jnp.transpose(normed_in).astype(bf16)
    projected = matmul(normed_in.astype(bf16), w_in[...])
    logistic = sigmoid(projected)
    active = projected * logistic
    dsilu_ref[...] = logistic + active * (1.0 - logistic)
    gate_ref[...] = active[:, :width]
    heads_ref[...] = active[:, width:].astype(bf16)

    pair_width = 2 * head_width
    low = lax.broadcasted_iota(jnp.int32, (slot_rows, pair_width), 1) < head_width
    row_at = lax.broadcasted_iota(jnp.int32, (slot_rows, slot_rows), 0)
    col_at = lax.broadcasted_iota(jnp.int32, (slot_rows, slot_rows), 1)

    def split(value):
        zero = jnp.zeros_like(value)
        return jnp.concatenate([jnp.where(low, value, zero), jnp.where(low, zero, value)], axis=0)

    def side_by_side(value):
        return jnp.concatenate([value[:slot_rows], value[slot_rows:]], axis=1)

    def part_of(slot, pair, which):
        first = which * width + pair * pair_width
        return heads_ref[slot * slot_rows : (slot + 1) * slot_rows, first : first + pair_width]

    pairs = HEADS // 2
    attended = []
    for slot in range(slots):
        live = (col_at <= row_at) & (row_at < lengths[slot])
        allowed = jnp.where(live, 1.0 / slot_rows, 0.0)
        allowed = jnp.concatenate([allowed, allowed], axis=0)
        across = []
        for pair in range(pairs):
            value, query, key = (part_of(slot, pair, which) for which in range(3))
            scores = matmul_nt(split(query), key) * score_scale
            q = sigmoid(scores)
            sq = scores * q
            weights = (sq * allowed).astype(bf16)
            weights_ref[slot * pairs + pair] = weights
            slope_ref[slot * pairs + pair] = allowed * (q + sq * (1.0 - q))
            across.append(matmul(side_by_side(weights), split(value)))
        attended.append(jnp.concatenate(across, axis=1))
    normed_out, out_inverse = norm(jnp.concatenate(attended, axis=0))
    gate = gate_ref[...]
    mixed = normed_out * gate
    mt_ref[...] = jnp.transpose(mixed).astype(bf16)
    layer_ref[...] = (x + matmul(mixed.astype(bf16), w_out[...])).astype(bf16)

    cot = cot_ref[...]
    grad_mixed = matmul_nt(cot, w_out[...])
    grad_attended = norm_back(grad_mixed * gate, normed_out, out_inverse).astype(bf16)
    grads_ref[:, :width] = (grad_mixed * normed_out * dsilu_ref[:, :width]).astype(bf16)

    chunk = TILE_ROWS if chunked else part

    def emit(ref, value, me):
        for index in range(part // chunk):
            at = (index ^ me) * chunk if chunked else index * chunk
            ref[pl.ds(pl.multiple_of(at, chunk), chunk), :] = value[index * chunk : (index + 1) * chunk]

    tables = part // chunk // groups if chunked else 1
    plane_first = group_here * tables + table_here
    table_first = table_here * groups + group_here
    for turn in range(bals):
        at = pl.ds(pl.multiple_of((bal ^ turn) * part, part), part)
        emit(part_out_refs[turn], matmul(mt_ref[at, :], cot).astype(bf16), table_first)

    for slot in range(slots):
        here = slice(slot * slot_rows, (slot + 1) * slot_rows)
        for pair in range(pairs):
            value, query, key = (part_of(slot, pair, which) for which in range(3))
            lanes = slice(pair * pair_width, (pair + 1) * pair_width)
            upper = split(grad_attended[here, lanes])
            grad_weights = matmul_nt(upper, value)
            grad_scores = (grad_weights * slope_ref[slot * pairs + pair]).astype(bf16)
            grad_value = matmul_tn(weights_ref[slot * pairs + pair], upper)
            grad_query = matmul(side_by_side(grad_scores), split(key)) * score_scale
            grad_key = matmul_tn(grad_scores, split(query)) * score_scale
            for which, found in enumerate((grad_value, grad_query, grad_key)):
                first = (1 + which) * width + pair * pair_width
                at = slice(first, first + pair_width)
                grads_ref[here, at] = (found * dsilu_ref[here, at]).astype(bf16)

    grad_projected = grads_ref[...]
    for turn in range(bals):
        at = pl.ds(pl.multiple_of((bal ^ turn) * part, part), part)
        emit(part_in_refs[turn], matmul(nt_ref[at, :], grad_projected).astype(bf16), plane_first)

    grad_normed = matmul_nt(grad_projected, w_in[...])
    grad_rows = (cot.astype(f32) + norm_back(grad_normed, normed_in, in_inverse)).astype(bf16)
    for group in range(groups):
        x_ref[group] = grad_rows[:, group * piece : (group + 1) * piece]
    for step in range(groups):
        grad_refs[step][...] = x_ref[group_here ^ step]


def place_kernel(scale, inner, pos_ref, me_ref, *refs):
    out_ref = refs[-1]
    me = me_ref[0]
    for outer, ref in enumerate(refs[:-1]):
        for index in range(inner):
            at = pl.multiple_of(((outer * inner + index) ^ me) * TILE_ROWS, TILE_ROWS)
            value = ref[index * TILE_ROWS : (index + 1) * TILE_ROWS, :]
            out_ref[pl.ds(at, TILE_ROWS), :] = value.astype(f32) * scale


def sum_rounded(terms):
    total = terms[0].astype(f32)
    for term in terms[1:]:
        total = total + term.astype(f32)
    return total.astype(bf16)


def reduce_scatter(value, count, stride, emb_count):
    pieces = value.reshape(count, value.shape[0] // count, value.shape[1])
    terms = [pieces[0]] + [
        emb_swap(pieces[step], step * stride, emb_count) for step in range(1, count)
    ]
    return sum_rounded(terms)


def gather(value, count, stride, emb_count):
    return [value] + [emb_swap(value, step * stride, emb_count) for step in range(1, count)]


def reduce_weights(terms, order, me, scale, emb_count, chunked, pos):
    own = sum_rounded(terms)
    rows, columns = own.shape
    if not chunked:
        return lax.psum(own.astype(f32), "emb") * scale
    (first, first_stride), (second, second_stride) = order
    own = reduce_scatter(own, first, first_stride, emb_count)
    own = reduce_scatter(own, second, second_stride, emb_count)
    inner = jnp.concatenate(gather(own, second, second_stride, emb_count), axis=0)
    outer = gather(inner, first, first_stride, emb_count)
    return pl.pallas_call(
        functools.partial(place_kernel, scale, second),
        out_shape=jax.ShapeDtypeStruct((rows, columns), f32),
        in_specs=[SMEM, SMEM] + [VMEM] * first,
        out_specs=VMEM,
        compiler_params=pltpu.CompilerParams(vmem_limit_bytes=ROOM),
    )(pos, me, *outer)


def on_device(
    item_ids, seq_lengths, surplus_slot, helper_map, embed_tables, weight_in, weight_out, cotangent
):
    bal = lax.axis_index("bal")
    emb = lax.axis_index("emb")
    bals = lax.axis_size("bal")
    embs = lax.axis_size("emb")
    tables = item_ids.shape[2]
    groups = embs // tables
    _, rows, width = cotangent.shape
    slots = seq_lengths.shape[2]
    slot_rows = rows // slots
    distinct, columns = embed_tables.shape[1:]
    features = weight_in.shape[1]
    part = distinct // bals
    weight_part = weight_in.shape[0]
    chunked = weight_part == embs * TILE_ROWS
    table_here = emb // groups
    group_here = emb % groups
    pos = jnp.stack([bal, table_here, group_here]).astype(jnp.int32)
    params = pltpu.CompilerParams(vmem_limit_bytes=ROOM)

    own_table = embed_tables[0]
    share = lax.dynamic_slice_in_dim(own_table, bal * part, part, 0)
    pieces = [own_table]
    for step in range(1, tables):
        fetched = emb_swap(share, step * groups, embs)
        pieces += [fetched] + [bal_swap(fetched, turn, bals) for turn in range(1, bals)]

    ids = lax.dynamic_slice_in_dim(jnp.transpose(item_ids[0]), emb * rows, rows, 1)
    ids = ids.reshape(tables, slots, slot_rows)
    my_slot = lax.dynamic_index_in_dim(surplus_slot[:, 0], bal, 0, keepdims=False)
    leaving = lax.dynamic_index_in_dim(ids, my_slot, 1, keepdims=False)
    bal_ids = jnp.arange(bals, dtype=jnp.int32)
    source = jnp.sum(jnp.where(helper_map[:, 0] == bal, bal_ids, 0))
    arrived = leaving
    for turn in range(1, bals):
        arrived = jnp.where(source == bal ^ turn, bal_swap(leaving, turn, bals), arrived)
    replaced = jnp.arange(slots, dtype=jnp.int32) == my_slot
    proc_ids = jnp.where(replaced[None, :, None], arrived[:, None, :], ids).reshape(tables, 1, rows)
    plane_ids = gather(proc_ids, groups, 1, embs)

    all_in = [weight_in] + [bal_swap(weight_in, turn, bals) for turn in range(1, bals)]
    all_out = [weight_out] + [bal_swap(weight_out, turn, bals) for turn in range(1, bals)]

    found = pl.pallas_call(
        functools.partial(lookup_kernel, tables, groups, bals),
        out_shape=[jax.ShapeDtypeStruct((rows, columns), bf16)] * groups,
        in_specs=[SMEM] + [VMEM] * (groups + len(pieces)),
        out_specs=[VMEM] * groups,
        compiler_params=params,
    )(pos, *plane_ids, *pieces)
    block = [found[0]] + [emb_swap(found[step], step, embs) for step in range(1, groups)]

    pairs = slots * HEADS // 2
    results = pl.pallas_call(
        functools.partial(layer_kernel, groups, bals, chunked),
        out_shape=[jax.ShapeDtypeStruct((rows, width), bf16)]
        + [jax.ShapeDtypeStruct((rows, columns), bf16)] * groups
        + [jax.ShapeDtypeStruct((weight_part, features), bf16)] * bals
        + [jax.ShapeDtypeStruct((weight_part, width), bf16)] * bals,
        in_specs=[SMEM] * 4 + [VMEM] * (groups + 2 * bals + 1),
        out_specs=[VMEM] * (1 + groups + 2 * bals),
        scratch_shapes=[
            pltpu.VMEM((groups, rows, columns), bf16),
            pltpu.VMEM((width, features), bf16),
            pltpu.VMEM((width, width), bf16),
            pltpu.VMEM((width, rows), bf16),
            pltpu.VMEM((width, rows), bf16),
            pltpu.VMEM((pairs, 2 * slot_rows, slot_rows), bf16),
            pltpu.VMEM((pairs, 2 * slot_rows, slot_rows), f32),
            pltpu.VMEM((rows, width), f32),
            pltpu.VMEM((rows, features - width), bf16),
            pltpu.VMEM((rows, features), f32),
            pltpu.VMEM((rows, features), bf16),
        ],
        compiler_params=params,
    )(
        pos,
        seq_lengths[:, 0, :],
        surplus_slot,
        helper_map,
        *block,
        *all_in,
        *all_out,
        cotangent[0],
    )
    layer_out, results = results[0], results[1:]
    grads, results = results[:groups], results[groups:]
    parts_in, parts_out = results[:bals], results[bals:]

    plane_grads = [grads[0]] + [emb_swap(grads[step], step, embs) for step in range(1, groups)]
    sums = pl.pallas_call(
        functools.partial(scatter_kernel, tables, groups, bals),
        out_shape=[jax.ShapeDtypeStruct((tables, part, columns), bf16)] * bals,
        in_specs=[SMEM] + [VMEM] * (2 * groups),
        out_specs=[VMEM] * bals,
        compiler_params=params,
    )(pos, *plane_ids, *plane_grads)
    own_sums = sum_rounded([sums[0]] + [bal_swap(sums[turn], turn, bals) for turn in range(1, bals)])
    table_sum = own_sums[0].astype(f32)
    for step in range(1, tables):
        table_sum = table_sum + emb_swap(own_sums[step], step * groups, embs).astype(f32)
    table_scale = (distinct / (bals * item_ids.shape[1])) ** 0.5

    grad_scale = (rows * embs * bals) ** -0.5
    plane, depth = (groups, 1), (tables, groups)
    plane_first = (group_here * tables + table_here).reshape(1).astype(jnp.int32)
    table_first = (table_here * groups + group_here).reshape(1).astype(jnp.int32)
    terms_in = [parts_in[0]] + [bal_swap(parts_in[turn], turn, bals) for turn in range(1, bals)]
    terms_out = [parts_out[0]] + [bal_swap(parts_out[turn], turn, bals) for turn in range(1, bals)]
    total_out = reduce_weights(terms_out, (depth, plane), table_first, grad_scale, embs, chunked, pos)
    total_in = reduce_weights(terms_in, (plane, depth), plane_first, grad_scale, embs, chunked, pos)
    return layer_out[None], (table_sum * table_scale)[None], total_in, total_out


def solution(mesh):
    placed = (
        P("bal", None, None),
        P(None, "emb", None),
        P(None, "emb"),
        P(None, "emb"),
        P("emb", None, None),
        P("bal", None),
        P("bal", None),
        P("bal", "emb", None),
    )
    return jax.shard_map(
        on_device,
        mesh=mesh,
        in_specs=placed,
        out_specs=(P("bal", "emb", None), P("emb", "bal", None), P("bal", None), P("bal", None)),
        check_vma=False,
    )
```

```python
import functools

import jax
import jax.numpy as jnp
from jax import lax
from jax.experimental import pallas as pl
from jax.experimental.pallas import tpu as pltpu
from jax.sharding import PartitionSpec as P

HEADS = 8
EPS = 1e-05
LANES = 128
ROOM = 48 * 1024 * 1024

VMEM = pl.BlockSpec(memory_space=pltpu.VMEM)
SMEM = pl.BlockSpec(memory_space=pltpu.SMEM)
ANY = pl.BlockSpec(memory_space=pl.ANY)
f32 = jnp.float32
bf16 = jnp.bfloat16


def matmul(left, right):
    return lax.dot_general(left, right, (((1,), (0,)), ((), ())), preferred_element_type=f32)


def matmul_nt(left, right):
    return lax.dot_general(left, right, (((1,), (1,)), ((), ())), preferred_element_type=f32)


def matmul_tn(left, right):
    return lax.dot_general(left, right, (((0,), (0,)), ((), ())), preferred_element_type=f32)


def sigmoid(value):
    return 0.5 * jnp.tanh(0.5 * value) + 0.5


def bal_swap(value, step, count):
    return lax.ppermute(value, "bal", [(i, i ^ step) for i in range(count)])


def with_swapped(value, count):
    return [value] + [bal_swap(value, turn, count) for turn in range(1, count)]


def exchange(value, members):
    return lax.all_to_all(value, "emb", 0, 0, axis_index_groups=members, tiled=True)


def gather(value, members):
    count = len(members[0])
    copies = jnp.broadcast_to(value[None], (count,) + value.shape)
    return exchange(copies.reshape((count * value.shape[0],) + value.shape[1:]), members)


def pick_ids(pos_ref, moves_ref, ids_refs, groups, slots, tables):
    bal = pos_ref[0]
    bals = len(ids_refs)
    found = []
    for group in range(groups):
        source = jnp.int32(0)
        for index in range(bals):
            source = source + jnp.where(moves_ref[group, bals + index] == bal, index, 0)
        my_slot = moves_ref[group, bal]
        from_slot = moves_ref[group, source]
        turn_of = source ^ bal
        by_slot = [[] for _ in range(slots)]
        for table in range(tables):
            arrived = ids_refs[0][table, group * slots + from_slot]
            for turn in range(1, bals):
                other = ids_refs[turn][table, group * slots + from_slot]
                arrived = jnp.where(turn_of == turn, other, arrived)
            for slot in range(slots):
                own = ids_refs[0][table, group * slots + slot]
                by_slot[slot].append(jnp.where(my_slot == slot, arrived, own))
        found.append(by_slot)
    return found


def lookup_kernel(groups, slots, pos_ref, moves_ref, *refs):
    bals = (len(refs) - 1) // 2
    ids_refs, piece_refs, out_ref = refs[:bals], refs[bals : 2 * bals], refs[-1]
    bal = pos_ref[0]
    tables, part, columns = piece_refs[0].shape
    slot_rows = ids_refs[0].shape[3]
    lane = lax.broadcasted_iota(jnp.int32, (LANES, LANES), 1)
    ids = pick_ids(pos_ref, moves_ref, ids_refs, groups, slots, tables)
    for group in range(groups):
        for slot in range(slots):
            for first in range(0, slot_rows, LANES):
                total = jnp.zeros((LANES, columns), f32)
                for table in range(tables):
                    row = ids[group][slot][table][:, first : first + LANES]
                    column = jnp.transpose(jnp.broadcast_to(row, (LANES, LANES)))
                    for turn in range(bals):
                        shifted = column - (bal ^ turn) * part
                        hot = jnp.concatenate(
                            [
                                jnp.where(shifted == lane + at, 1.0, 0.0).astype(bf16)
                                for at in range(0, part, LANES)
                            ],
                            axis=1,
                        )
                        total = total + matmul(hot, piece_refs[turn][table])
                at = (group * slots + slot) * slot_rows + first
                out_ref[at : at + LANES, :] = total.astype(bf16)


def scatter_kernel(groups, slots, pos_ref, moves_ref, *refs):
    bals = (len(refs) - 1) // 2
    ids_refs, grad_ref, out_refs = refs[:bals], refs[bals], refs[bals + 1 :]
    bal = pos_ref[0]
    tables, part, _ = out_refs[0].shape
    slot_rows = ids_refs[0].shape[3]
    height = min(part, 256)
    iota = lax.broadcasted_iota(jnp.int32, (height, slot_rows), 0)
    ids = pick_ids(pos_ref, moves_ref, ids_refs, groups, slots, tables)
    grads = grad_ref[...]
    for table in range(tables):
        for turn in range(bals):
            for at in range(0, part, height):
                start = (bal ^ turn) * part + at
                hot = jnp.concatenate(
                    [
                        jnp.where(iota == ids[group][slot][table] - start, 1.0, 0.0).astype(bf16)
                        for group in range(groups)
                        for slot in range(slots)
                    ],
                    axis=1,
                )
                out_refs[turn][table, at : at + height, :] = matmul(hot, grads).astype(bf16)


def norm(values):
    average = jnp.mean(values, axis=1, keepdims=True)
    centred = values - average
    inverse = lax.rsqrt(jnp.mean(centred * centred, axis=1, keepdims=True) + EPS)
    return centred * inverse, inverse


def norm_back(incoming, normed, inverse):
    first = jnp.mean(incoming, axis=1, keepdims=True)
    second = jnp.mean(incoming * normed, axis=1, keepdims=True)
    return inverse * (incoming - first - normed * second)


def layer_kernel(groups, bals, pos_ref, seq_ref, surplus_ref, helper_ref, *refs):
    refs = list(refs)
    take = lambda count: [refs.pop(0) for _ in range(count)]
    (block_ref,) = take(1)
    in_refs = take(bals)
    out_refs = take(bals)
    (cot_ref,) = take(1)
    (layer_ref,) = take(1)
    (grad_ref,) = take(1)
    early_refs = take(bals)
    late_refs = take(bals)
    (w_in, w_out, cot_here, nt_ref, mt_ref, weights_ref, slope_ref, gate_ref, heads_ref, dsilu_ref, grads_ref, sems) = refs

    bal = pos_ref[0]
    rows, width = cot_here.shape
    slots = seq_ref.shape[1]
    slot_rows = rows // slots
    head_width = width // HEADS
    score_scale = head_width**-0.5
    piece = block_ref.shape[1]
    part = in_refs[0].shape[0]

    in_copies, out_copies = [], []
    for turn in range(bals):
        at = pl.ds(pl.multiple_of((bal ^ turn) * part, part), part)
        in_copies.append(pltpu.make_async_copy(in_refs[turn], w_in.at[at, :], sems.at[2 * turn]))
        out_copies.append(pltpu.make_async_copy(out_refs[turn], w_out.at[at, :], sems.at[2 * turn + 1]))
    cot_copy = pltpu.make_async_copy(cot_ref, cot_here, sems.at[2 * bals])
    for copy in in_copies + out_copies + [cot_copy]:
        copy.start()

    source = jnp.int32(0)
    for index in range(bals):
        source = source + jnp.where(helper_ref[index, 0] == bal, index, 0)
    my_slot = surplus_ref[bal, 0]
    moved = seq_ref[source, surplus_ref[source, 0]]
    lengths = [jnp.where(my_slot == slot, moved, seq_ref[bal, slot]) for slot in range(slots)]

    x = jnp.concatenate(
        [block_ref[group * rows : (group + 1) * rows, :] for group in range(groups)], axis=1
    ).astype(f32)
    normed_in, in_inverse = norm(x)
    nt_ref[...] = jnp.transpose(normed_in).astype(bf16)
    for copy in in_copies:
        copy.wait()
    projected = matmul(normed_in.astype(bf16), w_in[...])
    logistic = sigmoid(projected)
    active = projected * logistic
    dsilu_ref[...] = logistic + active * (1.0 - logistic)
    gate_ref[...] = active[:, :width]
    heads_ref[...] = active[:, width:].astype(bf16)

    pair_width = 2 * head_width
    low = lax.broadcasted_iota(jnp.int32, (slot_rows, pair_width), 1) < head_width
    row_at = lax.broadcasted_iota(jnp.int32, (slot_rows, slot_rows), 0)
    col_at = lax.broadcasted_iota(jnp.int32, (slot_rows, slot_rows), 1)

    def split(value):
        zero = jnp.zeros_like(value)
        return jnp.concatenate([jnp.where(low, value, zero), jnp.where(low, zero, value)], axis=0)

    def side_by_side(value):
        return jnp.concatenate([value[:slot_rows], value[slot_rows:]], axis=1)

    def part_of(slot, pair, which):
        first = which * width + pair * pair_width
        return heads_ref[slot * slot_rows : (slot + 1) * slot_rows, first : first + pair_width]

    pairs = HEADS // 2
    attended = []
    for slot in range(slots):
        live = (col_at <= row_at) & (row_at < lengths[slot])
        allowed = jnp.where(live, 1.0 / slot_rows, 0.0)
        allowed = jnp.concatenate([allowed, allowed], axis=0)
        across = []
        for pair in range(pairs):
            value, query, key = (part_of(slot, pair, which) for which in range(3))
            scores = matmul_nt(split(query), key) * score_scale
            q = sigmoid(scores)
            sq = scores * q
            weights = (sq * allowed).astype(bf16)
            weights_ref[slot * pairs + pair] = weights
            slope_ref[slot * pairs + pair] = allowed * (q + sq * (1.0 - q))
            across.append(matmul(side_by_side(weights), split(value)))
        attended.append(jnp.concatenate(across, axis=1))
    normed_out, out_inverse = norm(jnp.concatenate(attended, axis=0))
    gate = gate_ref[...]
    mixed = normed_out * gate
    mt_ref[...] = jnp.transpose(mixed).astype(bf16)
    for copy in out_copies + [cot_copy]:
        copy.wait()
    layer_ref[...] = (x + matmul(mixed.astype(bf16), w_out[...])).astype(bf16)

    cot = cot_here[...]
    grad_mixed = matmul_nt(cot, w_out[...])
    grad_attended = norm_back(grad_mixed * gate, normed_out, out_inverse).astype(bf16)
    grads_ref[:, :width] = (grad_mixed * normed_out * dsilu_ref[:, :width]).astype(bf16)

    for turn in range(bals):
        at = pl.ds(pl.multiple_of((bal ^ turn) * part, part), part)
        early_refs[turn][:, :width] = matmul(mt_ref[at, :], cot).astype(bf16)
        early_refs[turn][:, width:] = matmul(nt_ref[at, :], grads_ref[:, :width]).astype(bf16)

    for slot in range(slots):
        here = slice(slot * slot_rows, (slot + 1) * slot_rows)
        for pair in range(pairs):
            value, query, key = (part_of(slot, pair, which) for which in range(3))
            lanes = slice(pair * pair_width, (pair + 1) * pair_width)
            upper = split(grad_attended[here, lanes])
            grad_weights = matmul_nt(upper, value)
            grad_scores = (grad_weights * slope_ref[slot * pairs + pair]).astype(bf16)
            grad_value = matmul_tn(weights_ref[slot * pairs + pair], upper)
            grad_query = matmul(side_by_side(grad_scores), split(key)) * score_scale
            grad_key = matmul_tn(grad_scores, split(query)) * score_scale
            for which, found in enumerate((grad_value, grad_query, grad_key)):
                first = (1 + which) * width + pair * pair_width
                at = slice(first, first + pair_width)
                grads_ref[here, at] = (found * dsilu_ref[here, at]).astype(bf16)

    for turn in range(bals):
        at = pl.ds(pl.multiple_of((bal ^ turn) * part, part), part)
        late_refs[turn][...] = matmul(nt_ref[at, :], grads_ref[:, width:]).astype(bf16)

    grad_normed = matmul_nt(grads_ref[...], w_in[...])
    grad_rows = (cot.astype(f32) + norm_back(grad_normed, normed_in, in_inverse)).astype(bf16)
    for group in range(groups):
        grad_ref[group * rows : (group + 1) * rows, :] = grad_rows[:, group * piece : (group + 1) * piece]


def sum_rounded(terms):
    total = terms[0].astype(f32)
    for term in terms[1:]:
        total = total + term.astype(f32)
    return total.astype(bf16)


def sum_exchanged(value, members):
    count = len(members[0])
    came = exchange(value, members)
    came = came.reshape((count, came.shape[0] // count) + came.shape[1:])
    return sum_rounded([came[index] for index in range(count)])


def on_device(
    item_ids, seq_lengths, surplus_slot, helper_map, embed_tables, weight_in, weight_out, cotangent
):
    bal = lax.axis_index("bal")
    emb = lax.axis_index("emb")
    bals = lax.axis_size("bal")
    embs = lax.axis_size("emb")
    tables = item_ids.shape[2]
    groups = embs // tables
    _, rows, width = cotangent.shape
    slots = seq_lengths.shape[2]
    slot_rows = rows // slots
    distinct, columns = embed_tables.shape[1:]
    features = weight_in.shape[1]
    part = distinct // bals
    weight_part = weight_in.shape[0]
    table_here = emb // groups
    pos = bal.reshape(1).astype(jnp.int32)
    params = pltpu.CompilerParams(vmem_limit_bytes=ROOM)

    plane = [[table * groups + group for group in range(groups)] for table in range(tables)]
    depth = [[table * groups + group for table in range(tables)] for group in range(groups)]

    share = lax.dynamic_slice_in_dim(embed_tables[0], bal * part, part, 0)
    fetched = gather(share, depth).reshape(tables, part, columns)
    pieces = with_swapped(fetched, bals)

    ids = lax.dynamic_slice_in_dim(
        jnp.transpose(item_ids[0]), table_here * groups * rows, groups * rows, 1
    )
    plane_ids = with_swapped(ids.reshape(tables, groups * slots, 1, slot_rows), bals)
    moves = jnp.concatenate([surplus_slot[:, 0], helper_map[:, 0]])
    moves = gather(jnp.pad(moves, (0, LANES - 2 * bals))[None], plane)

    all_in = with_swapped(weight_in, bals)
    all_out = with_swapped(weight_out, bals)

    found = pl.pallas_call(
        functools.partial(lookup_kernel, groups, slots),
        out_shape=jax.ShapeDtypeStruct((groups * rows, columns), bf16),
        in_specs=[SMEM] * 2 + [VMEM] * (2 * bals),
        out_specs=VMEM,
        compiler_params=params,
    )(pos, moves, *plane_ids, *pieces)
    block = exchange(found, plane)

    pairs = slots * HEADS // 2
    early, late = 2 * width, features - width
    results = pl.pallas_call(
        functools.partial(layer_kernel, groups, bals),
        out_shape=[jax.ShapeDtypeStruct((rows, width), bf16)]
        + [jax.ShapeDtypeStruct((groups * rows, columns), bf16)]
        + [jax.ShapeDtypeStruct((weight_part, early), bf16)] * bals
        + [jax.ShapeDtypeStruct((weight_part, late), bf16)] * bals,
        in_specs=[SMEM] * 4 + [VMEM] + [ANY] * (2 * bals + 1),
        out_specs=[VMEM] * (2 + 2 * bals),
        scratch_shapes=[
            pltpu.VMEM((width, features), bf16),
            pltpu.VMEM((width, width), bf16),
            pltpu.VMEM((rows, width), bf16),
            pltpu.VMEM((width, rows), bf16),
            pltpu.VMEM((width, rows), bf16),
            pltpu.VMEM((pairs, 2 * slot_rows, slot_rows), bf16),
            pltpu.VMEM((pairs, 2 * slot_rows, slot_rows), f32),
            pltpu.VMEM((rows, width), f32),
            pltpu.VMEM((rows, features - width), bf16),
            pltpu.VMEM((rows, features), f32),
            pltpu.VMEM((rows, features), bf16),
            pltpu.SemaphoreType.DMA((2 * bals + 1,)),
        ],
        compiler_params=params,
    )(
        pos,
        seq_lengths[:, 0, :],
        surplus_slot,
        helper_map,
        block,
        *all_in,
        *all_out,
        cotangent[0],
    )
    layer_out, grads = results[:2]
    early_parts, late_parts = results[2 : 2 + bals], results[2 + bals :]

    def over_cores(parts):
        return sum_rounded([parts[0]] + [bal_swap(parts[turn], turn, bals) for turn in range(1, bals)])

    plane_grads = exchange(grads, plane)
    early_sum = sum_exchanged(over_cores(early_parts), plane)
    sums = pl.pallas_call(
        functools.partial(scatter_kernel, groups, slots),
        out_shape=[jax.ShapeDtypeStruct((tables, part, columns), bf16)] * bals,
        in_specs=[SMEM] * 2 + [VMEM] * (bals + 1),
        out_specs=[VMEM] * bals,
        compiler_params=params,
    )(pos, moves, *plane_ids, plane_grads)
    late_sum = sum_exchanged(over_cores(late_parts), plane)
    table_rows = exchange(over_cores(sums), depth)
    table_sum = jnp.sum(table_rows.astype(f32), axis=0)
    table_scale = (distinct / (bals * item_ids.shape[1])) ** 0.5

    grad_scale = (rows * embs * bals) ** -0.5
    early_all = gather(gather(sum_exchanged(early_sum, depth), depth), plane)
    late_all = gather(gather(sum_exchanged(late_sum, depth), depth), plane)
    total_out = early_all[:, :width].astype(f32) * grad_scale
    total_in = jnp.concatenate([early_all[:, width:], late_all], axis=1).astype(f32) * grad_scale
    return layer_out[None], (table_sum * table_scale)[None], total_in, total_out


def solution(mesh):
    placed = (
        P("bal", None, None),
        P(None, "emb", None),
        P(None, "emb"),
        P(None, "emb"),
        P("emb", None, None),
        P("bal", None),
        P("bal", None),
        P("bal", "emb", None),
    )
    return jax.shard_map(
        on_device,
        mesh=mesh,
        in_specs=placed,
        out_specs=(P("bal", "emb", None), P("emb", "bal", None), P("bal", None), P("bal", None)),
        check_vma=False,
    )
```

```python
import functools

import jax
import jax.numpy as jnp
from jax import lax
from jax.experimental import pallas as pl
from jax.experimental.pallas import tpu as pltpu
from jax.sharding import PartitionSpec as P

HEADS = 8
EPS = 1e-05
LANES = 128
ROOM = 48 * 1024 * 1024

VMEM = pl.BlockSpec(memory_space=pltpu.VMEM)
SMEM = pl.BlockSpec(memory_space=pltpu.SMEM)
HBM = pl.BlockSpec(memory_space=pltpu.HBM)
f32 = jnp.float32
bf16 = jnp.bfloat16


def matmul(left, right):
    return lax.dot_general(left, right, (((1,), (0,)), ((), ())), preferred_element_type=f32)


def matmul_nt(left, right):
    return lax.dot_general(left, right, (((1,), (1,)), ((), ())), preferred_element_type=f32)


def matmul_tn(left, right):
    return lax.dot_general(left, right, (((0,), (0,)), ((), ())), preferred_element_type=f32)


def sigmoid(value):
    return 0.5 * jnp.tanh(0.5 * value) + 0.5


def bal_swap(value, step, count):
    return lax.ppermute(value, "bal", [(i, i ^ step) for i in range(count)])


def with_swapped(value, count):
    return [value] + [bal_swap(value, turn, count) for turn in range(1, count)]


def emb_swap(value, step, count):
    return lax.ppermute(value, "emb", [(i, i ^ step) for i in range(count)])


def pick_ids(pos_ref, moves_refs, ids_refs, slots, tables):
    bal = pos_ref[0]
    bals = len(ids_refs)
    found = []
    for step, moves_ref in enumerate(moves_refs):
        group = pos_ref[1] ^ step
        source = jnp.int32(0)
        for index in range(bals):
            source = source + jnp.where(moves_ref[0, bals + index] == bal, index, 0)
        my_slot = moves_ref[0, bal]
        from_slot = moves_ref[0, source]
        turn_of = source ^ bal
        by_slot = [[] for _ in range(slots)]
        for table in tables:
            arrived = ids_refs[0][table, group * slots + from_slot]
            for turn in range(1, bals):
                other = ids_refs[turn][table, group * slots + from_slot]
                arrived = jnp.where(turn_of == turn, other, arrived)
            for slot in range(slots):
                own = ids_refs[0][table, group * slots + slot]
                by_slot[slot].append(jnp.where(my_slot == slot, arrived, own))
        found.append(by_slot)
    return found


def table_order(table_here, tables):
    return [table_here ^ step for step in range(tables)]


def lookup_kernel(groups, slots, tables, bals, pos_ref, *refs):
    refs = list(refs)
    take = lambda count: [refs.pop(0) for _ in range(count)]
    moves_refs, ids_refs = take(groups), take(bals)
    (own_ref,) = take(1)
    others = [take(bals) for _ in range(1, tables)]
    out_refs = refs
    bal = pos_ref[0]
    table_here = pos_ref[2]
    distinct, columns = own_ref.shape
    part = distinct // bals
    slot_rows = ids_refs[0].shape[3]
    lane = lax.broadcasted_iota(jnp.int32, (LANES, LANES), 1)
    ids = pick_ids(pos_ref, moves_refs, ids_refs, slots, table_order(table_here, tables))
    for group in range(groups):
        for slot in range(slots):
            for first in range(0, slot_rows, LANES):
                total = jnp.zeros((LANES, columns), f32)
                for table in range(tables):
                    row = ids[group][slot][table][:, first : first + LANES]
                    column = jnp.transpose(jnp.broadcast_to(row, (LANES, LANES)))
                    if table == 0:
                        pieces = [(own_ref, 0, distinct)]
                    else:
                        pieces = [
                            (ref, (bal ^ turn) * part, part)
                            for turn, ref in enumerate(others[table - 1])
                        ]
                    for ref, start, height in pieces:
                        shifted = column - start
                        hot = jnp.concatenate(
                            [
                                jnp.where(shifted == lane + at, 1.0, 0.0).astype(bf16)
                                for at in range(0, height, LANES)
                            ],
                            axis=1,
                        )
                        total = total + matmul(hot, ref[...])
                at = slot * slot_rows + first
                out_refs[group][at : at + LANES, :] = total.astype(bf16)


def scatter_kernel(groups, slots, bals, pos_ref, *refs):
    refs = list(refs)
    take = lambda count: [refs.pop(0) for _ in range(count)]
    moves_refs, ids_refs, grad_refs, out_refs = take(groups), take(bals), take(groups), refs
    bal = pos_ref[0]
    table_here = pos_ref[2]
    tables, part, _ = out_refs[0].shape
    slot_rows = ids_refs[0].shape[3]
    height = min(part, 256)
    iota = lax.broadcasted_iota(jnp.int32, (height, slot_rows), 0)
    ids = pick_ids(pos_ref, moves_refs, ids_refs, slots, table_order(table_here, tables))
    grads = jnp.concatenate([ref[...] for ref in grad_refs], axis=0)
    for table in range(tables):
        for turn in range(bals):
            for at in range(0, part, height):
                start = (bal ^ turn) * part + at
                hot = jnp.concatenate(
                    [
                        jnp.where(iota == ids[group][slot][table] - start, 1.0, 0.0).astype(bf16)
                        for group in range(groups)
                        for slot in range(slots)
                    ],
                    axis=1,
                )
                out_refs[turn][table, at : at + height, :] = matmul(hot, grads).astype(bf16)


def norm(values):
    average = jnp.mean(values, axis=1, keepdims=True)
    centred = values - average
    inverse = lax.rsqrt(jnp.mean(centred * centred, axis=1, keepdims=True) + EPS)
    return centred * inverse, inverse


def norm_back(incoming, normed, inverse):
    first = jnp.mean(incoming, axis=1, keepdims=True)
    second = jnp.mean(incoming * normed, axis=1, keepdims=True)
    return inverse * (incoming - first - normed * second)


def layer_kernel(groups, bals, pos_ref, seq_ref, surplus_ref, helper_ref, *refs):
    refs = list(refs)
    take = lambda count: [refs.pop(0) for _ in range(count)]
    block_refs = take(groups)
    in_refs = take(bals)
    out_refs = take(bals)
    (cot_ref,) = take(1)
    (layer_ref,) = take(1)
    grad_refs = take(groups)
    early_refs = take(bals)
    late_refs = take(bals)
    (x_ref, w_in, w_out, cot_here, nt_ref, mt_ref, weights_ref, slope_ref, gate_ref, heads_ref, dsilu_ref, grads_ref, sems) = refs

    bal = pos_ref[0]
    rows, width = cot_here.shape
    slots = seq_ref.shape[1]
    slot_rows = rows // slots
    head_width = width // HEADS
    score_scale = head_width**-0.5
    piece = block_refs[0].shape[1]
    group_here = pos_ref[1]
    part = in_refs[0].shape[0]

    in_copies, out_copies = [], []
    for turn in range(bals):
        at = pl.ds(pl.multiple_of((bal ^ turn) * part, part), part)
        in_copies.append(pltpu.make_async_copy(in_refs[turn], w_in.at[at, :], sems.at[2 * turn]))
        out_copies.append(pltpu.make_async_copy(out_refs[turn], w_out.at[at, :], sems.at[2 * turn + 1]))
    cot_copy = pltpu.make_async_copy(cot_ref, cot_here, sems.at[2 * bals])
    for copy in in_copies + out_copies + [cot_copy]:
        copy.start()

    source = jnp.int32(0)
    for index in range(bals):
        source = source + jnp.where(helper_ref[index, 0] == bal, index, 0)
    my_slot = surplus_ref[bal, 0]
    moved = seq_ref[source, surplus_ref[source, 0]]
    lengths = [jnp.where(my_slot == slot, moved, seq_ref[bal, slot]) for slot in range(slots)]

    for step in range(groups):
        x_ref[group_here ^ step] = block_refs[step][...]
    x = jnp.concatenate([x_ref[group] for group in range(groups)], axis=1).astype(f32)
    normed_in, in_inverse = norm(x)
    nt_ref[...] = jnp.transpose(normed_in).astype(bf16)
    for copy in in_copies:
        copy.wait()
    projected = matmul(normed_in.astype(bf16), w_in[...])
    logistic = sigmoid(projected)
    active = projected * logistic
    dsilu_ref[...] = logistic + active * (1.0 - logistic)
    gate_ref[...] = active[:, :width]
    heads_ref[...] = active[:, width:].astype(bf16)

    pair_width = 2 * head_width
    low = lax.broadcasted_iota(jnp.int32, (slot_rows, pair_width), 1) < head_width
    row_at = lax.broadcasted_iota(jnp.int32, (slot_rows, slot_rows), 0)
    col_at = lax.broadcasted_iota(jnp.int32, (slot_rows, slot_rows), 1)

    def split(value):
        zero = jnp.zeros_like(value)
        return jnp.concatenate([jnp.where(low, value, zero), jnp.where(low, zero, value)], axis=0)

    def side_by_side(value):
        return jnp.concatenate([value[:slot_rows], value[slot_rows:]], axis=1)

    def part_of(slot, pair, which):
        first = which * width + pair * pair_width
        return heads_ref[slot * slot_rows : (slot + 1) * slot_rows, first : first + pair_width]

    pairs = HEADS // 2
    attended = []
    for slot in range(slots):
        live = (col_at <= row_at) & (row_at < lengths[slot])
        allowed = jnp.where(live, 1.0 / slot_rows, 0.0)
        allowed = jnp.concatenate([allowed, allowed], axis=0)
        across = []
        for pair in range(pairs):
            value, query, key = (part_of(slot, pair, which) for which in range(3))
            scores = matmul_nt(split(query), key) * score_scale
            q = sigmoid(scores)
            sq = scores * q
            weights = (sq * allowed).astype(bf16)
            weights_ref[slot * pairs + pair] = weights
            slope_ref[slot * pairs + pair] = allowed * (q + sq * (1.0 - q))
            across.append(matmul(side_by_side(weights), split(value)))
        attended.append(jnp.concatenate(across, axis=1))
    normed_out, out_inverse = norm(jnp.concatenate(attended, axis=0))
    gate = gate_ref[...]
    mixed = normed_out * gate
    mt_ref[...] = jnp.transpose(mixed).astype(bf16)
    for copy in out_copies + [cot_copy]:
        copy.wait()
    layer_ref[...] = (x + matmul(mixed.astype(bf16), w_out[...])).astype(bf16)

    cot = cot_here[...]
    grad_mixed = matmul_nt(cot, w_out[...])
    grad_attended = norm_back(grad_mixed * gate, normed_out, out_inverse).astype(bf16)
    grads_ref[:, :width] = (grad_mixed * normed_out * dsilu_ref[:, :width]).astype(bf16)

    for turn in range(bals):
        at = pl.ds(pl.multiple_of((bal ^ turn) * part, part), part)
        early_refs[turn][:, :width] = matmul(mt_ref[at, :], cot).astype(bf16)
        early_refs[turn][:, width:] = matmul(nt_ref[at, :], grads_ref[:, :width]).astype(bf16)

    for slot in range(slots):
        here = slice(slot * slot_rows, (slot + 1) * slot_rows)
        for pair in range(pairs):
            value, query, key = (part_of(slot, pair, which) for which in range(3))
            lanes = slice(pair * pair_width, (pair + 1) * pair_width)
            upper = split(grad_attended[here, lanes])
            grad_weights = matmul_nt(upper, value)
            grad_scores = (grad_weights * slope_ref[slot * pairs + pair]).astype(bf16)
            grad_value = matmul_tn(weights_ref[slot * pairs + pair], upper)
            grad_query = matmul(side_by_side(grad_scores), split(key)) * score_scale
            grad_key = matmul_tn(grad_scores, split(query)) * score_scale
            for which, found in enumerate((grad_value, grad_query, grad_key)):
                first = (1 + which) * width + pair * pair_width
                at = slice(first, first + pair_width)
                grads_ref[here, at] = (found * dsilu_ref[here, at]).astype(bf16)

    for turn in range(bals):
        at = pl.ds(pl.multiple_of((bal ^ turn) * part, part), part)
        late_refs[turn][...] = matmul(nt_ref[at, :], grads_ref[:, width:]).astype(bf16)

    grad_normed = matmul_nt(grads_ref[...], w_in[...])
    grad_rows = (cot.astype(f32) + norm_back(grad_normed, normed_in, in_inverse)).astype(bf16)
    for group in range(groups):
        x_ref[group] = grad_rows[:, group * piece : (group + 1) * piece]
    for step in range(groups):
        grad_refs[step][...] = x_ref[group_here ^ step]


def sum_rounded(terms):
    total = terms[0].astype(f32)
    for term in terms[1:]:
        total = total + term.astype(f32)
    return total.astype(bf16)


def on_device(
    item_ids, seq_lengths, surplus_slot, helper_map, embed_tables, weight_in, weight_out, cotangent
):
    bal = lax.axis_index("bal")
    emb = lax.axis_index("emb")
    bals = lax.axis_size("bal")
    embs = lax.axis_size("emb")
    tables = item_ids.shape[2]
    groups = embs // tables
    _, rows, width = cotangent.shape
    slots = seq_lengths.shape[2]
    slot_rows = rows // slots
    distinct, columns = embed_tables.shape[1:]
    features = weight_in.shape[1]
    part = distinct // bals
    weight_part = weight_in.shape[0]
    table_here = emb // groups
    group_here = emb % groups
    pos = jnp.stack([bal, group_here, table_here]).astype(jnp.int32)
    params = pltpu.CompilerParams(vmem_limit_bytes=ROOM)


    share = lax.dynamic_slice_in_dim(embed_tables[0], bal * part, part, 0)
    fetched = [emb_swap(share, step * groups, embs) for step in range(1, tables)]
    pieces = [embed_tables[0]] + [piece for one in fetched for piece in with_swapped(one, bals)]

    ids = lax.dynamic_slice_in_dim(
        jnp.transpose(item_ids[0]), table_here * groups * rows, groups * rows, 1
    )
    plane_ids = with_swapped(ids.reshape(tables, groups * slots, 1, slot_rows), bals)
    moves = jnp.concatenate([surplus_slot[:, 0], helper_map[:, 0]])
    moves = jnp.pad(moves, (0, LANES - 2 * bals))[None]
    plane_moves = [moves] + [emb_swap(moves, step, embs) for step in range(1, groups)]

    all_in = with_swapped(weight_in, bals)
    all_out = with_swapped(weight_out, bals)

    found = pl.pallas_call(
        functools.partial(lookup_kernel, groups, slots, tables, bals),
        out_shape=[jax.ShapeDtypeStruct((rows, columns), bf16)] * groups,
        in_specs=[SMEM] * (1 + groups) + [VMEM] * (bals + len(pieces)),
        out_specs=[VMEM] * groups,
        compiler_params=params,
    )(pos, *plane_moves, *plane_ids, *pieces)
    block = [found[0]] + [emb_swap(found[step], step, embs) for step in range(1, groups)]

    pairs = slots * HEADS // 2
    early, late = 2 * width, features - width
    results = pl.pallas_call(
        functools.partial(layer_kernel, groups, bals),
        out_shape=[jax.ShapeDtypeStruct((rows, width), bf16)]
        + [jax.ShapeDtypeStruct((rows, columns), bf16)] * groups
        + [jax.ShapeDtypeStruct((weight_part, early), bf16)] * bals
        + [jax.ShapeDtypeStruct((weight_part, late), bf16)] * bals,
        in_specs=[SMEM] * 4 + [VMEM] * groups + [HBM] * (2 * bals + 1),
        out_specs=[VMEM] * (1 + groups + 2 * bals),
        scratch_shapes=[
            pltpu.VMEM((groups, rows, columns), bf16),
            pltpu.VMEM((width, features), bf16),
            pltpu.VMEM((width, width), bf16),
            pltpu.VMEM((rows, width), bf16),
            pltpu.VMEM((width, rows), bf16),
            pltpu.VMEM((width, rows), bf16),
            pltpu.VMEM((pairs, 2 * slot_rows, slot_rows), bf16),
            pltpu.VMEM((pairs, 2 * slot_rows, slot_rows), f32),
            pltpu.VMEM((rows, width), f32),
            pltpu.VMEM((rows, features - width), bf16),
            pltpu.VMEM((rows, features), f32),
            pltpu.VMEM((rows, features), bf16),
            pltpu.SemaphoreType.DMA((2 * bals + 1,)),
        ],
        compiler_params=params,
    )(
        pos,
        seq_lengths[:, 0, :],
        surplus_slot,
        helper_map,
        *block,
        *all_in,
        *all_out,
        cotangent[0],
    )
    layer_out, results = results[0], results[1:]
    grads, results = results[:groups], results[groups:]
    early_parts, late_parts = results[:bals], results[bals:]

    def over_cores(parts):
        return sum_rounded([parts[0]] + [bal_swap(parts[turn], turn, bals) for turn in range(1, bals)])

    plane_grads = [grads[0]] + [emb_swap(grads[step], step, embs) for step in range(1, groups)]
    weight_sum = jnp.concatenate([over_cores(early_parts), over_cores(late_parts)], axis=1)
    owned = lax.psum_scatter(weight_sum, "emb", scatter_dimension=0, tiled=True)
    total = lax.all_gather(owned, "emb", axis=0, tiled=True)
    sums = pl.pallas_call(
        functools.partial(scatter_kernel, groups, slots, bals),
        out_shape=[jax.ShapeDtypeStruct((tables, part, columns), bf16)] * bals,
        in_specs=[SMEM] * (1 + groups) + [VMEM] * (bals + groups),
        out_specs=[VMEM] * bals,
        compiler_params=params,
    )(pos, *plane_moves, *plane_ids, *plane_grads)
    own_sums = over_cores(sums)
    table_sum = own_sums[0].astype(f32)
    for step in range(1, tables):
        table_sum = table_sum + emb_swap(own_sums[step], step * groups, embs).astype(f32)
    table_scale = (distinct / (bals * item_ids.shape[1])) ** 0.5

    grad_scale = (rows * embs * bals) ** -0.5
    total_out = total[:, :width].astype(f32) * grad_scale
    total_in = total[:, width:].astype(f32) * grad_scale
    return layer_out[None], (table_sum * table_scale)[None], total_in, total_out


def solution(mesh):
    placed = (
        P("bal", None, None),
        P(None, "emb", None),
        P(None, "emb"),
        P(None, "emb"),
        P("emb", None, None),
        P("bal", None),
        P("bal", None),
        P("bal", "emb", None),
    )
    return jax.shard_map(
        on_device,
        mesh=mesh,
        in_specs=placed,
        out_specs=(P("bal", "emb", None), P("emb", "bal", None), P("bal", None), P("bal", None)),
        check_vma=False,
    )
```

```python
import functools

import jax
import jax.numpy as jnp
from jax import lax
from jax.experimental import pallas as pl
from jax.experimental.pallas import tpu as pltpu
from jax.sharding import PartitionSpec as P

HEADS = 8
EPS = 1e-05
LANES = 128
ROOM = 48 * 1024 * 1024

VMEM = pl.BlockSpec(memory_space=pltpu.VMEM)
SMEM = pl.BlockSpec(memory_space=pltpu.SMEM)
HBM = pl.BlockSpec(memory_space=pltpu.HBM)
f32 = jnp.float32
bf16 = jnp.bfloat16


def matmul(left, right):
    return lax.dot_general(left, right, (((1,), (0,)), ((), ())), preferred_element_type=f32)


def matmul_nt(left, right):
    return lax.dot_general(left, right, (((1,), (1,)), ((), ())), preferred_element_type=f32)


def matmul_tn(left, right):
    return lax.dot_general(left, right, (((0,), (0,)), ((), ())), preferred_element_type=f32)


def sigmoid(value):
    return 0.5 * jnp.tanh(0.5 * value) + 0.5


def bal_swap(value, step, count):
    return lax.ppermute(value, "bal", [(i, i ^ step) for i in range(count)])


def with_swapped(value, count):
    return [value] + [bal_swap(value, turn, count) for turn in range(1, count)]


def emb_swap(value, step, count):
    return lax.ppermute(value, "emb", [(i, i ^ step) for i in range(count)])


class Scalars:
    def __init__(self, ref, bals, slots):
        self.ref, self.bals, self.slots = ref, bals, slots

    def surplus(self, bal):
        return self.ref[0, bal]

    def source(self, bal):
        found = jnp.int32(0)
        for index in range(self.bals):
            found = found + jnp.where(self.ref[0, self.bals + index] == bal, index, 0)
        return found

    def length(self, bal, slot):
        return self.ref[0, 2 * self.bals + bal * self.slots + slot]

    def place(self):
        first = self.bals * (2 + self.slots)
        return self.ref[0, first], self.ref[0, first + 1], self.ref[0, first + 2]


def pick_ids(scalars, ids_refs, slots, tables):
    bal, group_here, _ = scalars[0].place()
    found = []
    for step, there in enumerate(scalars):
        group = group_here ^ step
        my_slot = there.surplus(bal)
        source = there.source(bal)
        from_slot = there.surplus(source)
        by_slot = [[] for _ in range(slots)]
        for table in tables:
            arrived = ids_refs[0][table, group * slots + from_slot]
            for turn in range(1, len(ids_refs)):
                other = ids_refs[turn][table, group * slots + from_slot]
                arrived = jnp.where(source ^ bal == turn, other, arrived)
            for slot in range(slots):
                own = ids_refs[0][table, group * slots + slot]
                by_slot[slot].append(jnp.where(my_slot == slot, arrived, own))
        found.append(by_slot)
    return found


def table_order(table_here, tables):
    return [table_here ^ step for step in range(tables)]


def stage_kernel(*refs):
    count = len(refs) // 2
    copies = [
        pltpu.make_async_copy(refs[index], refs[count + index], refs[-1].at[index])
        for index in range(count)
    ]
    for copy in copies:
        copy.start()
    for copy in copies:
        copy.wait()


def lookup_kernel(groups, slots, tables, bals, *refs):
    refs = list(refs)
    take = lambda count: [refs.pop(0) for _ in range(count)]
    scalars = [Scalars(ref, bals, slots) for ref in take(groups)]
    ids_refs = take(bals)
    (own_ref,) = take(1)
    others = [take(bals) for _ in range(1, tables)]
    out_refs = refs
    bal, _, table_here = scalars[0].place()
    distinct, columns = own_ref.shape
    part = distinct // bals
    slot_rows = ids_refs[0].shape[3]
    lane = lax.broadcasted_iota(jnp.int32, (LANES, LANES), 1)
    ids = pick_ids(scalars, ids_refs, slots, table_order(table_here, tables))
    for group in range(groups):
        for slot in range(slots):
            for first in range(0, slot_rows, LANES):
                total = jnp.zeros((LANES, columns), f32)
                for table in range(tables):
                    row = ids[group][slot][table][:, first : first + LANES]
                    column = jnp.transpose(jnp.broadcast_to(row, (LANES, LANES)))
                    if table == 0:
                        pieces = [(own_ref, 0, distinct)]
                    else:
                        pieces = [
                            (ref, (bal ^ turn) * part, part)
                            for turn, ref in enumerate(others[table - 1])
                        ]
                    for ref, start, height in pieces:
                        shifted = column - start
                        hot = jnp.concatenate(
                            [
                                jnp.where(shifted == lane + at, 1.0, 0.0).astype(bf16)
                                for at in range(0, height, LANES)
                            ],
                            axis=1,
                        )
                        total = total + matmul(hot, ref[...])
                at = slot * slot_rows + first
                out_refs[group][at : at + LANES, :] = total.astype(bf16)


def scatter_kernel(groups, slots, bals, *refs):
    refs = list(refs)
    take = lambda count: [refs.pop(0) for _ in range(count)]
    scalars = [Scalars(ref, bals, slots) for ref in take(groups)]
    ids_refs, grad_refs, out_refs = take(bals), take(groups), refs
    bal, _, table_here = scalars[0].place()
    tables, part, _ = out_refs[0].shape
    slot_rows = ids_refs[0].shape[3]
    height = min(part, 256)
    iota = lax.broadcasted_iota(jnp.int32, (height, slot_rows), 0)
    ids = pick_ids(scalars, ids_refs, slots, table_order(table_here, tables))
    grads = jnp.concatenate([ref[...] for ref in grad_refs], axis=0)
    for table in range(tables):
        for turn in range(bals):
            for at in range(0, part, height):
                start = (bal ^ turn) * part + at
                hot = jnp.concatenate(
                    [
                        jnp.where(iota == ids[group][slot][table] - start, 1.0, 0.0).astype(bf16)
                        for group in range(groups)
                        for slot in range(slots)
                    ],
                    axis=1,
                )
                out_refs[turn][table, at : at + height, :] = matmul(hot, grads).astype(bf16)


def norm(values):
    average = jnp.mean(values, axis=1, keepdims=True)
    centred = values - average
    inverse = lax.rsqrt(jnp.mean(centred * centred, axis=1, keepdims=True) + EPS)
    return centred * inverse, inverse


def norm_back(incoming, normed, inverse):
    first = jnp.mean(incoming, axis=1, keepdims=True)
    second = jnp.mean(incoming * normed, axis=1, keepdims=True)
    return inverse * (incoming - first - normed * second)


def layer_kernel(groups, slots, tables, bals, unit, scalar_ref, *refs):
    refs = list(refs)
    take = lambda count: [refs.pop(0) for _ in range(count)]
    block_refs = take(groups)
    in_refs = take(bals)
    out_refs = take(bals)
    (cot_ref,) = take(1)
    (layer_ref,) = take(1)
    grad_refs = take(groups)
    far_refs = take(bals)
    near_refs = take(bals)
    (x_ref, w_in, w_out, cot_here, nt_ref, mt_ref, weights_ref, slope_ref, gate_ref, heads_ref, dsilu_ref, grads_ref, sems) = refs

    scalars = Scalars(scalar_ref, bals, slots)
    bal, group_here, table_here = scalars.place()
    rows, width = cot_here.shape
    slot_rows = rows // slots
    head_width = width // HEADS
    score_scale = head_width**-0.5
    piece = block_refs[0].shape[1]
    part, features = in_refs[0].shape

    in_copies, out_copies = [], []
    for turn in range(bals):
        at = pl.ds(pl.multiple_of((bal ^ turn) * part, part), part)
        in_copies.append(pltpu.make_async_copy(in_refs[turn], w_in.at[at, :], sems.at[2 * turn]))
        out_copies.append(pltpu.make_async_copy(out_refs[turn], w_out.at[at, :], sems.at[2 * turn + 1]))
    cot_copy = pltpu.make_async_copy(cot_ref, cot_here, sems.at[2 * bals])
    for copy in in_copies + out_copies + [cot_copy]:
        copy.start()

    my_slot = scalars.surplus(bal)
    source = scalars.source(bal)
    moved = scalars.length(source, scalars.surplus(source))
    lengths = [jnp.where(my_slot == slot, moved, scalars.length(bal, slot)) for slot in range(slots)]

    for step in range(groups):
        x_ref[group_here ^ step] = block_refs[step][...]
    x = jnp.concatenate([x_ref[group] for group in range(groups)], axis=1).astype(f32)
    normed_in, in_inverse = norm(x)
    nt_ref[...] = jnp.transpose(normed_in).astype(bf16)
    for copy in in_copies:
        copy.wait()
    projected = matmul(normed_in.astype(bf16), w_in[...])
    logistic = sigmoid(projected)
    active = projected * logistic
    dsilu_ref[...] = logistic + active * (1.0 - logistic)
    gate_ref[...] = active[:, :width]
    heads_ref[...] = active[:, width:].astype(bf16)

    pair_width = 2 * head_width
    low = lax.broadcasted_iota(jnp.int32, (slot_rows, pair_width), 1) < head_width
    row_at = lax.broadcasted_iota(jnp.int32, (slot_rows, slot_rows), 0)
    col_at = lax.broadcasted_iota(jnp.int32, (slot_rows, slot_rows), 1)

    def split(value):
        zero = jnp.zeros_like(value)
        return jnp.concatenate([jnp.where(low, value, zero), jnp.where(low, zero, value)], axis=0)

    def side_by_side(value):
        return jnp.concatenate([value[:slot_rows], value[slot_rows:]], axis=1)

    def part_of(slot, pair, which):
        first = which * width + pair * pair_width
        return heads_ref[slot * slot_rows : (slot + 1) * slot_rows, first : first + pair_width]

    pairs = HEADS // 2
    attended = []
    for slot in range(slots):
        live = (col_at <= row_at) & (row_at < lengths[slot])
        allowed = jnp.where(live, 1.0 / slot_rows, 0.0)
        allowed = jnp.concatenate([allowed, allowed], axis=0)
        across = []
        for pair in range(pairs):
            value, query, key = (part_of(slot, pair, which) for which in range(3))
            scores = matmul_nt(split(query), key) * score_scale
            q = sigmoid(scores)
            sq = scores * q
            weights = (sq * allowed).astype(bf16)
            weights_ref[slot * pairs + pair] = weights
            slope_ref[slot * pairs + pair] = allowed * (q + sq * (1.0 - q))
            across.append(matmul(side_by_side(weights), split(value)))
        attended.append(jnp.concatenate(across, axis=1))
    normed_out, out_inverse = norm(jnp.concatenate(attended, axis=0))
    gate = gate_ref[...]
    mixed = normed_out * gate
    mt_ref[...] = jnp.transpose(mixed).astype(bf16)
    for copy in out_copies + [cot_copy]:
        copy.wait()
    layer_ref[...] = (x + matmul(mixed.astype(bf16), w_out[...])).astype(bf16)

    cot = cot_here[...]
    grad_mixed = matmul_nt(cot, w_out[...])
    grad_attended = norm_back(grad_mixed * gate, normed_out, out_inverse).astype(bf16)
    grads_ref[:, :width] = (grad_mixed * normed_out * dsilu_ref[:, :width]).astype(bf16)

    def owner_order(ref, turn, far):
        start = (bal ^ turn) * part
        if part != groups * tables * unit:
            half = part // 2
            at = pl.multiple_of(start + (0 if far else half), half)
            return ref[pl.ds(at, half), :]
        steps = range(tables // 2, tables) if far else range(tables // 2)
        found = []
        for group_step in range(groups):
            for table_step in steps:
                owner = (group_here ^ group_step) * tables + (table_here ^ table_step)
                at = pl.multiple_of(start + owner * unit, unit)
                found.append(ref[pl.ds(at, unit), :])
        return jnp.concatenate(found, axis=0)

    for turn in range(bals):
        for far, out in ((True, far_refs[turn]), (False, near_refs[turn])):
            out[:, features:] = matmul(owner_order(mt_ref, turn, far), cot).astype(bf16)

    for slot in range(slots):
        here = slice(slot * slot_rows, (slot + 1) * slot_rows)
        for pair in range(pairs):
            value, query, key = (part_of(slot, pair, which) for which in range(3))
            lanes = slice(pair * pair_width, (pair + 1) * pair_width)
            upper = split(grad_attended[here, lanes])
            grad_weights = matmul_nt(upper, value)
            grad_scores = (grad_weights * slope_ref[slot * pairs + pair]).astype(bf16)
            grad_value = matmul_tn(weights_ref[slot * pairs + pair], upper)
            grad_query = matmul(side_by_side(grad_scores), split(key)) * score_scale
            grad_key = matmul_tn(grad_scores, split(query)) * score_scale
            for which, found in enumerate((grad_value, grad_query, grad_key)):
                first = (1 + which) * width + pair * pair_width
                at = slice(first, first + pair_width)
                grads_ref[here, at] = (found * dsilu_ref[here, at]).astype(bf16)

    for turn in range(bals):
        for far, out in ((True, far_refs[turn]), (False, near_refs[turn])):
            out[:, :features] = matmul(owner_order(nt_ref, turn, far), grads_ref[...]).astype(bf16)

    grad_normed = matmul_nt(grads_ref[...], w_in[...])
    grad_rows = (cot.astype(f32) + norm_back(grad_normed, normed_in, in_inverse)).astype(bf16)
    for group in range(groups):
        x_ref[group] = grad_rows[:, group * piece : (group + 1) * piece]
    for step in range(groups):
        grad_refs[step][...] = x_ref[group_here ^ step]


def place_kernel(scale, groups, slots, tables, bals, unit, scalar_ref, *refs):
    pieces = refs[: 2 * groups]
    in_ref, out_ref, scaled_ref, sems = refs[2 * groups :]
    _, group_here, table_here = Scalars(scalar_ref, bals, slots).place()
    features = in_ref.shape[1]
    half = tables // 2
    copies = []
    for index, piece in enumerate(pieces):
        far, group_step = divmod(index, groups)
        for inner in range(half):
            table_step = far * half + inner
            at = (index * half + inner) * unit
            scaled_ref[at : at + unit, :] = piece[inner * unit : (inner + 1) * unit, :].astype(f32) * scale
            owner = (group_here ^ group_step) * tables + (table_here ^ table_step)
            to = pl.ds(pl.multiple_of(owner * unit, unit), unit)
            rows = scaled_ref.at[pl.ds(at, unit), :]
            sem = sems.at[index * half + inner]
            copies.append(
                pltpu.make_async_copy(rows.at[:, pl.ds(0, features)], in_ref.at[to, :], sem.at[0])
            )
            copies.append(
                pltpu.make_async_copy(
                    rows.at[:, pl.ds(features, out_ref.shape[1])], out_ref.at[to, :], sem.at[1]
                )
            )
            copies[-2].start()
            copies[-1].start()
    for copy in copies:
        copy.wait()


def sum_rounded(terms):
    total = terms[0].astype(f32)
    for term in terms[1:]:
        total = total + term.astype(f32)
    return total.astype(bf16)


def after(value, *others):
    return lax.optimization_barrier((value,) + others)[0]


def on_device(
    item_ids, seq_lengths, surplus_slot, helper_map, embed_tables, weight_in, weight_out, cotangent
):
    bal = lax.axis_index("bal")
    emb = lax.axis_index("emb")
    bals = lax.axis_size("bal")
    embs = lax.axis_size("emb")
    tables = item_ids.shape[2]
    groups = embs // tables
    _, rows, width = cotangent.shape
    slots = seq_lengths.shape[2]
    slot_rows = rows // slots
    distinct, columns = embed_tables.shape[1:]
    part = distinct // bals
    weight_part = weight_in.shape[0]
    table_here = emb // groups
    group_here = emb % groups
    width, features = weight_out.shape[1], weight_in.shape[1]
    unit = weight_part // embs
    owned = unit % 16 == 0 and tables % 2 == 0
    unit = unit if owned else 0
    params = pltpu.CompilerParams(vmem_limit_bytes=ROOM)
    place = jnp.stack([bal, group_here, table_here]).astype(jnp.int32)
    scalars = jnp.concatenate(
        [surplus_slot[:, 0], helper_map[:, 0], seq_lengths[:, 0, :].reshape(-1), place]
    )
    scalars = jnp.pad(scalars, (0, LANES - scalars.shape[0]))[None]

    share = lax.dynamic_slice_in_dim(embed_tables[0], bal * part, part, 0)
    fetched = [emb_swap(share, step * groups, embs) for step in range(1, tables)]

    ids = lax.dynamic_slice_in_dim(
        jnp.transpose(after(item_ids[0], share)), table_here * groups * rows, groups * rows, 1
    )
    plane_ids = with_swapped(ids.reshape(tables, groups * slots, 1, slot_rows), bals)
    sent = after(scalars, fetched[0])
    plane_scalars = [scalars] + [emb_swap(sent, step, embs) for step in range(1, groups)]

    all_in = with_swapped(weight_in, bals)
    all_out = with_swapped(weight_out, bals)
    to_stage = [embed_tables[0], weight_in, weight_out, cotangent[0]]
    own_table, own_in, own_out, cot = pl.pallas_call(
        stage_kernel,
        out_shape=[jax.ShapeDtypeStruct(value.shape, value.dtype) for value in to_stage],
        in_specs=[HBM] * len(to_stage),
        out_specs=[VMEM] * len(to_stage),
        scratch_shapes=[pltpu.SemaphoreType.DMA((len(to_stage),))],
        compiler_params=params,
    )(*to_stage)
    fetched[-1] = after(fetched[-1], own_table)
    pieces = [own_table] + [piece for one in fetched for piece in with_swapped(one, bals)]

    found = pl.pallas_call(
        functools.partial(lookup_kernel, groups, slots, tables, bals),
        out_shape=[jax.ShapeDtypeStruct((rows, columns), bf16)] * groups,
        in_specs=[SMEM] * groups + [VMEM] * (bals + len(pieces)),
        out_specs=[VMEM] * groups,
        compiler_params=params,
    )(*plane_scalars, *plane_ids, *pieces)
    block = [found[0]] + [emb_swap(found[step], step, embs) for step in range(1, groups)]

    pairs = slots * HEADS // 2
    terms = jax.ShapeDtypeStruct((weight_part // 2, features + width), bf16)
    results = pl.pallas_call(
        functools.partial(layer_kernel, groups, slots, tables, bals, unit),
        out_shape=[jax.ShapeDtypeStruct((rows, width), bf16)]
        + [jax.ShapeDtypeStruct((rows, columns), bf16)] * groups
        + [terms] * (2 * bals),
        in_specs=[SMEM] + [VMEM] * groups + [HBM] * (2 * bals + 1),
        out_specs=[VMEM] * (1 + groups + 2 * bals),
        scratch_shapes=[
            pltpu.VMEM((groups, rows, columns), bf16),
            pltpu.VMEM((width, features), bf16),
            pltpu.VMEM((width, width), bf16),
            pltpu.VMEM((rows, width), bf16),
            pltpu.VMEM((width, rows), bf16),
            pltpu.VMEM((width, rows), bf16),
            pltpu.VMEM((pairs, 2 * slot_rows, slot_rows), bf16),
            pltpu.VMEM((pairs, 2 * slot_rows, slot_rows), f32),
            pltpu.VMEM((rows, width), f32),
            pltpu.VMEM((rows, features - width), bf16),
            pltpu.VMEM((rows, features), f32),
            pltpu.VMEM((rows, features), bf16),
            pltpu.SemaphoreType.DMA((2 * bals + 1,)),
        ],
        compiler_params=params,
    )(scalars, *block, own_in, *all_in[1:], own_out, *all_out[1:], cot)
    layer_out, results = results[0], results[1:]
    grads, results = results[:groups], results[groups:]
    far_terms, near_terms = results[:bals], results[bals:]

    def over_cores(parts):
        return [parts[0]] + [bal_swap(parts[turn], turn, bals) for turn in range(1, bals)]

    def over_plane(value, *others):
        pieces = value.reshape(groups, value.shape[0] // groups, value.shape[1])
        came = [emb_swap(pieces[step], step, embs) for step in range(1, groups)]
        return sum_rounded([pieces[0]] + [after(piece, *others) for piece in came])

    def to_plane(value):
        return [value] + [emb_swap(value, step, embs) for step in range(1, groups)]

    far_terms = over_cores(far_terms)
    near_terms = over_cores([near_terms[0]] + [after(term, far_terms[-1]) for term in near_terms[1:]])
    far, near = sum_rounded(far_terms), sum_rounded(near_terms)
    grad_scale = (rows * embs * bals) ** -0.5
    if owned:
        half = tables // 2
        far, near = over_plane(far, near), over_plane(near)
        grads = [grads[0]] + [after(grad, far) for grad in grads[1:]]
        rel = [near[at * unit : (at + 1) * unit] for at in range(half)]
        rel += [far[at * unit : (at + 1) * unit] for at in range(half)]
        final = sum_rounded(
            [rel[0]] + [emb_swap(rel[step], step * groups, embs) for step in range(1, tables)]
        )
        gathered = [final] + [emb_swap(final, step * groups, embs) for step in range(1, tables)]
        ready = gathered[half - 1]
        back = to_plane(jnp.concatenate(gathered[:half], axis=0))
        back += to_plane(jnp.concatenate(gathered[half:], axis=0))
        total_in, total_out = pl.pallas_call(
            functools.partial(place_kernel, grad_scale, groups, slots, tables, bals, unit),
            out_shape=[
                jax.ShapeDtypeStruct((weight_part, features), f32),
                jax.ShapeDtypeStruct((weight_part, width), f32),
            ],
            in_specs=[SMEM] + [VMEM] * (2 * groups),
            out_specs=[HBM] * 2,
            scratch_shapes=[
                pltpu.VMEM((weight_part, features + width), f32),
                pltpu.SemaphoreType.DMA((groups * tables, 2)),
            ],
            compiler_params=params,
        )(scalars, *back)
    else:
        total = lax.psum(jnp.concatenate([far, near], axis=0).astype(f32), "emb") * grad_scale
        total_in, total_out = total[:, :features], total[:, features:]
        ready = far

    plane_grads = [grads[0]] + [emb_swap(grads[step], step, embs) for step in range(1, groups)]
    sums = pl.pallas_call(
        functools.partial(scatter_kernel, groups, slots, bals),
        out_shape=[jax.ShapeDtypeStruct((tables, part, columns), bf16)] * bals,
        in_specs=[SMEM] * groups + [VMEM] * (bals + groups),
        out_specs=[VMEM] * bals,
        compiler_params=params,
    )(*plane_scalars, *plane_ids, *plane_grads)
    own_sums = after(sum_rounded(over_cores(sums)), ready)
    table_sum = own_sums[0].astype(f32)
    for step in range(1, tables):
        table_sum = table_sum + emb_swap(own_sums[step], step * groups, embs).astype(f32)
    table_scale = (distinct / (bals * item_ids.shape[1])) ** 0.5
    return layer_out[None], (table_sum * table_scale)[None], total_in, total_out


def solution(mesh):
    placed = (
        P("bal", None, None),
        P(None, "emb", None),
        P(None, "emb"),
        P(None, "emb"),
        P("emb", None, None),
        P("bal", None),
        P("bal", None),
        P("bal", "emb", None),
    )
    return jax.shard_map(
        on_device,
        mesh=mesh,
        in_specs=placed,
        out_specs=(P("bal", "emb", None), P("emb", "bal", None), P("bal", None), P("bal", None)),
        check_vma=False,
    )
```

```python
import functools

import jax
import jax.numpy as jnp
from jax import lax
from jax.experimental import pallas as pl
from jax.experimental.pallas import tpu as pltpu
from jax.sharding import PartitionSpec as P

HEADS = 8
EPS = 1e-05
LANES = 128

VMEM = pl.BlockSpec(memory_space=pltpu.VMEM)
SMEM = pl.BlockSpec(memory_space=pltpu.SMEM)
HBM = pl.BlockSpec(memory_space=pltpu.HBM)
f32 = jnp.float32
bf16 = jnp.bfloat16


def room(mib):
    return pltpu.CompilerParams(vmem_limit_bytes=mib * 1024 * 1024)


def estimate(microseconds):
    return pl.CostEstimate(flops=0, bytes_accessed=microseconds * 3_500_000, transcendentals=0)


def matmul(left, right):
    return lax.dot_general(left, right, (((1,), (0,)), ((), ())), preferred_element_type=f32)


def matmul_nt(left, right):
    return lax.dot_general(left, right, (((1,), (1,)), ((), ())), preferred_element_type=f32)


def matmul_tn(left, right):
    return lax.dot_general(left, right, (((0,), (0,)), ((), ())), preferred_element_type=f32)


def sigmoid(value):
    return 0.5 * jnp.tanh(0.5 * value) + 0.5


def bal_swap(value, step, count):
    return lax.ppermute(value, "bal", [(i, i ^ step) for i in range(count)])


def with_swapped(value, count):
    return [value] + [bal_swap(value, turn, count) for turn in range(1, count)]


def emb_swap(value, step, count):
    return lax.ppermute(value, "emb", [(i, i ^ step) for i in range(count)])


class Scalars:
    def __init__(self, ref, bals, slots):
        self.ref, self.bals, self.slots = ref, bals, slots

    def surplus(self, bal):
        return self.ref[0, bal]

    def source(self, bal):
        found = jnp.int32(0)
        for index in range(self.bals):
            found = found + jnp.where(self.ref[0, self.bals + index] == bal, index, 0)
        return found

    def length(self, bal, slot):
        return self.ref[0, 2 * self.bals + bal * self.slots + slot]

    def place(self):
        first = self.bals * (2 + self.slots)
        return self.ref[0, first], self.ref[0, first + 1], self.ref[0, first + 2]


def pick_ids(scalars, ids_refs, slots, tables):
    bal, group_here, _ = scalars[0].place()
    found = []
    for step, there in enumerate(scalars):
        group = group_here ^ step
        my_slot = there.surplus(bal)
        source = there.source(bal)
        from_slot = there.surplus(source)
        by_slot = [[] for _ in range(slots)]
        for table in tables:
            arrived = ids_refs[0][table, group * slots + from_slot]
            for turn in range(1, len(ids_refs)):
                other = ids_refs[turn][table, group * slots + from_slot]
                arrived = jnp.where(source ^ bal == turn, other, arrived)
            for slot in range(slots):
                own = ids_refs[0][table, group * slots + slot]
                by_slot[slot].append(jnp.where(my_slot == slot, arrived, own))
        found.append(by_slot)
    return found


def table_order(table_here, tables):
    return [table_here ^ step for step in range(tables)]


def lookup_kernel(groups, slots, tables, bals, *refs):
    refs = list(refs)
    take = lambda count: [refs.pop(0) for _ in range(count)]
    scalars = [Scalars(ref, bals, slots) for ref in take(groups)]
    ids_refs = take(bals)
    (own_ref,) = take(1)
    others = [take(bals) for _ in range(1, tables)]
    out_refs = refs
    bal, _, table_here = scalars[0].place()
    distinct, columns = own_ref.shape
    part = distinct // bals
    slot_rows = ids_refs[0].shape[3]
    lane = lax.broadcasted_iota(jnp.int32, (LANES, LANES), 1)
    ids = pick_ids(scalars, ids_refs, slots, table_order(table_here, tables))
    for group in range(groups):
        for slot in range(slots):
            for first in range(0, slot_rows, LANES):
                total = jnp.zeros((LANES, columns), f32)
                for table in range(tables):
                    row = ids[group][slot][table][:, first : first + LANES]
                    column = jnp.transpose(jnp.broadcast_to(row, (LANES, LANES)))
                    if table == 0:
                        pieces = [(own_ref, 0, distinct)]
                    else:
                        pieces = [
                            (ref, (bal ^ turn) * part, part)
                            for turn, ref in enumerate(others[table - 1])
                        ]
                    for ref, start, height in pieces:
                        shifted = column - start
                        hot = jnp.concatenate(
                            [
                                jnp.where(shifted == lane + at, 1.0, 0.0).astype(bf16)
                                for at in range(0, height, LANES)
                            ],
                            axis=1,
                        )
                        total = total + matmul(hot, ref[...])
                at = slot * slot_rows + first
                out_refs[group][at : at + LANES, :] = total.astype(bf16)


def scatter_kernel(groups, slots, bals, *refs):
    refs = list(refs)
    take = lambda count: [refs.pop(0) for _ in range(count)]
    scalars = [Scalars(ref, bals, slots) for ref in take(groups)]
    ids_refs, grad_refs, out_refs = take(bals), take(groups), refs
    bal, _, table_here = scalars[0].place()
    tables, part, _ = out_refs[0].shape
    slot_rows = ids_refs[0].shape[3]
    height = min(part, 256)
    iota = lax.broadcasted_iota(jnp.int32, (height, slot_rows), 0)
    ids = pick_ids(scalars, ids_refs, slots, table_order(table_here, tables))
    grads = jnp.concatenate([ref[...] for ref in grad_refs], axis=0)
    for table in range(tables):
        for turn in range(bals):
            for at in range(0, part, height):
                start = (bal ^ turn) * part + at
                hot = jnp.concatenate(
                    [
                        jnp.where(iota == ids[group][slot][table] - start, 1.0, 0.0).astype(bf16)
                        for group in range(groups)
                        for slot in range(slots)
                    ],
                    axis=1,
                )
                out_refs[turn][table, at : at + height, :] = matmul(hot, grads).astype(bf16)


def norm(values):
    average = jnp.mean(values, axis=1, keepdims=True)
    centred = values - average
    inverse = lax.rsqrt(jnp.mean(centred * centred, axis=1, keepdims=True) + EPS)
    return centred * inverse, inverse


def norm_back(incoming, normed, inverse):
    first = jnp.mean(incoming, axis=1, keepdims=True)
    second = jnp.mean(incoming * normed, axis=1, keepdims=True)
    return inverse * (incoming - first - normed * second)


def layer_kernel(groups, slots, tables, bals, unit, scalar_ref, *refs):
    refs = list(refs)
    take = lambda count: [refs.pop(0) for _ in range(count)]
    block_refs = take(groups)
    in_refs = take(bals)
    out_refs = take(bals)
    (cot_ref,) = take(1)
    (layer_ref,) = take(1)
    grad_refs = take(groups)
    term_refs = take(bals)
    (x_ref, w_in, w_out, cot_here, nt_ref, mt_ref, weights_ref, slope_ref, gate_ref, heads_ref, dsilu_ref, grads_ref, sems) = refs

    scalars = Scalars(scalar_ref, bals, slots)
    bal, group_here, table_here = scalars.place()
    rows, width = cot_here.shape
    slot_rows = rows // slots
    head_width = width // HEADS
    score_scale = head_width**-0.5
    piece = block_refs[0].shape[1]
    part, features = in_refs[0].shape

    in_copies, out_copies = [], []
    for turn in range(bals):
        at = pl.ds(pl.multiple_of((bal ^ turn) * part, part), part)
        in_copies.append(pltpu.make_async_copy(in_refs[turn], w_in.at[at, :], sems.at[2 * turn]))
        out_copies.append(pltpu.make_async_copy(out_refs[turn], w_out.at[at, :], sems.at[2 * turn + 1]))
    cot_copy = pltpu.make_async_copy(cot_ref, cot_here, sems.at[2 * bals])
    for copy in in_copies + out_copies + [cot_copy]:
        copy.start()

    my_slot = scalars.surplus(bal)
    source = scalars.source(bal)
    moved = scalars.length(source, scalars.surplus(source))
    lengths = [jnp.where(my_slot == slot, moved, scalars.length(bal, slot)) for slot in range(slots)]

    for step in range(groups):
        x_ref[group_here ^ step] = block_refs[step][...]
    x = jnp.concatenate([x_ref[group] for group in range(groups)], axis=1).astype(f32)
    normed_in, in_inverse = norm(x)
    nt_ref[...] = jnp.transpose(normed_in).astype(bf16)
    for copy in in_copies:
        copy.wait()
    projected = matmul(normed_in.astype(bf16), w_in[...])
    logistic = sigmoid(projected)
    active = projected * logistic
    dsilu_ref[...] = logistic + active * (1.0 - logistic)
    gate_ref[...] = active[:, :width]
    heads_ref[...] = active[:, width:].astype(bf16)

    pair_width = 2 * head_width
    low = lax.broadcasted_iota(jnp.int32, (slot_rows, pair_width), 1) < head_width
    row_at = lax.broadcasted_iota(jnp.int32, (slot_rows, slot_rows), 0)
    col_at = lax.broadcasted_iota(jnp.int32, (slot_rows, slot_rows), 1)

    def split(value):
        zero = jnp.zeros_like(value)
        return jnp.concatenate([jnp.where(low, value, zero), jnp.where(low, zero, value)], axis=0)

    def side_by_side(value):
        return jnp.concatenate([value[:slot_rows], value[slot_rows:]], axis=1)

    def part_of(slot, pair, which):
        first = which * width + pair * pair_width
        return heads_ref[slot * slot_rows : (slot + 1) * slot_rows, first : first + pair_width]

    pairs = HEADS // 2
    attended = []
    for slot in range(slots):
        live = (col_at <= row_at) & (row_at < lengths[slot])
        allowed = jnp.where(live, 1.0 / slot_rows, 0.0)
        allowed = jnp.concatenate([allowed, allowed], axis=0)
        across = []
        for pair in range(pairs):
            value, query, key = (part_of(slot, pair, which) for which in range(3))
            scores = matmul_nt(split(query), key) * score_scale
            q = sigmoid(scores)
            sq = scores * q
            weights = (sq * allowed).astype(bf16)
            weights_ref[slot * pairs + pair] = weights
            slope_ref[slot * pairs + pair] = allowed * (q + sq * (1.0 - q))
            across.append(matmul(side_by_side(weights), split(value)))
        attended.append(jnp.concatenate(across, axis=1))
    normed_out, out_inverse = norm(jnp.concatenate(attended, axis=0))
    gate = gate_ref[...]
    mixed = normed_out * gate
    mt_ref[...] = jnp.transpose(mixed).astype(bf16)
    for copy in out_copies + [cot_copy]:
        copy.wait()
    layer_ref[...] = (x + matmul(mixed.astype(bf16), w_out[...])).astype(bf16)

    cot = cot_here[...]
    grad_mixed = matmul_nt(cot, w_out[...])
    grad_attended = norm_back(grad_mixed * gate, normed_out, out_inverse).astype(bf16)
    grads_ref[:, :width] = (grad_mixed * normed_out * dsilu_ref[:, :width]).astype(bf16)

    def owner_order(ref, turn):
        start = (bal ^ turn) * part
        if part != groups * tables * unit:
            return ref[pl.ds(pl.multiple_of(start, part), part), :]
        found = []
        for group_step in range(groups):
            for table_step in range(tables):
                owner = (group_here ^ group_step) * tables + (table_here ^ table_step)
                at = pl.multiple_of(start + owner * unit, unit)
                found.append(ref[pl.ds(at, unit), :])
        return jnp.concatenate(found, axis=0)

    for turn in range(bals):
        term_refs[turn][:, features:] = matmul(owner_order(mt_ref, turn), cot).astype(bf16)

    for slot in range(slots):
        here = slice(slot * slot_rows, (slot + 1) * slot_rows)
        for pair in range(pairs):
            value, query, key = (part_of(slot, pair, which) for which in range(3))
            lanes = slice(pair * pair_width, (pair + 1) * pair_width)
            upper = split(grad_attended[here, lanes])
            grad_weights = matmul_nt(upper, value)
            grad_scores = (grad_weights * slope_ref[slot * pairs + pair]).astype(bf16)
            grad_value = matmul_tn(weights_ref[slot * pairs + pair], upper)
            grad_query = matmul(side_by_side(grad_scores), split(key)) * score_scale
            grad_key = matmul_tn(grad_scores, split(query)) * score_scale
            for which, found in enumerate((grad_value, grad_query, grad_key)):
                first = (1 + which) * width + pair * pair_width
                at = slice(first, first + pair_width)
                grads_ref[here, at] = (found * dsilu_ref[here, at]).astype(bf16)

    for turn in range(bals):
        term_refs[turn][:, :features] = matmul(owner_order(nt_ref, turn), grads_ref[...]).astype(bf16)

    grad_normed = matmul_nt(grads_ref[...], w_in[...])
    grad_rows = (cot.astype(f32) + norm_back(grad_normed, normed_in, in_inverse)).astype(bf16)
    for group in range(groups):
        x_ref[group] = grad_rows[:, group * piece : (group + 1) * piece]
    for step in range(groups):
        grad_refs[step][...] = x_ref[group_here ^ step]


def place_kernel(scale, groups, slots, tables, bals, unit, scalar_ref, *refs):
    pieces = refs[:groups]
    in_ref, out_ref, scaled_ref, sems = refs[groups:]
    _, group_here, table_here = Scalars(scalar_ref, bals, slots).place()
    features = in_ref.shape[1]
    copies = []
    for group_step, piece in enumerate(pieces):
        for table_step in range(tables):
            index = group_step * tables + table_step
            at = index * unit
            from_rows = slice(table_step * unit, (table_step + 1) * unit)
            scaled_ref[at : at + unit, :] = piece[from_rows, :].astype(f32) * scale
            owner = (group_here ^ group_step) * tables + (table_here ^ table_step)
            to = pl.ds(pl.multiple_of(owner * unit, unit), unit)
            rows = scaled_ref.at[pl.ds(at, unit), :]
            sem = sems.at[index]
            copies.append(
                pltpu.make_async_copy(rows.at[:, pl.ds(0, features)], in_ref.at[to, :], sem.at[0])
            )
            copies.append(
                pltpu.make_async_copy(
                    rows.at[:, pl.ds(features, out_ref.shape[1])], out_ref.at[to, :], sem.at[1]
                )
            )
            copies[-2].start()
            copies[-1].start()
    for copy in copies:
        copy.wait()


def sum_rounded(terms):
    total = terms[0].astype(f32)
    for term in terms[1:]:
        total = total + term.astype(f32)
    return total.astype(bf16)


def after(value, *others):
    return lax.optimization_barrier((value,) + others)[0]


def on_device(
    item_ids, seq_lengths, surplus_slot, helper_map, embed_tables, weight_in, weight_out, cotangent
):
    bal = lax.axis_index("bal")
    emb = lax.axis_index("emb")
    bals = lax.axis_size("bal")
    embs = lax.axis_size("emb")
    tables = item_ids.shape[2]
    groups = embs // tables
    _, rows, width = cotangent.shape
    slots = seq_lengths.shape[2]
    slot_rows = rows // slots
    distinct, columns = embed_tables.shape[1:]
    part = distinct // bals
    weight_part = weight_in.shape[0]
    table_here = emb // groups
    group_here = emb % groups
    width, features = weight_out.shape[1], weight_in.shape[1]
    unit = weight_part // embs
    owned = unit % 16 == 0
    unit = unit if owned else 0
    place = [index.reshape(1, 1).astype(jnp.int32) for index in (bal, group_here, table_here)]
    scalars = [surplus_slot.T, helper_map.T, seq_lengths[:, 0, :].reshape(1, -1)] + place
    scalars = jnp.concatenate(scalars, axis=1)
    scalars = jnp.pad(scalars, ((0, 0), (0, LANES - scalars.shape[1])))

    share = lax.dynamic_slice_in_dim(embed_tables[0], bal * part, part, 0)
    fetched = [emb_swap(share, step * groups, embs) for step in range(1, tables)]

    ids = lax.dynamic_slice_in_dim(
        jnp.transpose(after(item_ids[0], share)), table_here * groups * rows, groups * rows, 1
    )
    plane_ids = with_swapped(ids.reshape(tables, groups * slots, 1, slot_rows), bals)
    sent = after(scalars, fetched[0])
    plane_scalars = [scalars] + [emb_swap(sent, step, embs) for step in range(1, groups)]

    all_in = with_swapped(weight_in, bals)
    all_out = with_swapped(weight_out, bals)
    pieces = [embed_tables[0]] + [piece for one in fetched for piece in with_swapped(one, bals)]

    found = pl.pallas_call(
        functools.partial(lookup_kernel, groups, slots, tables, bals),
        out_shape=[jax.ShapeDtypeStruct((rows, columns), bf16)] * groups,
        in_specs=[SMEM] * groups + [VMEM] * (bals + len(pieces)),
        out_specs=[VMEM] * groups,
        cost_estimate=estimate(3),
        compiler_params=room(16),
    )(*plane_scalars, *plane_ids, *pieces)
    block = [found[0]] + [emb_swap(found[step], step, embs) for step in range(1, groups)]

    pairs = slots * HEADS // 2
    terms = jax.ShapeDtypeStruct((weight_part, features + width), bf16)
    results = pl.pallas_call(
        functools.partial(layer_kernel, groups, slots, tables, bals, unit),
        out_shape=[jax.ShapeDtypeStruct((rows, width), bf16)]
        + [jax.ShapeDtypeStruct((rows, columns), bf16)] * groups
        + [terms] * bals,
        in_specs=[SMEM] + [VMEM] * groups + [HBM] * (2 * bals + 1),
        out_specs=[VMEM] * (1 + groups + bals),
        scratch_shapes=[
            pltpu.VMEM((groups, rows, columns), bf16),
            pltpu.VMEM((width, features), bf16),
            pltpu.VMEM((width, width), bf16),
            pltpu.VMEM((rows, width), bf16),
            pltpu.VMEM((width, rows), bf16),
            pltpu.VMEM((width, rows), bf16),
            pltpu.VMEM((pairs, 2 * slot_rows, slot_rows), bf16),
            pltpu.VMEM((pairs, 2 * slot_rows, slot_rows), f32),
            pltpu.VMEM((rows, width), f32),
            pltpu.VMEM((rows, features - width), bf16),
            pltpu.VMEM((rows, features), f32),
            pltpu.VMEM((rows, features), bf16),
            pltpu.SemaphoreType.DMA((2 * bals + 1,)),
        ],
        cost_estimate=estimate(7),
        compiler_params=room(36),
    )(scalars, *block, *all_in, *all_out, cotangent[0])
    layer_out, results = results[0], results[1:]
    grads, results = results[:groups], results[groups:]

    def over_cores(parts):
        return sum_rounded([parts[0]] + [bal_swap(parts[turn], turn, bals) for turn in range(1, bals)])

    def to_plane(value):
        return [value] + [emb_swap(value, step, embs) for step in range(1, groups)]

    total = over_cores(results)
    plane_grads = [grads[0]] + [emb_swap(grads[step], step, embs) for step in range(1, groups)]
    sums = pl.pallas_call(
        functools.partial(scatter_kernel, groups, slots, bals),
        out_shape=[jax.ShapeDtypeStruct((tables, part, columns), bf16)] * bals,
        in_specs=[SMEM] * groups + [VMEM] * (bals + groups),
        out_specs=[VMEM] * bals,
        cost_estimate=estimate(3),
        compiler_params=room(16),
    )(*plane_scalars, *plane_ids, *plane_grads)
    own_sums = over_cores(sums)

    grad_scale = (rows * embs * bals) ** -0.5
    if owned:
        pieces = total.reshape(groups, weight_part // groups, features + width)
        came = [after(emb_swap(pieces[step], step, embs), sums[0]) for step in range(1, groups)]
        mine = sum_rounded([pieces[0]] + came)
        mine = mine.reshape(tables, unit, features + width)
        final = sum_rounded(
            [mine[0]] + [emb_swap(mine[step], step * groups, embs) for step in range(1, tables)]
        )
        gathered = [final] + [emb_swap(final, step * groups, embs) for step in range(1, tables)]
        own_sums = after(own_sums, *gathered[1:])
        back = to_plane(jnp.concatenate(gathered, axis=0))

    table_sum = own_sums[0].astype(f32)
    for step in range(1, tables):
        table_sum = table_sum + emb_swap(own_sums[step], step * groups, embs).astype(f32)
    table_scale = (distinct / (bals * item_ids.shape[1])) ** 0.5

    if owned:
        total_in, total_out = pl.pallas_call(
            functools.partial(place_kernel, grad_scale, groups, slots, tables, bals, unit),
            out_shape=[
                jax.ShapeDtypeStruct((weight_part, features), f32),
                jax.ShapeDtypeStruct((weight_part, width), f32),
            ],
            in_specs=[SMEM] + [VMEM] * groups,
            out_specs=[HBM] * 2,
            scratch_shapes=[
                pltpu.VMEM((weight_part, features + width), f32),
                pltpu.SemaphoreType.DMA((groups * tables, 2)),
            ],
            cost_estimate=estimate(2),
            compiler_params=room(12),
        )(scalars, *back)
    else:
        total = lax.psum(total.astype(f32), "emb") * grad_scale
        total_in, total_out = total[:, :features], total[:, features:]

    return layer_out[None], (table_sum * table_scale)[None], total_in, total_out


def solution(mesh):
    placed = (
        P("bal", None, None),
        P(None, "emb", None),
        P(None, "emb"),
        P(None, "emb"),
        P("emb", None, None),
        P("bal", None),
        P("bal", None),
        P("bal", "emb", None),
    )
    return jax.shard_map(
        on_device,
        mesh=mesh,
        in_specs=placed,
        out_specs=(P("bal", "emb", None), P("emb", "bal", None), P("bal", None), P("bal", None)),
        check_vma=False,
    )
```

```python
import functools

import jax
import jax.numpy as jnp
from jax import lax
from jax.experimental import pallas as pl
from jax.experimental.pallas import tpu as pltpu
from jax.sharding import PartitionSpec as P

HEADS = 8
EPS = 1e-05
LANES = 128

VMEM = pl.BlockSpec(memory_space=pltpu.VMEM)
SMEM = pl.BlockSpec(memory_space=pltpu.SMEM)
HBM = pl.BlockSpec(memory_space=pltpu.HBM)
f32 = jnp.float32
bf16 = jnp.bfloat16


def room(mib):
    return pltpu.CompilerParams(vmem_limit_bytes=mib * 1024 * 1024)


def estimate(microseconds):
    return pl.CostEstimate(flops=0, bytes_accessed=microseconds * 3_500_000, transcendentals=0)


def matmul(left, right):
    return lax.dot_general(left, right, (((1,), (0,)), ((), ())), preferred_element_type=f32)


def matmul_nt(left, right):
    return lax.dot_general(left, right, (((1,), (1,)), ((), ())), preferred_element_type=f32)


def matmul_tn(left, right):
    return lax.dot_general(left, right, (((0,), (0,)), ((), ())), preferred_element_type=f32)


def sigmoid(value):
    return 0.5 * jnp.tanh(0.5 * value) + 0.5


def bal_swap(value, step, count):
    return lax.ppermute(value, "bal", [(i, i ^ step) for i in range(count)])


def with_swapped(value, count):
    return [value] + [bal_swap(value, turn, count) for turn in range(1, count)]


def emb_swap(value, step, count):
    return lax.ppermute(value, "emb", [(i, i ^ step) for i in range(count)])


class Scalars:
    def __init__(self, ref, bals, slots):
        self.ref, self.bals, self.slots = ref, bals, slots

    def surplus(self, bal):
        return self.ref[0, bal]

    def source(self, bal):
        found = jnp.int32(0)
        for index in range(self.bals):
            found = found + jnp.where(self.ref[0, self.bals + index] == bal, index, 0)
        return found

    def length(self, bal, slot):
        return self.ref[0, 2 * self.bals + bal * self.slots + slot]

    def place(self):
        first = self.bals * (2 + self.slots)
        return self.ref[0, first], self.ref[0, first + 1], self.ref[0, first + 2]


def pick_ids(scalars, ids_refs, slots, tables):
    bal, group_here, _ = scalars[0].place()
    found = []
    for step, there in enumerate(scalars):
        group = group_here ^ step
        my_slot = there.surplus(bal)
        source = there.source(bal)
        from_slot = there.surplus(source)
        by_slot = [[] for _ in range(slots)]
        for table in tables:
            arrived = ids_refs[0][table, group * slots + from_slot]
            for turn in range(1, len(ids_refs)):
                other = ids_refs[turn][table, group * slots + from_slot]
                arrived = jnp.where(source ^ bal == turn, other, arrived)
            for slot in range(slots):
                own = ids_refs[0][table, group * slots + slot]
                by_slot[slot].append(jnp.where(my_slot == slot, arrived, own))
        found.append(by_slot)
    return found


def table_order(table_here, tables):
    return [table_here ^ step for step in range(tables)]


def lookup_kernel(groups, slots, tables, bals, *refs):
    refs = list(refs)
    take = lambda count: [refs.pop(0) for _ in range(count)]
    scalars = [Scalars(ref, bals, slots) for ref in take(groups)]
    ids_refs = take(bals)
    pieces = [take(bals) for _ in range(tables)]
    out_refs = refs
    bal, _, table_here = scalars[0].place()
    part, columns = pieces[0][0].shape
    slot_rows = ids_refs[0].shape[3]
    lane = lax.broadcasted_iota(jnp.int32, (LANES, LANES), 1)
    ids = pick_ids(scalars, ids_refs, slots, table_order(table_here, tables))
    for group in range(groups):
        for slot in range(slots):
            for first in range(0, slot_rows, LANES):
                total = jnp.zeros((LANES, columns), f32)
                for table in range(tables):
                    row = ids[group][slot][table][:, first : first + LANES]
                    column = jnp.transpose(jnp.broadcast_to(row, (LANES, LANES)))
                    for turn, ref in enumerate(pieces[table]):
                        shifted = column - (bal ^ turn) * part
                        hot = jnp.concatenate(
                            [
                                jnp.where(shifted == lane + at, 1.0, 0.0).astype(bf16)
                                for at in range(0, part, LANES)
                            ],
                            axis=1,
                        )
                        total = total + matmul(hot, ref[...])
                at = slot * slot_rows + first
                out_refs[group][at : at + LANES, :] = total.astype(bf16)


def scatter_kernel(groups, slots, bals, *refs):
    refs = list(refs)
    take = lambda count: [refs.pop(0) for _ in range(count)]
    scalars = [Scalars(ref, bals, slots) for ref in take(groups)]
    ids_refs, grad_refs, out_refs = take(bals), take(groups), refs
    bal, _, table_here = scalars[0].place()
    tables, part, _ = out_refs[0].shape
    slot_rows = ids_refs[0].shape[3]
    height = min(part, 256)
    iota = lax.broadcasted_iota(jnp.int32, (height, slot_rows), 0)
    ids = pick_ids(scalars, ids_refs, slots, table_order(table_here, tables))
    grads = jnp.concatenate([ref[...] for ref in grad_refs], axis=0)
    for table in range(tables):
        for turn in range(bals):
            for at in range(0, part, height):
                start = (bal ^ turn) * part + at
                hot = jnp.concatenate(
                    [
                        jnp.where(iota == ids[group][slot][table] - start, 1.0, 0.0).astype(bf16)
                        for group in range(groups)
                        for slot in range(slots)
                    ],
                    axis=1,
                )
                out_refs[turn][table, at : at + height, :] = matmul(hot, grads).astype(bf16)


def norm(values):
    average = jnp.mean(values, axis=1, keepdims=True)
    centred = values - average
    inverse = lax.rsqrt(jnp.mean(centred * centred, axis=1, keepdims=True) + EPS)
    return centred * inverse, inverse


def norm_back(incoming, normed, inverse):
    first = jnp.mean(incoming, axis=1, keepdims=True)
    second = jnp.mean(incoming * normed, axis=1, keepdims=True)
    return inverse * (incoming - first - normed * second)


def layer_kernel(groups, slots, tables, bals, unit, scalar_ref, *refs):
    refs = list(refs)
    take = lambda count: [refs.pop(0) for _ in range(count)]
    block_refs = take(groups)
    weight_refs = take(bals)
    (cot_ref,) = take(1)
    (layer_ref,) = take(1)
    grad_refs = take(groups)
    term_refs = take(bals)
    (x_ref, w_in, w_out, nt_ref, mt_ref, weights_ref, slope_ref, gate_ref, heads_ref, dsilu_ref, grads_ref, sems) = refs

    scalars = Scalars(scalar_ref, bals, slots)
    bal, group_here, table_here = scalars.place()
    rows, width = cot_ref.shape
    slot_rows = rows // slots
    head_width = width // HEADS
    score_scale = head_width**-0.5
    piece = block_refs[0].shape[1]
    part, features = weight_refs[0].shape[0], w_in.shape[1]

    in_copies, out_copies = [], []
    for turn in range(bals):
        at = pl.ds(pl.multiple_of((bal ^ turn) * part, part), part)
        here = weight_refs[turn]
        in_copies.append(
            pltpu.make_async_copy(here.at[:, pl.ds(0, features)], w_in.at[at, :], sems.at[2 * turn])
        )
        out_copies.append(
            pltpu.make_async_copy(
                here.at[:, pl.ds(features, width)], w_out.at[at, :], sems.at[2 * turn + 1]
            )
        )
    for copy in in_copies + out_copies:
        copy.start()

    my_slot = scalars.surplus(bal)
    source = scalars.source(bal)
    moved = scalars.length(source, scalars.surplus(source))
    lengths = [jnp.where(my_slot == slot, moved, scalars.length(bal, slot)) for slot in range(slots)]

    for step in range(groups):
        x_ref[group_here ^ step] = block_refs[step][...]
    x = jnp.concatenate([x_ref[group] for group in range(groups)], axis=1).astype(f32)
    normed_in, in_inverse = norm(x)
    nt_ref[...] = jnp.transpose(normed_in).astype(bf16)
    for copy in in_copies:
        copy.wait()
    projected = matmul(normed_in.astype(bf16), w_in[...])
    logistic = sigmoid(projected)
    active = projected * logistic
    dsilu_ref[...] = logistic + active * (1.0 - logistic)
    gate_ref[...] = active[:, :width]
    heads_ref[...] = active[:, width:].astype(bf16)

    pair_width = 2 * head_width
    low = lax.broadcasted_iota(jnp.int32, (slot_rows, pair_width), 1) < head_width
    row_at = lax.broadcasted_iota(jnp.int32, (slot_rows, slot_rows), 0)
    col_at = lax.broadcasted_iota(jnp.int32, (slot_rows, slot_rows), 1)

    def split(value):
        zero = jnp.zeros_like(value)
        return jnp.concatenate([jnp.where(low, value, zero), jnp.where(low, zero, value)], axis=0)

    def side_by_side(value):
        return jnp.concatenate([value[:slot_rows], value[slot_rows:]], axis=1)

    def part_of(slot, pair, which):
        first = which * width + pair * pair_width
        return heads_ref[slot * slot_rows : (slot + 1) * slot_rows, first : first + pair_width]

    pairs = HEADS // 2
    attended = []
    for slot in range(slots):
        live = (col_at <= row_at) & (row_at < lengths[slot])
        allowed = jnp.where(live, 1.0 / slot_rows, 0.0)
        allowed = jnp.concatenate([allowed, allowed], axis=0)
        across = []
        for pair in range(pairs):
            value, query, key = (part_of(slot, pair, which) for which in range(3))
            scores = matmul_nt(split(query), key) * score_scale
            q = sigmoid(scores)
            sq = scores * q
            weights = (sq * allowed).astype(bf16)
            weights_ref[slot * pairs + pair] = weights
            slope_ref[slot * pairs + pair] = allowed * (q + sq * (1.0 - q))
            across.append(matmul(side_by_side(weights), split(value)))
        attended.append(jnp.concatenate(across, axis=1))
    normed_out, out_inverse = norm(jnp.concatenate(attended, axis=0))
    gate = gate_ref[...]
    mixed = normed_out * gate
    mt_ref[...] = jnp.transpose(mixed).astype(bf16)
    for copy in out_copies:
        copy.wait()
    layer_ref[...] = (x + matmul(mixed.astype(bf16), w_out[...])).astype(bf16)

    wide_cot = cot_ref[...]
    cot = wide_cot.astype(bf16)
    grad_mixed = matmul_nt(cot, w_out[...])
    grad_attended = norm_back(grad_mixed * gate, normed_out, out_inverse).astype(bf16)
    grads_ref[:, :width] = (grad_mixed * normed_out * dsilu_ref[:, :width]).astype(bf16)

    def owner_order(ref, turn):
        start = (bal ^ turn) * part
        if part != groups * tables * unit:
            return ref[pl.ds(pl.multiple_of(start, part), part), :]
        found = []
        for group_step in range(groups):
            for table_step in range(tables):
                owner = (group_here ^ group_step) * tables + (table_here ^ table_step)
                at = pl.multiple_of(start + owner * unit, unit)
                found.append(ref[pl.ds(at, unit), :])
        return jnp.concatenate(found, axis=0)

    for turn in range(bals):
        term_refs[turn][:, features:] = matmul(owner_order(mt_ref, turn), cot).astype(bf16)

    for slot in range(slots):
        here = slice(slot * slot_rows, (slot + 1) * slot_rows)
        for pair in range(pairs):
            value, query, key = (part_of(slot, pair, which) for which in range(3))
            lanes = slice(pair * pair_width, (pair + 1) * pair_width)
            upper = split(grad_attended[here, lanes])
            grad_weights = matmul_nt(upper, value)
            grad_scores = (grad_weights * slope_ref[slot * pairs + pair]).astype(bf16)
            grad_value = matmul_tn(weights_ref[slot * pairs + pair], upper)
            grad_query = matmul(side_by_side(grad_scores), split(key)) * score_scale
            grad_key = matmul_tn(grad_scores, split(query)) * score_scale
            for which, found in enumerate((grad_value, grad_query, grad_key)):
                first = (1 + which) * width + pair * pair_width
                at = slice(first, first + pair_width)
                grads_ref[here, at] = (found * dsilu_ref[here, at]).astype(bf16)

    for turn in range(bals):
        term_refs[turn][:, :features] = matmul(owner_order(nt_ref, turn), grads_ref[...]).astype(bf16)

    grad_normed = matmul_nt(grads_ref[...], w_in[...])
    grad_rows = (wide_cot + norm_back(grad_normed, normed_in, in_inverse)).astype(bf16)
    for group in range(groups):
        x_ref[group] = grad_rows[:, group * piece : (group + 1) * piece]
    for step in range(groups):
        grad_refs[step][...] = x_ref[group_here ^ step]


def place_kernel(scale, groups, slots, tables, bals, unit, scalar_ref, *refs):
    pieces = refs[:groups]
    in_ref, out_ref, scaled_ref, sems = refs[groups:]
    _, group_here, table_here = Scalars(scalar_ref, bals, slots).place()
    features = in_ref.shape[1]
    copies = []
    for group_step, piece in enumerate(pieces):
        for table_step in range(tables):
            index = group_step * tables + table_step
            at = index * unit
            from_rows = slice(table_step * unit, (table_step + 1) * unit)
            scaled_ref[at : at + unit, :] = piece[from_rows, :].astype(f32) * scale
            owner = (group_here ^ group_step) * tables + (table_here ^ table_step)
            to = pl.ds(pl.multiple_of(owner * unit, unit), unit)
            rows = scaled_ref.at[pl.ds(at, unit), :]
            sem = sems.at[index]
            copies.append(
                pltpu.make_async_copy(rows.at[:, pl.ds(0, features)], in_ref.at[to, :], sem.at[0])
            )
            copies.append(
                pltpu.make_async_copy(
                    rows.at[:, pl.ds(features, out_ref.shape[1])], out_ref.at[to, :], sem.at[1]
                )
            )
            copies[-2].start()
            copies[-1].start()
    for copy in copies:
        copy.wait()


def sum_rounded(terms):
    total = terms[0].astype(f32)
    for term in terms[1:]:
        total = total + term.astype(f32)
    return total.astype(bf16)


def after(value, *others):
    return lax.optimization_barrier((value,) + others)[0]


def on_device(
    item_ids, seq_lengths, surplus_slot, helper_map, embed_tables, weight_in, weight_out, cotangent
):
    bal = lax.axis_index("bal")
    emb = lax.axis_index("emb")
    bals = lax.axis_size("bal")
    embs = lax.axis_size("emb")
    tables = item_ids.shape[2]
    groups = embs // tables
    _, rows, width = cotangent.shape
    slots = seq_lengths.shape[2]
    slot_rows = rows // slots
    distinct, columns = embed_tables.shape[1:]
    part = distinct // bals
    weight_part = weight_in.shape[0]
    table_here = emb // groups
    group_here = emb % groups
    width, features = weight_out.shape[1], weight_in.shape[1]
    unit = weight_part // embs
    owned = unit % 16 == 0
    unit = unit if owned else 0
    first = bals * (2 + slots)
    lane = lax.broadcasted_iota(jnp.int32, (1, LANES), 1)
    scalars = jnp.where(lane == first, bal, 0)
    scalars = jnp.where(lane == first + 1, group_here, scalars)
    scalars = jnp.where(lane == first + 2, table_here, scalars)
    fields = [surplus_slot.T, helper_map.T] + [seq_lengths[index] for index in range(bals)]
    at = 0
    for field in fields:
        width_here = field.shape[1]
        scalars = scalars + jnp.pad(field, ((0, 0), (at, LANES - at - width_here)))
        at += width_here

    share = lax.dynamic_slice_in_dim(embed_tables[0], bal * part, part, 0)
    fetched = [emb_swap(share, step * groups, embs) for step in range(1, tables)]

    ids = lax.dynamic_slice_in_dim(
        jnp.transpose(after(item_ids[0], share)), table_here * groups * rows, groups * rows, 1
    )
    plane_ids = with_swapped(ids.reshape(tables, groups * slots, 1, slot_rows), bals)
    wide_cot = cotangent[0].astype(f32)
    sent = after(scalars, share, wide_cot)
    plane_scalars = [scalars] + [emb_swap(sent, step, embs) for step in range(1, groups)]

    fetched[0] = after(fetched[0], *plane_scalars[1:])
    pieces = [piece for one in [share] + fetched for piece in with_swapped(one, bals)]

    weights = jnp.concatenate([weight_in, weight_out], axis=1)
    weights = with_swapped(weights, bals)

    found = pl.pallas_call(
        functools.partial(lookup_kernel, groups, slots, tables, bals),
        out_shape=[jax.ShapeDtypeStruct((rows, columns), bf16)] * groups,
        in_specs=[SMEM] * groups + [VMEM] * (bals + len(pieces)),
        out_specs=[VMEM] * groups,
        cost_estimate=estimate(3),
        compiler_params=room(16),
    )(*plane_scalars, *plane_ids, *pieces)
    block = [found[0]] + [emb_swap(found[step], step, embs) for step in range(1, groups)]

    pairs = slots * HEADS // 2
    terms = jax.ShapeDtypeStruct((weight_part, features + width), bf16)
    results = pl.pallas_call(
        functools.partial(layer_kernel, groups, slots, tables, bals, unit),
        out_shape=[jax.ShapeDtypeStruct((rows, width), bf16)]
        + [jax.ShapeDtypeStruct((rows, columns), bf16)] * groups
        + [terms] * bals,
        in_specs=[SMEM] + [VMEM] * groups + [HBM] * bals + [VMEM],
        out_specs=[VMEM] * (1 + groups + bals),
        scratch_shapes=[
            pltpu.VMEM((groups, rows, columns), bf16),
            pltpu.VMEM((width, features), bf16),
            pltpu.VMEM((width, width), bf16),
            pltpu.VMEM((width, rows), bf16),
            pltpu.VMEM((width, rows), bf16),
            pltpu.VMEM((pairs, 2 * slot_rows, slot_rows), bf16),
            pltpu.VMEM((pairs, 2 * slot_rows, slot_rows), f32),
            pltpu.VMEM((rows, width), f32),
            pltpu.VMEM((rows, features - width), bf16),
            pltpu.VMEM((rows, features), f32),
            pltpu.VMEM((rows, features), bf16),
            pltpu.SemaphoreType.DMA((2 * bals,)),
        ],
        cost_estimate=estimate(7),
        compiler_params=room(36),
    )(scalars, *block, *weights, wide_cot)
    layer_out, results = results[0], results[1:]
    grads, results = results[:groups], results[groups:]

    def over_cores(parts):
        return sum_rounded([parts[0]] + [bal_swap(parts[turn], turn, bals) for turn in range(1, bals)])

    def to_plane(value):
        return [value] + [emb_swap(value, step, embs) for step in range(1, groups)]

    plane_grads = [grads[0]] + [emb_swap(grads[step], step, embs) for step in range(1, groups)]
    total = over_cores(results)
    sums = pl.pallas_call(
        functools.partial(scatter_kernel, groups, slots, bals),
        out_shape=[jax.ShapeDtypeStruct((tables, part, columns), bf16)] * bals,
        in_specs=[SMEM] * groups + [VMEM] * (bals + groups),
        out_specs=[VMEM] * bals,
        cost_estimate=estimate(3),
        compiler_params=room(16),
    )(*plane_scalars, *plane_ids, *plane_grads)
    own_sums = over_cores(sums)

    grad_scale = (rows * embs * bals) ** -0.5
    if owned:
        pieces = total.reshape(groups, weight_part // groups, features + width)
        came = [emb_swap(pieces[step], step, embs) for step in range(1, groups)]
        came = [after(value, *plane_grads[1:]) for value in came]
        mine = sum_rounded([pieces[0]] + came)
        mine = mine.reshape(tables, unit, features + width)
        came = [emb_swap(mine[step], step * groups, embs) for step in range(1, tables)]
        final = sum_rounded([mine[0]] + [after(value, sums[0]) for value in came])
        gathered = [final] + [emb_swap(final, step * groups, embs) for step in range(1, tables)]
        own_sums = after(own_sums, *gathered[1:])
        back = to_plane(jnp.concatenate(gathered, axis=0))

    swapped = [emb_swap(own_sums[step], step * groups, embs) for step in range(1, tables)]
    if owned:
        swapped = [after(value, *back[1:]) for value in swapped]
    table_sum = own_sums[0].astype(f32)
    for value in swapped:
        table_sum = table_sum + value.astype(f32)
    table_scale = (distinct / (bals * item_ids.shape[1])) ** 0.5

    if owned:
        total_in, total_out = pl.pallas_call(
            functools.partial(place_kernel, grad_scale, groups, slots, tables, bals, unit),
            out_shape=[
                jax.ShapeDtypeStruct((weight_part, features), f32),
                jax.ShapeDtypeStruct((weight_part, width), f32),
            ],
            in_specs=[SMEM] + [VMEM] * groups,
            out_specs=[HBM] * 2,
            scratch_shapes=[
                pltpu.VMEM((weight_part, features + width), f32),
                pltpu.SemaphoreType.DMA((groups * tables, 2)),
            ],
            cost_estimate=estimate(2),
            compiler_params=room(12),
        )(scalars, *back)
    else:
        total = lax.psum(total.astype(f32), "emb") * grad_scale
        total_in, total_out = total[:, :features], total[:, features:]

    return layer_out[None], (table_sum * table_scale)[None], total_in, total_out


def solution(mesh):
    placed = (
        P("bal", None, None),
        P(None, "emb", None),
        P(None, "emb"),
        P(None, "emb"),
        P("emb", None, None),
        P("bal", None),
        P("bal", None),
        P("bal", "emb", None),
    )
    return jax.shard_map(
        on_device,
        mesh=mesh,
        in_specs=placed,
        out_specs=(P("bal", "emb", None), P("emb", "bal", None), P("bal", None), P("bal", None)),
        check_vma=False,
    )
```

```python
import functools

import jax
import jax.numpy as jnp
from jax import lax
from jax.experimental import pallas as pl
from jax.experimental.pallas import tpu as pltpu
from jax.sharding import PartitionSpec as P

HEADS = 8
EPS = 1e-05
LANES = 128

VMEM = pl.BlockSpec(memory_space=pltpu.VMEM)
SMEM = pl.BlockSpec(memory_space=pltpu.SMEM)
HBM = pl.BlockSpec(memory_space=pltpu.HBM)
f32 = jnp.float32
bf16 = jnp.bfloat16


def room(mib):
    return pltpu.CompilerParams(vmem_limit_bytes=mib * 1024 * 1024)


def estimate(microseconds):
    return pl.CostEstimate(flops=0, bytes_accessed=microseconds * 3_500_000, transcendentals=0)


def matmul(left, right):
    return lax.dot_general(left, right, (((1,), (0,)), ((), ())), preferred_element_type=f32)


def matmul_nt(left, right):
    return lax.dot_general(left, right, (((1,), (1,)), ((), ())), preferred_element_type=f32)


def matmul_tn(left, right):
    return lax.dot_general(left, right, (((0,), (0,)), ((), ())), preferred_element_type=f32)


def sigmoid(value):
    return 0.5 * jnp.tanh(0.5 * value) + 0.5


def bal_swap(value, step, count):
    return lax.ppermute(value, "bal", [(i, i ^ step) for i in range(count)])


def with_swapped(value, count):
    return [value] + [bal_swap(value, turn, count) for turn in range(1, count)]


def emb_swap(value, step, count):
    return lax.ppermute(value, "emb", [(i, i ^ step) for i in range(count)])


class Scalars:
    def __init__(self, ref, step, bals, slots):
        self.ref, self.step, self.bals, self.slots = ref, step, bals, slots

    def surplus(self, bal):
        return self.ref[self.step, bal]

    def source(self, bal):
        found = jnp.int32(0)
        for index in range(self.bals):
            found = found + jnp.where(self.ref[self.step, self.bals + index] == bal, index, 0)
        return found

    def length(self, bal, slot):
        return self.ref[self.step, 2 * self.bals + bal * self.slots + slot]

    def place(self):
        first = self.bals * (2 + self.slots)
        return self.ref[self.step, first], self.ref[self.step, first + 1], self.ref[self.step, first + 2]


def pick_ids(scalars, ids_refs, slots, tables):
    bal, group_here, _ = scalars[0].place()
    found = []
    for step, there in enumerate(scalars):
        group = group_here ^ step
        my_slot = there.surplus(bal)
        source = there.source(bal)
        from_slot = there.surplus(source)
        by_slot = [[] for _ in range(slots)]
        for table in tables:
            arrived = ids_refs[0][table, group * slots + from_slot]
            for turn in range(1, len(ids_refs)):
                other = ids_refs[turn][table, group * slots + from_slot]
                arrived = jnp.where(source ^ bal == turn, other, arrived)
            for slot in range(slots):
                own = ids_refs[0][table, group * slots + slot]
                by_slot[slot].append(jnp.where(my_slot == slot, arrived, own))
        found.append(by_slot)
    return found


def table_order(table_here, tables):
    return [table_here ^ step for step in range(tables)]


def lookup_kernel(groups, slots, tables, bals, *refs):
    refs = list(refs)
    take = lambda count: [refs.pop(0) for _ in range(count)]
    (scalar_ref,) = take(1)
    scalars = [Scalars(scalar_ref, step, bals, slots) for step in range(groups)]
    ids_refs = take(bals)
    pieces = [take(bals) for _ in range(tables)]
    out_refs = refs
    bal, _, table_here = scalars[0].place()
    part, columns = pieces[0][0].shape
    slot_rows = ids_refs[0].shape[3]
    lane = lax.broadcasted_iota(jnp.int32, (LANES, LANES), 1)
    ids = pick_ids(scalars, ids_refs, slots, table_order(table_here, tables))
    for group in range(groups):
        for slot in range(slots):
            for first in range(0, slot_rows, LANES):
                total = jnp.zeros((LANES, columns), f32)
                for table in range(tables):
                    row = ids[group][slot][table][:, first : first + LANES]
                    column = jnp.transpose(jnp.broadcast_to(row, (LANES, LANES)))
                    for turn, ref in enumerate(pieces[table]):
                        shifted = column - (bal ^ turn) * part
                        hot = jnp.concatenate(
                            [
                                jnp.where(shifted == lane + at, 1.0, 0.0).astype(bf16)
                                for at in range(0, part, LANES)
                            ],
                            axis=1,
                        )
                        total = total + matmul(hot, ref[...])
                at = slot * slot_rows + first
                out_refs[group][at : at + LANES, :] = total.astype(bf16)


def scatter_kernel(groups, slots, bals, *refs):
    refs = list(refs)
    take = lambda count: [refs.pop(0) for _ in range(count)]
    (scalar_ref,) = take(1)
    scalars = [Scalars(scalar_ref, step, bals, slots) for step in range(groups)]
    ids_refs, grad_refs, out_refs = take(bals), take(groups), refs
    bal, _, table_here = scalars[0].place()
    tables, part, _ = out_refs[0].shape
    slot_rows = ids_refs[0].shape[3]
    height = min(part, 256)
    iota = lax.broadcasted_iota(jnp.int32, (height, slot_rows), 0)
    ids = pick_ids(scalars, ids_refs, slots, table_order(table_here, tables))
    columns = out_refs[0].shape[2]

    def rows_of(ref):
        height = ref.shape[0]
        first = ref.shape[1] - slots * slot_rows // height * columns
        return [ref[:, at : at + columns] for at in range(first, ref.shape[1], columns)]

    grads = jnp.concatenate([piece for ref in grad_refs for piece in rows_of(ref)], axis=0)
    for table in range(tables):
        for turn in range(bals):
            for at in range(0, part, height):
                start = (bal ^ turn) * part + at
                hot = jnp.concatenate(
                    [
                        jnp.where(iota == ids[group][slot][table] - start, 1.0, 0.0).astype(bf16)
                        for group in range(groups)
                        for slot in range(slots)
                    ],
                    axis=1,
                )
                out_refs[turn][table, at : at + height, :] = matmul(hot, grads).astype(bf16)


def norm(values):
    average = jnp.mean(values, axis=1, keepdims=True)
    centred = values - average
    inverse = lax.rsqrt(jnp.mean(centred * centred, axis=1, keepdims=True) + EPS)
    return centred * inverse, inverse


def norm_back(incoming, normed, inverse):
    first = jnp.mean(incoming, axis=1, keepdims=True)
    second = jnp.mean(incoming * normed, axis=1, keepdims=True)
    return inverse * (incoming - first - normed * second)


def layer_kernel(groups, slots, tables, bals, unit, scalar_ref, *refs):
    refs = list(refs)
    take = lambda count: [refs.pop(0) for _ in range(count)]
    block_refs = take(groups)
    weight_refs = take(bals)
    (cot_ref,) = take(1)
    (layer_ref,) = take(1)
    grad_refs = take(groups)
    term_refs = take(bals)
    (x_ref, w_in, w_out, nt_ref, mt_ref, weights_ref, slope_ref, gate_ref, heads_ref, dsilu_ref, grads_ref, sems) = refs

    scalars = Scalars(scalar_ref, 0, bals, slots)
    bal, group_here, table_here = scalars.place()
    rows, width = cot_ref.shape
    slot_rows = rows // slots
    head_width = width // HEADS
    score_scale = head_width**-0.5
    piece = block_refs[0].shape[1]
    part, features = weight_refs[0].shape[0], w_in.shape[1]

    in_copies, out_copies = [], []
    for turn in range(bals):
        at = pl.ds(pl.multiple_of((bal ^ turn) * part, part), part)
        here = weight_refs[turn]
        in_copies.append(
            pltpu.make_async_copy(here.at[:, pl.ds(0, features)], w_in.at[at, :], sems.at[2 * turn])
        )
        out_copies.append(
            pltpu.make_async_copy(
                here.at[:, pl.ds(features, width)], w_out.at[at, :], sems.at[2 * turn + 1]
            )
        )
    for copy in in_copies + out_copies:
        copy.start()

    my_slot = scalars.surplus(bal)
    source = scalars.source(bal)
    moved = scalars.length(source, scalars.surplus(source))
    lengths = [jnp.where(my_slot == slot, moved, scalars.length(bal, slot)) for slot in range(slots)]

    for step in range(groups):
        x_ref[group_here ^ step] = block_refs[step][...]
    x = jnp.concatenate([x_ref[group] for group in range(groups)], axis=1).astype(f32)
    normed_in, in_inverse = norm(x)
    nt_ref[...] = jnp.transpose(normed_in).astype(bf16)
    for copy in in_copies:
        copy.wait()
    projected = matmul(normed_in.astype(bf16), w_in[...])
    logistic = sigmoid(projected)
    active = projected * logistic
    dsilu_ref[...] = logistic + active * (1.0 - logistic)
    gate_ref[...] = active[:, :width]
    heads_ref[...] = active[:, width:].astype(bf16)

    pair_width = 2 * head_width
    low = lax.broadcasted_iota(jnp.int32, (slot_rows, pair_width), 1) < head_width
    row_at = lax.broadcasted_iota(jnp.int32, (slot_rows, slot_rows), 0)
    col_at = lax.broadcasted_iota(jnp.int32, (slot_rows, slot_rows), 1)

    def split(value):
        zero = jnp.zeros_like(value)
        return jnp.concatenate([jnp.where(low, value, zero), jnp.where(low, zero, value)], axis=0)

    def side_by_side(value):
        return jnp.concatenate([value[:slot_rows], value[slot_rows:]], axis=1)

    def part_of(slot, pair, which):
        first = which * width + pair * pair_width
        return heads_ref[slot * slot_rows : (slot + 1) * slot_rows, first : first + pair_width]

    pairs = HEADS // 2
    attended = []
    for slot in range(slots):
        live = (col_at <= row_at) & (row_at < lengths[slot])
        allowed = jnp.where(live, 1.0 / slot_rows, 0.0)
        allowed = jnp.concatenate([allowed, allowed], axis=0)
        across = []
        for pair in range(pairs):
            value, query, key = (part_of(slot, pair, which) for which in range(3))
            scores = matmul_nt(split(query), key) * score_scale
            q = sigmoid(scores)
            sq = scores * q
            weights = (sq * allowed).astype(bf16)
            weights_ref[slot * pairs + pair] = weights
            slope_ref[slot * pairs + pair] = allowed * (q + sq * (1.0 - q))
            across.append(matmul(side_by_side(weights), split(value)))
        attended.append(jnp.concatenate(across, axis=1))
    normed_out, out_inverse = norm(jnp.concatenate(attended, axis=0))
    gate = gate_ref[...]
    mixed = normed_out * gate
    mt_ref[...] = jnp.transpose(mixed).astype(bf16)
    for copy in out_copies:
        copy.wait()
    layer_ref[...] = (x + matmul(mixed.astype(bf16), w_out[...])).astype(bf16)

    wide_cot = cot_ref[...]
    cot = wide_cot.astype(bf16)
    grad_mixed = matmul_nt(cot, w_out[...])
    grad_attended = norm_back(grad_mixed * gate, normed_out, out_inverse).astype(bf16)
    grads_ref[:, :width] = (grad_mixed * normed_out * dsilu_ref[:, :width]).astype(bf16)

    def owner_order(ref, turn):
        start = (bal ^ turn) * part
        if part != groups * tables * unit:
            return ref[pl.ds(pl.multiple_of(start, part), part), :]
        found = []
        for group_step in range(groups):
            for table_step in range(tables):
                owner = (group_here ^ group_step) * tables + (table_here ^ table_step)
                at = pl.multiple_of(start + owner * unit, unit)
                found.append(ref[pl.ds(at, unit), :])
        return jnp.concatenate(found, axis=0)

    for turn in range(bals):
        term_refs[turn][:, features:] = matmul(owner_order(mt_ref, turn), cot).astype(bf16)

    for slot in range(slots):
        here = slice(slot * slot_rows, (slot + 1) * slot_rows)
        for pair in range(pairs):
            value, query, key = (part_of(slot, pair, which) for which in range(3))
            lanes = slice(pair * pair_width, (pair + 1) * pair_width)
            upper = split(grad_attended[here, lanes])
            grad_weights = matmul_nt(upper, value)
            grad_scores = (grad_weights * slope_ref[slot * pairs + pair]).astype(bf16)
            grad_value = matmul_tn(weights_ref[slot * pairs + pair], upper)
            grad_query = matmul(side_by_side(grad_scores), split(key)) * score_scale
            grad_key = matmul_tn(grad_scores, split(query)) * score_scale
            for which, found in enumerate((grad_value, grad_query, grad_key)):
                first = (1 + which) * width + pair * pair_width
                at = slice(first, first + pair_width)
                grads_ref[here, at] = (found * dsilu_ref[here, at]).astype(bf16)

    for turn in range(bals):
        term_refs[turn][:, :features] = matmul(owner_order(nt_ref, turn), grads_ref[...]).astype(bf16)

    grad_normed = matmul_nt(grads_ref[...], w_in[...])
    grad_rows = (wide_cot + norm_back(grad_normed, normed_in, in_inverse)).astype(bf16)
    for group in range(groups):
        x_ref[group] = grad_rows[:, group * piece : (group + 1) * piece]
    for step in range(groups):
        grad_refs[step][...] = x_ref[group_here ^ step]


def pieces_kernel(bals, *refs):
    count = len(refs) - bals
    groups = (count + 1) // 2
    term_refs, grad_refs = refs[:bals], refs[bals : bals + groups - 1]
    out_refs = refs[bals + groups - 1 :]
    height, width = out_refs[0].shape
    for step, out in enumerate(out_refs):
        rows = slice(step * height, (step + 1) * height)
        total = term_refs[0][rows, :].astype(f32)
        for ref in term_refs[1:]:
            total = total + ref[rows, :].astype(f32)
        out[:, :width] = total.astype(bf16)
        if step:
            grad = grad_refs[step - 1]
            columns = grad.shape[1]
            for index in range(grad.shape[0] // height):
                at = width + index * columns
                out[:, at : at + columns] = grad[index * height : (index + 1) * height, :]


def place_kernel(scale, groups, slots, tables, bals, unit, scalar_ref, *refs):
    pieces = refs[:groups]
    in_ref, out_ref, scaled_ref, sems = refs[groups:]
    _, group_here, table_here = Scalars(scalar_ref, 0, bals, slots).place()
    features = in_ref.shape[1]
    copies = []
    for group_step, piece in enumerate(pieces):
        for table_step in range(tables):
            index = group_step * tables + table_step
            at = index * unit
            from_rows = slice(table_step * unit, (table_step + 1) * unit)
            scaled_ref[at : at + unit, :] = piece[from_rows, :].astype(f32) * scale
            owner = (group_here ^ group_step) * tables + (table_here ^ table_step)
            to = pl.ds(pl.multiple_of(owner * unit, unit), unit)
            rows = scaled_ref.at[pl.ds(at, unit), :]
            sem = sems.at[index]
            copies.append(
                pltpu.make_async_copy(rows.at[:, pl.ds(0, features)], in_ref.at[to, :], sem.at[0])
            )
            copies.append(
                pltpu.make_async_copy(
                    rows.at[:, pl.ds(features, out_ref.shape[1])], out_ref.at[to, :], sem.at[1]
                )
            )
            copies[-2].start()
            copies[-1].start()
    for copy in copies:
        copy.wait()


def sum_rounded(terms):
    total = terms[0].astype(f32)
    for term in terms[1:]:
        total = total + term.astype(f32)
    return total.astype(bf16)


def after(value, *others):
    return lax.optimization_barrier((value,) + others)[0]


def on_device(
    item_ids, seq_lengths, surplus_slot, helper_map, embed_tables, weight_in, weight_out, cotangent
):
    bal = lax.axis_index("bal")
    emb = lax.axis_index("emb")
    bals = lax.axis_size("bal")
    embs = lax.axis_size("emb")
    tables = item_ids.shape[2]
    groups = embs // tables
    _, rows, width = cotangent.shape
    slots = seq_lengths.shape[2]
    slot_rows = rows // slots
    distinct, columns = embed_tables.shape[1:]
    part = distinct // bals
    weight_part = weight_in.shape[0]
    table_here = emb // groups
    group_here = emb % groups
    width, features = weight_out.shape[1], weight_in.shape[1]
    unit = weight_part // embs
    owned = unit % 16 == 0
    unit = unit if owned else 0
    first = bals * (2 + slots)
    lane = lax.broadcasted_iota(jnp.int32, (1, LANES), 1)
    scalars = jnp.where(lane == first, bal, 0)
    scalars = jnp.where(lane == first + 1, group_here, scalars)
    scalars = jnp.where(lane == first + 2, table_here, scalars)
    fields = [surplus_slot.T, helper_map.T] + [seq_lengths[index] for index in range(bals)]
    at = 0
    for field in fields:
        width_here = field.shape[1]
        scalars = scalars + jnp.pad(field, ((0, 0), (at, LANES - at - width_here)))
        at += width_here

    share = lax.dynamic_slice_in_dim(embed_tables[0], bal * part, part, 0)
    fetched = [emb_swap(share, step * groups, embs) for step in range(1, tables)]

    ids = lax.dynamic_slice_in_dim(
        jnp.transpose(after(item_ids[0], share)), table_here * groups * rows, groups * rows, 1
    )
    plane_ids = with_swapped(ids.reshape(tables, groups * slots, 1, slot_rows), bals)
    wide_cot = cotangent[0].astype(f32)
    scalars = after(scalars, share, wide_cot)
    for bit in range((groups - 1).bit_length()):
        scalars = jnp.concatenate([scalars, emb_swap(scalars, 1 << bit, embs)], axis=0)

    fetched[0] = after(fetched[0], scalars)
    pieces = [piece for one in [share] + fetched for piece in with_swapped(one, bals)]

    found = pl.pallas_call(
        functools.partial(lookup_kernel, groups, slots, tables, bals),
        out_shape=[jax.ShapeDtypeStruct((rows, columns), bf16)] * groups,
        in_specs=[SMEM] + [VMEM] * (bals + len(pieces)),
        out_specs=[VMEM] * groups,
        cost_estimate=estimate(3),
        compiler_params=room(16),
    )(scalars, *plane_ids, *pieces)
    weights = jnp.concatenate([weight_in, weight_out], axis=1)
    weights = with_swapped(after(weights, found[0]), bals)
    block = [found[0]] + [emb_swap(found[step], step, embs) for step in range(1, groups)]

    pairs = slots * HEADS // 2
    terms = jax.ShapeDtypeStruct((weight_part, features + width), bf16)
    results = pl.pallas_call(
        functools.partial(layer_kernel, groups, slots, tables, bals, unit),
        out_shape=[jax.ShapeDtypeStruct((rows, width), bf16)]
        + [jax.ShapeDtypeStruct((rows, columns), bf16)] * groups
        + [terms] * bals,
        in_specs=[SMEM] + [VMEM] * groups + [HBM] * bals + [VMEM],
        out_specs=[VMEM] * (1 + groups + bals),
        scratch_shapes=[
            pltpu.VMEM((groups, rows, columns), bf16),
            pltpu.VMEM((width, features), bf16),
            pltpu.VMEM((width, width), bf16),
            pltpu.VMEM((width, rows), bf16),
            pltpu.VMEM((width, rows), bf16),
            pltpu.VMEM((pairs, 2 * slot_rows, slot_rows), bf16),
            pltpu.VMEM((pairs, 2 * slot_rows, slot_rows), f32),
            pltpu.VMEM((rows, width), f32),
            pltpu.VMEM((rows, features - width), bf16),
            pltpu.VMEM((rows, features), f32),
            pltpu.VMEM((rows, features), bf16),
            pltpu.SemaphoreType.DMA((2 * bals,)),
        ],
        cost_estimate=estimate(7),
        compiler_params=room(36),
    )(scalars, *block, *weights, wide_cot)
    layer_out, results = results[0], results[1:]
    grads, results = results[:groups], results[groups:]

    def over_cores(parts):
        return sum_rounded([parts[0]] + [bal_swap(parts[turn], turn, bals) for turn in range(1, bals)])

    def to_plane(value):
        return [value] + [emb_swap(value, step, embs) for step in range(1, groups)]

    def table_sums(plane_grads):
        return pl.pallas_call(
            functools.partial(scatter_kernel, groups, slots, bals),
            out_shape=[jax.ShapeDtypeStruct((tables, part, columns), bf16)] * bals,
            in_specs=[SMEM] + [VMEM] * (bals + groups),
            out_specs=[VMEM] * bals,
            cost_estimate=estimate(3),
            compiler_params=room(16),
        )(scalars, *plane_ids, *plane_grads)

    grad_scale = (rows * embs * bals) ** -0.5
    if owned:
        height, wide = weight_part // groups, features + width
        terms = [results[0]] + [bal_swap(results[turn], turn, bals) for turn in range(1, bals)]
        pieces = pl.pallas_call(
            functools.partial(pieces_kernel, bals),
            out_shape=[jax.ShapeDtypeStruct((height, wide), bf16)]
            + [jax.ShapeDtypeStruct((height, wide + rows // height * columns), bf16)] * (groups - 1),
            in_specs=[VMEM] * (bals + groups - 1),
            out_specs=[VMEM] * groups,
            compiler_params=room(12),
        )(*terms, *grads[1:])
        came = [emb_swap(pieces[step], step, embs) for step in range(1, groups)]
        mine = sum_rounded([pieces[0]] + [value[:, :wide] for value in came])
        mine = mine.reshape(tables, unit, wide)
        sums = table_sums([grads[0]] + came)
        own_sums = over_cores(sums)
        came = [emb_swap(mine[step], step * groups, embs) for step in range(1, tables)]
        final = sum_rounded([mine[0]] + came)
        gathered = [final] + [emb_swap(final, step * groups, embs) for step in range(1, tables)]
        back = to_plane(jnp.concatenate(gathered, axis=0))
        later = after(own_sums, *gathered[1:])
        swapped = [emb_swap(later[step], step * groups, embs) for step in range(1, tables)]
        swapped = [after(value, *back[1:]) for value in swapped]
    else:
        sums = table_sums([grads[0]] + [emb_swap(grads[step], step, embs) for step in range(1, groups)])
        own_sums = over_cores(sums)
        swapped = [emb_swap(own_sums[step], step * groups, embs) for step in range(1, tables)]
    table_sum = own_sums[0].astype(f32)
    for value in swapped:
        table_sum = table_sum + value.astype(f32)
    table_scale = (distinct / (bals * item_ids.shape[1])) ** 0.5

    if owned:
        total_in, total_out = pl.pallas_call(
            functools.partial(place_kernel, grad_scale, groups, slots, tables, bals, unit),
            out_shape=[
                jax.ShapeDtypeStruct((weight_part, features), f32),
                jax.ShapeDtypeStruct((weight_part, width), f32),
            ],
            in_specs=[SMEM] + [VMEM] * groups,
            out_specs=[HBM] * 2,
            scratch_shapes=[
                pltpu.VMEM((weight_part, features + width), f32),
                pltpu.SemaphoreType.DMA((groups * tables, 2)),
            ],
            cost_estimate=estimate(2),
            compiler_params=room(12),
        )(scalars, *back)
    else:
        total = lax.psum(over_cores(results).astype(f32), "emb") * grad_scale
        total_in, total_out = total[:, :features], total[:, features:]

    return layer_out[None], (table_sum * table_scale)[None], total_in, total_out


def solution(mesh):
    placed = (
        P("bal", None, None),
        P(None, "emb", None),
        P(None, "emb"),
        P(None, "emb"),
        P("emb", None, None),
        P("bal", None),
        P("bal", None),
        P("bal", "emb", None),
    )
    return jax.shard_map(
        on_device,
        mesh=mesh,
        in_specs=placed,
        out_specs=(P("bal", "emb", None), P("emb", "bal", None), P("bal", None), P("bal", None)),
        check_vma=False,
    )
```

```python
import functools

import jax
import jax.numpy as jnp
from jax import lax
from jax.experimental import pallas as pl
from jax.experimental.pallas import tpu as pltpu
from jax.sharding import PartitionSpec as P

HEADS = 8
EPS = 1e-05
LANES = 128

VMEM = pl.BlockSpec(memory_space=pltpu.VMEM)
SMEM = pl.BlockSpec(memory_space=pltpu.SMEM)
HBM = pl.BlockSpec(memory_space=pltpu.HBM)
f32 = jnp.float32
bf16 = jnp.bfloat16


def room(mib):
    return pltpu.CompilerParams(vmem_limit_bytes=mib * 1024 * 1024)


def estimate(microseconds):
    return pl.CostEstimate(flops=0, bytes_accessed=microseconds * 3_500_000, transcendentals=0)


def matmul(left, right):
    return lax.dot_general(left, right, (((1,), (0,)), ((), ())), preferred_element_type=f32)


def matmul_nt(left, right):
    return lax.dot_general(left, right, (((1,), (1,)), ((), ())), preferred_element_type=f32)


def matmul_tn(left, right):
    return lax.dot_general(left, right, (((0,), (0,)), ((), ())), preferred_element_type=f32)


def sigmoid(value):
    return 0.5 * jnp.tanh(0.5 * value) + 0.5


def bal_swap(value, step, count):
    return lax.ppermute(value, "bal", [(i, i ^ step) for i in range(count)])


def with_swapped(value, count):
    return [value] + [bal_swap(value, turn, count) for turn in range(1, count)]


def emb_swap(value, step, count):
    return lax.ppermute(value, "emb", [(i, i ^ step) for i in range(count)])


class Scalars:
    def __init__(self, ref, step, bals, slots):
        self.ref, self.step, self.bals, self.slots = ref, step, bals, slots

    def surplus(self, bal):
        return self.ref[self.step, bal]

    def source(self, bal):
        found = jnp.int32(0)
        for index in range(self.bals):
            found = found + jnp.where(self.ref[self.step, self.bals + index] == bal, index, 0)
        return found

    def length(self, bal, slot):
        return self.ref[self.step, 2 * self.bals + bal * self.slots + slot]

    def place(self):
        first = self.bals * (2 + self.slots)
        return self.ref[self.step, first], self.ref[self.step, first + 1], self.ref[self.step, first + 2]


def pick_ids(scalars, ids_refs, slots, tables):
    bal, group_here, _ = scalars[0].place()
    found = []
    for step, there in enumerate(scalars):
        group = group_here ^ step
        my_slot = there.surplus(bal)
        source = there.source(bal)
        from_slot = there.surplus(source)
        by_slot = [[] for _ in range(slots)]
        for table in tables:
            arrived = ids_refs[0][table, group * slots + from_slot]
            for turn in range(1, len(ids_refs)):
                other = ids_refs[turn][table, group * slots + from_slot]
                arrived = jnp.where(source ^ bal == turn, other, arrived)
            for slot in range(slots):
                own = ids_refs[0][table, group * slots + slot]
                by_slot[slot].append(jnp.where(my_slot == slot, arrived, own))
        found.append(by_slot)
    return found


def table_order(table_here, tables):
    return [table_here ^ step for step in range(tables)]


def lookup_kernel(groups, slots, tables, bals, *refs):
    refs = list(refs)
    take = lambda count: [refs.pop(0) for _ in range(count)]
    (scalar_ref,) = take(1)
    scalars = [Scalars(scalar_ref, step, bals, slots) for step in range(groups)]
    ids_refs = take(bals)
    pieces = [take(bals) for _ in range(tables)]
    out_refs = refs
    bal, _, table_here = scalars[0].place()
    part, columns = pieces[0][0].shape
    slot_rows = ids_refs[0].shape[3]
    lane = lax.broadcasted_iota(jnp.int32, (LANES, LANES), 1)
    ids = pick_ids(scalars, ids_refs, slots, table_order(table_here, tables))
    for group in range(groups):
        for slot in range(slots):
            for first in range(0, slot_rows, LANES):
                total = jnp.zeros((LANES, columns), f32)
                for table in range(tables):
                    row = ids[group][slot][table][:, first : first + LANES]
                    column = jnp.transpose(jnp.broadcast_to(row, (LANES, LANES)))
                    for turn, ref in enumerate(pieces[table]):
                        shifted = column - (bal ^ turn) * part
                        hot = jnp.concatenate(
                            [
                                jnp.where(shifted == lane + at, 1.0, 0.0).astype(bf16)
                                for at in range(0, part, LANES)
                            ],
                            axis=1,
                        )
                        total = total + matmul(hot, ref[...])
                at = slot * slot_rows + first
                out_refs[group][at : at + LANES, :] = total.astype(bf16)


def scatter_kernel(groups, slots, bals, *refs):
    refs = list(refs)
    take = lambda count: [refs.pop(0) for _ in range(count)]
    (scalar_ref,) = take(1)
    scalars = [Scalars(scalar_ref, step, bals, slots) for step in range(groups)]
    ids_refs, grad_refs, out_refs = take(bals), take(groups), refs
    bal, _, table_here = scalars[0].place()
    tables, part, _ = out_refs[0].shape
    slot_rows = ids_refs[0].shape[3]
    height = min(part, 256)
    iota = lax.broadcasted_iota(jnp.int32, (height, slot_rows), 0)
    ids = pick_ids(scalars, ids_refs, slots, table_order(table_here, tables))
    columns = out_refs[0].shape[2]

    def rows_of(ref):
        height = ref.shape[0]
        first = ref.shape[1] - slots * slot_rows // height * columns
        return [ref[:, at : at + columns] for at in range(first, ref.shape[1], columns)]

    grads = jnp.concatenate([piece for ref in grad_refs for piece in rows_of(ref)], axis=0)
    for table in range(tables):
        for turn in range(bals):
            for at in range(0, part, height):
                start = (bal ^ turn) * part + at
                hot = jnp.concatenate(
                    [
                        jnp.where(iota == ids[group][slot][table] - start, 1.0, 0.0).astype(bf16)
                        for group in range(groups)
                        for slot in range(slots)
                    ],
                    axis=1,
                )
                out_refs[turn][table, at : at + height, :] = matmul(hot, grads).astype(bf16)


def norm(values):
    average = jnp.mean(values, axis=1, keepdims=True)
    centred = values - average
    inverse = lax.rsqrt(jnp.mean(centred * centred, axis=1, keepdims=True) + EPS)
    return centred * inverse, inverse


def norm_back(incoming, normed, inverse):
    first = jnp.mean(incoming, axis=1, keepdims=True)
    second = jnp.mean(incoming * normed, axis=1, keepdims=True)
    return inverse * (incoming - first - normed * second)


def layer_kernel(groups, slots, tables, bals, unit, scalar_ref, *refs):
    refs = list(refs)
    take = lambda count: [refs.pop(0) for _ in range(count)]
    block_refs = take(groups)
    weight_refs = take(bals)
    (cot_ref,) = take(1)
    (layer_ref,) = take(1)
    grad_refs = take(groups)
    term_refs = take(bals)
    (x_ref, w_in, w_out, nt_ref, mt_ref, weights_ref, slope_ref, gate_ref, heads_ref, dsilu_ref, grads_ref, sems) = refs

    scalars = Scalars(scalar_ref, 0, bals, slots)
    bal, group_here, table_here = scalars.place()
    rows, width = cot_ref.shape
    slot_rows = rows // slots
    head_width = width // HEADS
    score_scale = head_width**-0.5
    piece = block_refs[0].shape[1]
    part, features = weight_refs[0].shape[0], w_in.shape[1]

    in_copies, out_copies = [], []
    for turn in range(bals):
        at = pl.ds(pl.multiple_of((bal ^ turn) * part, part), part)
        here = weight_refs[turn]
        in_copies.append(
            pltpu.make_async_copy(here.at[:, pl.ds(0, features)], w_in.at[at, :], sems.at[2 * turn])
        )
        out_copies.append(
            pltpu.make_async_copy(
                here.at[:, pl.ds(features, width)], w_out.at[at, :], sems.at[2 * turn + 1]
            )
        )
    for copy in in_copies + out_copies:
        copy.start()

    my_slot = scalars.surplus(bal)
    source = scalars.source(bal)
    moved = scalars.length(source, scalars.surplus(source))
    lengths = [jnp.where(my_slot == slot, moved, scalars.length(bal, slot)) for slot in range(slots)]

    for step in range(groups):
        x_ref[group_here ^ step] = block_refs[step][...]
    x = jnp.concatenate([x_ref[group] for group in range(groups)], axis=1).astype(f32)
    normed_in, in_inverse = norm(x)
    nt_ref[...] = jnp.transpose(normed_in).astype(bf16)
    for copy in in_copies:
        copy.wait()
    projected = matmul(normed_in.astype(bf16), w_in[...])
    logistic = sigmoid(projected)
    active = projected * logistic
    dsilu_ref[...] = logistic + active * (1.0 - logistic)
    gate_ref[...] = active[:, :width]
    heads_ref[...] = active[:, width:].astype(bf16)

    pair_width = 2 * head_width
    low = lax.broadcasted_iota(jnp.int32, (slot_rows, pair_width), 1) < head_width
    row_at = lax.broadcasted_iota(jnp.int32, (slot_rows, slot_rows), 0)
    col_at = lax.broadcasted_iota(jnp.int32, (slot_rows, slot_rows), 1)

    def split(value):
        zero = jnp.zeros_like(value)
        return jnp.concatenate([jnp.where(low, value, zero), jnp.where(low, zero, value)], axis=0)

    def side_by_side(value):
        return jnp.concatenate([value[:slot_rows], value[slot_rows:]], axis=1)

    def part_of(slot, pair, which):
        first = which * width + pair * pair_width
        return heads_ref[slot * slot_rows : (slot + 1) * slot_rows, first : first + pair_width]

    pairs = HEADS // 2
    attended = []
    for slot in range(slots):
        live = (col_at <= row_at) & (row_at < lengths[slot])
        allowed = jnp.where(live, 1.0 / slot_rows, 0.0)
        allowed = jnp.concatenate([allowed, allowed], axis=0)
        across = []
        for pair in range(pairs):
            value, query, key = (part_of(slot, pair, which) for which in range(3))
            scores = matmul_nt(split(query), key) * score_scale
            q = sigmoid(scores)
            sq = scores * q
            weights = (sq * allowed).astype(bf16)
            weights_ref[slot * pairs + pair] = weights
            slope_ref[slot * pairs + pair] = allowed * (q + sq * (1.0 - q))
            across.append(matmul(side_by_side(weights), split(value)))
        attended.append(jnp.concatenate(across, axis=1))
    normed_out, out_inverse = norm(jnp.concatenate(attended, axis=0))
    gate = gate_ref[...]
    mixed = normed_out * gate
    mt_ref[...] = jnp.transpose(mixed).astype(bf16)
    for copy in out_copies:
        copy.wait()
    layer_ref[...] = (x + matmul(mixed.astype(bf16), w_out[...])).astype(bf16)

    wide_cot = cot_ref[...]
    cot = wide_cot.astype(bf16)
    grad_mixed = matmul_nt(cot, w_out[...])
    grad_attended = norm_back(grad_mixed * gate, normed_out, out_inverse).astype(bf16)
    grads_ref[:, :width] = (grad_mixed * normed_out * dsilu_ref[:, :width]).astype(bf16)

    def owner_order(ref, turn):
        start = (bal ^ turn) * part
        if part != groups * tables * unit:
            return ref[pl.ds(pl.multiple_of(start, part), part), :]
        found = []
        for group_step in range(groups):
            for table_step in range(tables):
                owner = (group_here ^ group_step) * tables + (table_here ^ table_step)
                at = pl.multiple_of(start + owner * unit, unit)
                found.append(ref[pl.ds(at, unit), :])
        return jnp.concatenate(found, axis=0)

    for turn in range(bals):
        term_refs[turn][:, features:] = matmul(owner_order(mt_ref, turn), cot).astype(bf16)

    for slot in range(slots):
        here = slice(slot * slot_rows, (slot + 1) * slot_rows)
        for pair in range(pairs):
            value, query, key = (part_of(slot, pair, which) for which in range(3))
            lanes = slice(pair * pair_width, (pair + 1) * pair_width)
            upper = split(grad_attended[here, lanes])
            grad_weights = matmul_nt(upper, value)
            grad_scores = (grad_weights * slope_ref[slot * pairs + pair]).astype(bf16)
            grad_value = matmul_tn(weights_ref[slot * pairs + pair], upper)
            grad_query = matmul(side_by_side(grad_scores), split(key)) * score_scale
            grad_key = matmul_tn(grad_scores, split(query)) * score_scale
            for which, found in enumerate((grad_value, grad_query, grad_key)):
                first = (1 + which) * width + pair * pair_width
                at = slice(first, first + pair_width)
                grads_ref[here, at] = (found * dsilu_ref[here, at]).astype(bf16)

    for turn in range(bals):
        term_refs[turn][:, :features] = matmul(owner_order(nt_ref, turn), grads_ref[...]).astype(bf16)

    grad_normed = matmul_nt(grads_ref[...], w_in[...])
    grad_rows = (wide_cot + norm_back(grad_normed, normed_in, in_inverse)).astype(bf16)
    for group in range(groups):
        x_ref[group] = grad_rows[:, group * piece : (group + 1) * piece]
    for step in range(groups):
        grad_refs[step][...] = x_ref[group_here ^ step]


def pieces_kernel(tables, groups, bals, *refs):
    term_refs, grad_refs = refs[:bals], refs[bals : bals + groups - 1]
    plane_refs = refs[bals + groups - 1 : bals + 2 * groups - 1]
    table_refs = refs[bals + 2 * groups - 1 :]
    height, width = plane_refs[0].shape
    unit = height // tables

    def total(rows, columns):
        found = term_refs[0][rows, columns].astype(f32)
        for ref in term_refs[1:]:
            found = found + ref[rows, columns].astype(f32)
        return found.astype(bf16)

    for step, out in enumerate(plane_refs):
        rows = slice(step * height, (step + 1) * height)
        out[:, :width] = total(rows, slice(0, width))
        if step:
            grad = grad_refs[step - 1]
            columns = grad.shape[1]
            for index in range(grad.shape[0] // height):
                at = width + index * columns
                out[:, at : at + columns] = grad[index * height : (index + 1) * height, :]
    for table_step, out in enumerate(table_refs):
        for step in range(groups):
            first = step * height + table_step * unit
            rows = slice(first, first + unit)
            columns = slice(width, width + out.shape[1])
            out[step * unit : (step + 1) * unit, :] = total(rows, columns)


def place_kernel(scale, groups, slots, tables, bals, unit, scalar_ref, *refs):
    pieces = refs[:groups]
    in_ref, out_ref, scaled_ref, sems = refs[groups:]
    _, group_here, table_here = Scalars(scalar_ref, 0, bals, slots).place()
    features = in_ref.shape[1]
    copies = []
    for group_step, piece in enumerate(pieces):
        for table_step in range(tables):
            index = group_step * tables + table_step
            at = index * unit
            from_rows = slice(table_step * unit, (table_step + 1) * unit)
            scaled_ref[at : at + unit, :] = piece[from_rows, :].astype(f32) * scale
            owner = (group_here ^ group_step) * tables + (table_here ^ table_step)
            to = pl.ds(pl.multiple_of(owner * unit, unit), unit)
            rows = scaled_ref.at[pl.ds(at, unit), :]
            sem = sems.at[index]
            copies.append(
                pltpu.make_async_copy(rows.at[:, pl.ds(0, features)], in_ref.at[to, :], sem.at[0])
            )
            copies.append(
                pltpu.make_async_copy(
                    rows.at[:, pl.ds(features, out_ref.shape[1])], out_ref.at[to, :], sem.at[1]
                )
            )
            copies[-2].start()
            copies[-1].start()
    for copy in copies:
        copy.wait()


def sum_rounded(terms):
    total = terms[0].astype(f32)
    for term in terms[1:]:
        total = total + term.astype(f32)
    return total.astype(bf16)


def after(value, *others):
    return lax.optimization_barrier((value,) + others)[0]


def on_device(
    item_ids, seq_lengths, surplus_slot, helper_map, embed_tables, weight_in, weight_out, cotangent
):
    bal = lax.axis_index("bal")
    emb = lax.axis_index("emb")
    bals = lax.axis_size("bal")
    embs = lax.axis_size("emb")
    tables = item_ids.shape[2]
    groups = embs // tables
    _, rows, width = cotangent.shape
    slots = seq_lengths.shape[2]
    slot_rows = rows // slots
    distinct, columns = embed_tables.shape[1:]
    part = distinct // bals
    weight_part = weight_in.shape[0]
    table_here = emb // groups
    group_here = emb % groups
    width, features = weight_out.shape[1], weight_in.shape[1]
    unit = weight_part // embs
    owned = unit % 16 == 0
    unit = unit if owned else 0
    first = bals * (2 + slots)
    lane = lax.broadcasted_iota(jnp.int32, (1, LANES), 1)
    scalars = jnp.where(lane == first, bal, 0)
    scalars = jnp.where(lane == first + 1, group_here, scalars)
    scalars = jnp.where(lane == first + 2, table_here, scalars)
    fields = [surplus_slot.T, helper_map.T] + [seq_lengths[index] for index in range(bals)]
    at = 0
    for field in fields:
        width_here = field.shape[1]
        scalars = scalars + jnp.pad(field, ((0, 0), (at, LANES - at - width_here)))
        at += width_here

    share = lax.dynamic_slice_in_dim(embed_tables[0], bal * part, part, 0)
    fetched = [emb_swap(share, step * groups, embs) for step in range(1, tables)]

    ids = lax.dynamic_slice_in_dim(
        jnp.transpose(after(item_ids[0], share)), table_here * groups * rows, groups * rows, 1
    )
    plane_ids = with_swapped(ids.reshape(tables, groups * slots, 1, slot_rows), bals)
    wide_cot = cotangent[0].astype(f32)
    weights = jnp.concatenate([weight_in, weight_out], axis=1)
    scalars = after(scalars, share, wide_cot, weights)
    for bit in range((groups - 1).bit_length()):
        scalars = jnp.concatenate([scalars, emb_swap(scalars, 1 << bit, embs)], axis=0)

    fetched[0] = after(fetched[0], scalars, *plane_ids[1:])
    pieces = [piece for one in [share] + fetched for piece in with_swapped(one, bals)]

    found = pl.pallas_call(
        functools.partial(lookup_kernel, groups, slots, tables, bals),
        out_shape=[jax.ShapeDtypeStruct((rows, columns), bf16)] * groups,
        in_specs=[SMEM] + [VMEM] * (bals + len(pieces)),
        out_specs=[VMEM] * groups,
        cost_estimate=estimate(3),
        compiler_params=room(16),
    )(scalars, *plane_ids, *pieces)
    weights = with_swapped(after(weights, found[0]), bals)
    block = [found[0]] + [emb_swap(found[step], step, embs) for step in range(1, groups)]

    pairs = slots * HEADS // 2
    terms = jax.ShapeDtypeStruct((weight_part, features + width), bf16)
    results = pl.pallas_call(
        functools.partial(layer_kernel, groups, slots, tables, bals, unit),
        out_shape=[jax.ShapeDtypeStruct((rows, width), bf16)]
        + [jax.ShapeDtypeStruct((rows, columns), bf16)] * groups
        + [terms] * bals,
        in_specs=[SMEM] + [VMEM] * groups + [HBM] * bals + [VMEM],
        out_specs=[VMEM] * (1 + groups + bals),
        scratch_shapes=[
            pltpu.VMEM((groups, rows, columns), bf16),
            pltpu.VMEM((width, features), bf16),
            pltpu.VMEM((width, width), bf16),
            pltpu.VMEM((width, rows), bf16),
            pltpu.VMEM((width, rows), bf16),
            pltpu.VMEM((pairs, 2 * slot_rows, slot_rows), bf16),
            pltpu.VMEM((pairs, 2 * slot_rows, slot_rows), f32),
            pltpu.VMEM((rows, width), f32),
            pltpu.VMEM((rows, features - width), bf16),
            pltpu.VMEM((rows, features), f32),
            pltpu.VMEM((rows, features), bf16),
            pltpu.SemaphoreType.DMA((2 * bals,)),
        ],
        cost_estimate=estimate(7),
        compiler_params=room(36),
    )(scalars, *block, *weights, wide_cot)
    layer_out, results = results[0], results[1:]
    grads, results = results[:groups], results[groups:]

    def over_cores(parts):
        return sum_rounded([parts[0]] + [bal_swap(parts[turn], turn, bals) for turn in range(1, bals)])

    def to_plane(value):
        return [value] + [emb_swap(value, step, embs) for step in range(1, groups)]

    def table_sums(plane_grads):
        return pl.pallas_call(
            functools.partial(scatter_kernel, groups, slots, bals),
            out_shape=[jax.ShapeDtypeStruct((tables, part, columns), bf16)] * bals,
            in_specs=[SMEM] + [VMEM] * (bals + groups),
            out_specs=[VMEM] * bals,
            cost_estimate=estimate(3),
            compiler_params=room(16),
        )(scalars, *plane_ids, *plane_grads)

    grad_scale = (rows * embs * bals) ** -0.5
    if owned:
        height, wide = weight_part // groups, features + width
        last = wide // 2
        first = wide - last
        terms = [results[0]] + [bal_swap(results[turn], turn, bals) for turn in range(1, bals)]
        pieces = pl.pallas_call(
            functools.partial(pieces_kernel, tables, groups, bals),
            out_shape=[jax.ShapeDtypeStruct((height, first), bf16)]
            + [jax.ShapeDtypeStruct((height, first + rows // height * columns), bf16)] * (groups - 1)
            + [jax.ShapeDtypeStruct((groups * unit, last), bf16)] * tables,
            in_specs=[VMEM] * (bals + groups - 1),
            out_specs=[VMEM] * (groups + tables),
            compiler_params=room(12),
        )(*terms, *grads[1:])
        plane_pieces, table_pieces = pieces[:groups], pieces[groups:]
        came = [emb_swap(plane_pieces[step], step, embs) for step in range(1, groups)]
        mine = sum_rounded([plane_pieces[0]] + [value[:, :first] for value in came])
        mine = mine.reshape(tables, unit, first)
        sums = table_sums([grads[0]] + came)
        other = [emb_swap(table_pieces[step], step * groups, embs) for step in range(1, tables)]
        other = sum_rounded([table_pieces[0]] + other).reshape(groups, unit, last)
        own_sums = over_cores(sums)
        came = [emb_swap(mine[step], step * groups, embs) for step in range(1, tables)]
        other = [other[0]] + [emb_swap(other[step], step, embs) for step in range(1, groups)]
        final = jnp.concatenate([sum_rounded([mine[0]] + came), sum_rounded(other)], axis=1)
        gathered = [final] + [emb_swap(final, step * groups, embs) for step in range(1, tables)]
        back = to_plane(jnp.concatenate(gathered, axis=0))
        later = after(own_sums, *gathered[1:])
        swapped = [emb_swap(later[step], step * groups, embs) for step in range(1, tables)]
        swapped = [after(value, *back[1:]) for value in swapped]
    else:
        sums = table_sums([grads[0]] + [emb_swap(grads[step], step, embs) for step in range(1, groups)])
        own_sums = over_cores(sums)
        swapped = [emb_swap(own_sums[step], step * groups, embs) for step in range(1, tables)]
    table_sum = own_sums[0].astype(f32)
    for value in swapped:
        table_sum = table_sum + value.astype(f32)
    table_scale = (distinct / (bals * item_ids.shape[1])) ** 0.5

    if owned:
        total_in, total_out = pl.pallas_call(
            functools.partial(place_kernel, grad_scale, groups, slots, tables, bals, unit),
            out_shape=[
                jax.ShapeDtypeStruct((weight_part, features), f32),
                jax.ShapeDtypeStruct((weight_part, width), f32),
            ],
            in_specs=[SMEM] + [VMEM] * groups,
            out_specs=[HBM] * 2,
            scratch_shapes=[
                pltpu.VMEM((weight_part, features + width), f32),
                pltpu.SemaphoreType.DMA((groups * tables, 2)),
            ],
            cost_estimate=estimate(2),
            compiler_params=room(12),
        )(scalars, *back)
    else:
        total = lax.psum(over_cores(results).astype(f32), "emb") * grad_scale
        total_in, total_out = total[:, :features], total[:, features:]

    return layer_out[None], (table_sum * table_scale)[None], total_in, total_out


def solution(mesh):
    placed = (
        P("bal", None, None),
        P(None, "emb", None),
        P(None, "emb"),
        P(None, "emb"),
        P("emb", None, None),
        P("bal", None),
        P("bal", None),
        P("bal", "emb", None),
    )
    return jax.shard_map(
        on_device,
        mesh=mesh,
        in_specs=placed,
        out_specs=(P("bal", "emb", None), P("emb", "bal", None), P("bal", None), P("bal", None)),
        check_vma=False,
    )
```

```python
import functools

import jax
import jax.numpy as jnp
from jax import lax
from jax.experimental import pallas as pl
from jax.experimental.pallas import tpu as pltpu
from jax.sharding import PartitionSpec as P

HEADS = 8
EPS = 1e-05
LANES = 128

VMEM = pl.BlockSpec(memory_space=pltpu.VMEM)
SMEM = pl.BlockSpec(memory_space=pltpu.SMEM)
HBM = pl.BlockSpec(memory_space=pltpu.HBM)
f32 = jnp.float32
bf16 = jnp.bfloat16


def room(mib):
    return pltpu.CompilerParams(vmem_limit_bytes=mib * 1024 * 1024)


def estimate(microseconds):
    return pl.CostEstimate(flops=0, bytes_accessed=microseconds * 3_500_000, transcendentals=0)


def matmul(left, right):
    return lax.dot_general(left, right, (((1,), (0,)), ((), ())), preferred_element_type=f32)


def matmul_nt(left, right):
    return lax.dot_general(left, right, (((1,), (1,)), ((), ())), preferred_element_type=f32)


def matmul_tn(left, right):
    return lax.dot_general(left, right, (((0,), (0,)), ((), ())), preferred_element_type=f32)


def sigmoid(value):
    return 0.5 * jnp.tanh(0.5 * value) + 0.5


def bal_swap(value, step, count):
    return lax.ppermute(value, "bal", [(i, i ^ step) for i in range(count)])


def with_swapped(value, count):
    return [value] + [bal_swap(value, turn, count) for turn in range(1, count)]


def emb_swap(value, step, count):
    return lax.ppermute(value, "emb", [(i, i ^ step) for i in range(count)])


class Scalars:
    def __init__(self, ref, step, bals, slots):
        self.ref, self.step, self.bals, self.slots = ref, step, bals, slots

    def surplus(self, bal):
        return self.ref[self.step, bal]

    def source(self, bal):
        found = jnp.int32(0)
        for index in range(self.bals):
            found = found + jnp.where(self.ref[self.step, self.bals + index] == bal, index, 0)
        return found

    def length(self, bal, slot):
        return self.ref[self.step, 2 * self.bals + bal * self.slots + slot]

    def place(self):
        first = self.bals * (2 + self.slots)
        return self.ref[self.step, first], self.ref[self.step, first + 1], self.ref[self.step, first + 2]


def pick_ids(scalars, ids_refs, slots, tables):
    bal, group_here, _ = scalars[0].place()
    found = []
    for step, there in enumerate(scalars):
        group = group_here ^ step
        my_slot = there.surplus(bal)
        source = there.source(bal)
        from_slot = there.surplus(source)
        by_slot = [[] for _ in range(slots)]
        for table in tables:
            arrived = ids_refs[0][table, group * slots + from_slot]
            for turn in range(1, len(ids_refs)):
                other = ids_refs[turn][table, group * slots + from_slot]
                arrived = jnp.where(source ^ bal == turn, other, arrived)
            for slot in range(slots):
                own = ids_refs[0][table, group * slots + slot]
                by_slot[slot].append(jnp.where(my_slot == slot, arrived, own))
        found.append(by_slot)
    return found


def table_order(table_here, tables):
    return [table_here ^ step for step in range(tables)]


def lookup_kernel(groups, slots, tables, bals, *refs):
    refs = list(refs)
    take = lambda count: [refs.pop(0) for _ in range(count)]
    (scalar_ref,) = take(1)
    scalars = [Scalars(scalar_ref, step, bals, slots) for step in range(groups)]
    ids_refs = take(bals)
    pieces = [take(bals) for _ in range(tables)]
    out_refs = refs
    bal, _, table_here = scalars[0].place()
    part, columns = pieces[0][0].shape
    slot_rows = ids_refs[0].shape[3]
    lane = lax.broadcasted_iota(jnp.int32, (LANES, LANES), 1)
    ids = pick_ids(scalars, ids_refs, slots, table_order(table_here, tables))
    for group in range(groups):
        for slot in range(slots):
            for first in range(0, slot_rows, LANES):
                total = jnp.zeros((LANES, columns), f32)
                for table in range(tables):
                    row = ids[group][slot][table][:, first : first + LANES]
                    column = jnp.transpose(jnp.broadcast_to(row, (LANES, LANES)))
                    for turn, ref in enumerate(pieces[table]):
                        shifted = column - (bal ^ turn) * part
                        hot = jnp.concatenate(
                            [
                                jnp.where(shifted == lane + at, 1.0, 0.0).astype(bf16)
                                for at in range(0, part, LANES)
                            ],
                            axis=1,
                        )
                        total = total + matmul(hot, ref[...])
                at = slot * slot_rows + first
                out_refs[group][at : at + LANES, :] = total.astype(bf16)


def scatter_kernel(groups, slots, bals, *refs):
    refs = list(refs)
    take = lambda count: [refs.pop(0) for _ in range(count)]
    (scalar_ref,) = take(1)
    scalars = [Scalars(scalar_ref, step, bals, slots) for step in range(groups)]
    ids_refs, grad_refs, out_refs = take(bals), take(groups)[::-1], refs
    bal, _, table_here = scalars[0].place()
    tables, part, _ = out_refs[0].shape
    slot_rows = ids_refs[0].shape[3]
    height = min(part, 256)
    iota = lax.broadcasted_iota(jnp.int32, (height, slot_rows), 0)
    ids = pick_ids(scalars, ids_refs, slots, table_order(table_here, tables))
    columns = out_refs[0].shape[2]

    def rows_of(ref):
        height = ref.shape[0]
        first = ref.shape[1] - slots * slot_rows // height * columns
        return [ref[:, at : at + columns] for at in range(first, ref.shape[1], columns)]

    grads = jnp.concatenate([piece for ref in grad_refs for piece in rows_of(ref)], axis=0)
    for table in range(tables):
        for turn in range(bals):
            for at in range(0, part, height):
                start = (bal ^ turn) * part + at
                hot = jnp.concatenate(
                    [
                        jnp.where(iota == ids[group][slot][table] - start, 1.0, 0.0).astype(bf16)
                        for group in range(groups)
                        for slot in range(slots)
                    ],
                    axis=1,
                )
                out_refs[turn][table, at : at + height, :] = matmul(hot, grads).astype(bf16)


def norm(values):
    average = jnp.mean(values, axis=1, keepdims=True)
    centred = values - average
    inverse = lax.rsqrt(jnp.mean(centred * centred, axis=1, keepdims=True) + EPS)
    return centred * inverse, inverse


def norm_back(incoming, normed, inverse):
    first = jnp.mean(incoming, axis=1, keepdims=True)
    second = jnp.mean(incoming * normed, axis=1, keepdims=True)
    return inverse * (incoming - first - normed * second)


def layer_kernel(groups, slots, tables, bals, unit, scalar_ref, *refs):
    refs = list(refs)
    take = lambda count: [refs.pop(0) for _ in range(count)]
    block_refs = take(groups)[::-1]
    weight_refs = take(bals)
    (cot_ref,) = take(1)
    (layer_ref,) = take(1)
    grad_refs = take(groups)
    term_refs = take(bals)
    (x_ref, halves_ref, wide_ref, nt_ref, mt_ref, weights_ref, slope_ref, gate_ref, heads_ref, dsilu_ref, grads_ref) = refs

    scalars = Scalars(scalar_ref, 0, bals, slots)
    bal, group_here, table_here = scalars.place()
    rows, width = cot_ref.shape
    slot_rows = rows // slots
    head_width = width // HEADS
    score_scale = head_width**-0.5
    piece = block_refs[0].shape[1]
    part, features = weight_refs[0].shape[0], weight_refs[0].shape[1] - width

    def times_parts(value, first, last):
        for index in range(bals):
            halves_ref[index] = value[:, index * part : (index + 1) * part]
        found = matmul(halves_ref[bal], weight_refs[0][:, first:last])
        for turn in range(1, bals):
            found = found + matmul(halves_ref[bal ^ turn], weight_refs[turn][:, first:last])
        return found

    def times_parts_nt(value, first, last):
        for turn in range(bals):
            wide_ref[bal ^ turn] = matmul_nt(value, weight_refs[turn][:, first:last])
        return jnp.concatenate([wide_ref[index] for index in range(bals)], axis=1)

    my_slot = scalars.surplus(bal)
    source = scalars.source(bal)
    moved = scalars.length(source, scalars.surplus(source))
    lengths = [jnp.where(my_slot == slot, moved, scalars.length(bal, slot)) for slot in range(slots)]

    for step in range(groups):
        x_ref[group_here ^ step] = block_refs[step][...]
    x = jnp.concatenate([x_ref[group] for group in range(groups)], axis=1).astype(f32)
    normed_in, in_inverse = norm(x)
    nt_ref[...] = jnp.transpose(normed_in).astype(bf16)
    projected = times_parts(normed_in.astype(bf16), 0, features)
    logistic = sigmoid(projected)
    active = projected * logistic
    dsilu_ref[...] = logistic + active * (1.0 - logistic)
    gate_ref[...] = active[:, :width]
    heads_ref[...] = active[:, width:].astype(bf16)

    pair_width = 2 * head_width
    low = lax.broadcasted_iota(jnp.int32, (slot_rows, pair_width), 1) < head_width
    row_at = lax.broadcasted_iota(jnp.int32, (slot_rows, slot_rows), 0)
    col_at = lax.broadcasted_iota(jnp.int32, (slot_rows, slot_rows), 1)

    def split(value):
        zero = jnp.zeros_like(value)
        return jnp.concatenate([jnp.where(low, value, zero), jnp.where(low, zero, value)], axis=0)

    def side_by_side(value):
        return jnp.concatenate([value[:slot_rows], value[slot_rows:]], axis=1)

    def part_of(slot, pair, which):
        first = which * width + pair * pair_width
        return heads_ref[slot * slot_rows : (slot + 1) * slot_rows, first : first + pair_width]

    pairs = HEADS // 2
    attended = []
    for slot in range(slots):
        live = (col_at <= row_at) & (row_at < lengths[slot])
        allowed = jnp.where(live, 1.0 / slot_rows, 0.0)
        allowed = jnp.concatenate([allowed, allowed], axis=0)
        across = []
        for pair in range(pairs):
            value, query, key = (part_of(slot, pair, which) for which in range(3))
            scores = matmul_nt(split(query), key) * score_scale
            q = sigmoid(scores)
            sq = scores * q
            weights = (sq * allowed).astype(bf16)
            weights_ref[slot * pairs + pair] = weights
            slope_ref[slot * pairs + pair] = allowed * (q + sq * (1.0 - q))
            across.append(matmul(side_by_side(weights), split(value)))
        attended.append(jnp.concatenate(across, axis=1))
    normed_out, out_inverse = norm(jnp.concatenate(attended, axis=0))
    gate = gate_ref[...]
    mixed = normed_out * gate
    mt_ref[...] = jnp.transpose(mixed).astype(bf16)
    layer_ref[...] = (x + times_parts(mixed.astype(bf16), features, features + width)).astype(bf16)

    wide_cot = cot_ref[...]
    cot = wide_cot.astype(bf16)
    grad_mixed = times_parts_nt(cot, features, features + width)
    grad_attended = norm_back(grad_mixed * gate, normed_out, out_inverse).astype(bf16)
    grads_ref[:, :width] = (grad_mixed * normed_out * dsilu_ref[:, :width]).astype(bf16)

    def owner_order(ref, turn):
        start = (bal ^ turn) * part
        if part != groups * tables * unit:
            return ref[pl.ds(pl.multiple_of(start, part), part), :]
        found = []
        for group_step in range(groups):
            for table_step in range(tables):
                owner = (group_here ^ group_step) * tables + (table_here ^ table_step)
                at = pl.multiple_of(start + owner * unit, unit)
                found.append(ref[pl.ds(at, unit), :])
        return jnp.concatenate(found, axis=0)

    for turn in range(bals):
        term_refs[turn][:, features:] = matmul(owner_order(mt_ref, turn), cot).astype(bf16)

    for slot in range(slots):
        here = slice(slot * slot_rows, (slot + 1) * slot_rows)
        for pair in range(pairs):
            value, query, key = (part_of(slot, pair, which) for which in range(3))
            lanes = slice(pair * pair_width, (pair + 1) * pair_width)
            upper = split(grad_attended[here, lanes])
            grad_weights = matmul_nt(upper, value)
            grad_scores = (grad_weights * slope_ref[slot * pairs + pair]).astype(bf16)
            grad_value = matmul_tn(weights_ref[slot * pairs + pair], upper)
            grad_query = matmul(side_by_side(grad_scores), split(key)) * score_scale
            grad_key = matmul_tn(grad_scores, split(query)) * score_scale
            for which, found in enumerate((grad_value, grad_query, grad_key)):
                first = (1 + which) * width + pair * pair_width
                at = slice(first, first + pair_width)
                grads_ref[here, at] = (found * dsilu_ref[here, at]).astype(bf16)

    for turn in range(bals):
        term_refs[turn][:, :features] = matmul(owner_order(nt_ref, turn), grads_ref[...]).astype(bf16)

    grad_normed = times_parts_nt(grads_ref[...], 0, features)
    grad_rows = (wide_cot + norm_back(grad_normed, normed_in, in_inverse)).astype(bf16)
    for group in range(groups):
        x_ref[group] = grad_rows[:, group * piece : (group + 1) * piece]
    for step in range(groups):
        grad_refs[step][...] = x_ref[group_here ^ step]


def pieces_kernel(bals, *refs):
    count = len(refs) - bals
    groups = (count + 1) // 2
    term_refs, grad_refs = refs[:bals], refs[bals : bals + groups - 1]
    out_refs = refs[bals + groups - 1 :]
    height, width = out_refs[0].shape
    for step, out in enumerate(out_refs):
        rows = slice(step * height, (step + 1) * height)
        total = term_refs[0][rows, :].astype(f32)
        for ref in term_refs[1:]:
            total = total + ref[rows, :].astype(f32)
        out[:, :width] = total.astype(bf16)
        if step:
            grad = grad_refs[step - 1]
            columns = grad.shape[1]
            for index in range(grad.shape[0] // height):
                at = width + index * columns
                out[:, at : at + columns] = grad[index * height : (index + 1) * height, :]


def place_kernel(scale, steps, slots, tables, bals, unit, scalar_ref, *refs):
    pieces = refs[: len(steps)]
    in_ref, out_ref, scaled_ref, sems = refs[-4:]
    _, group_here, table_here = Scalars(scalar_ref, 0, bals, slots).place()
    features = in_ref.shape[1]
    copies = []
    for number, (group_step, piece) in enumerate(zip(steps, pieces)):
        for table_step in range(tables):
            index = number * tables + table_step
            at = index * unit
            from_rows = slice(table_step * unit, (table_step + 1) * unit)
            scaled_ref[at : at + unit, :] = piece[from_rows, :].astype(f32) * scale
            owner = (group_here ^ group_step) * tables + (table_here ^ table_step)
            to = pl.ds(pl.multiple_of(owner * unit, unit), unit)
            rows = scaled_ref.at[pl.ds(at, unit), :]
            sem = sems.at[index]
            copies.append(
                pltpu.make_async_copy(rows.at[:, pl.ds(0, features)], in_ref.at[to, :], sem.at[0])
            )
            copies.append(
                pltpu.make_async_copy(
                    rows.at[:, pl.ds(features, out_ref.shape[1])], out_ref.at[to, :], sem.at[1]
                )
            )
            copies[-2].start()
            copies[-1].start()
    for copy in copies:
        copy.wait()


def sum_rounded(terms):
    total = terms[0].astype(f32)
    for term in terms[1:]:
        total = total + term.astype(f32)
    return total.astype(bf16)


def after(value, *others):
    return lax.optimization_barrier((value,) + others)[0]


def on_device(
    item_ids, seq_lengths, surplus_slot, helper_map, embed_tables, weight_in, weight_out, cotangent
):
    bal = lax.axis_index("bal")
    emb = lax.axis_index("emb")
    bals = lax.axis_size("bal")
    embs = lax.axis_size("emb")
    tables = item_ids.shape[2]
    groups = embs // tables
    _, rows, width = cotangent.shape
    slots = seq_lengths.shape[2]
    slot_rows = rows // slots
    distinct, columns = embed_tables.shape[1:]
    part = distinct // bals
    weight_part = weight_in.shape[0]
    table_here = emb // groups
    group_here = emb % groups
    width, features = weight_out.shape[1], weight_in.shape[1]
    unit = weight_part // embs
    owned = unit % 16 == 0
    unit = unit if owned else 0
    first = bals * (2 + slots)
    lane = lax.broadcasted_iota(jnp.int32, (1, LANES), 1)
    scalars = jnp.where(lane == first, bal, 0)
    scalars = jnp.where(lane == first + 1, group_here, scalars)
    scalars = jnp.where(lane == first + 2, table_here, scalars)
    fields = [surplus_slot.T, helper_map.T] + [seq_lengths[index] for index in range(bals)]
    at = 0
    for field in fields:
        width_here = field.shape[1]
        scalars = scalars + jnp.pad(field, ((0, 0), (at, LANES - at - width_here)))
        at += width_here

    share = lax.dynamic_slice_in_dim(embed_tables[0], bal * part, part, 0)
    fetched = [emb_swap(share, step * groups, embs) for step in range(1, tables)]

    ids = lax.dynamic_slice_in_dim(
        jnp.transpose(after(item_ids[0], share)), table_here * groups * rows, groups * rows, 1
    )
    plane_ids = with_swapped(ids.reshape(tables, groups * slots, 1, slot_rows), bals)
    wide_cot = cotangent[0].astype(f32)
    scalars = after(scalars, share, wide_cot)
    for bit in range((groups - 1).bit_length()):
        scalars = jnp.concatenate([scalars, emb_swap(scalars, 1 << bit, embs)], axis=0)

    fetched[0] = after(fetched[0], scalars)
    pieces = [piece for one in [share] + fetched for piece in with_swapped(one, bals)]

    found = pl.pallas_call(
        functools.partial(lookup_kernel, groups, slots, tables, bals),
        out_shape=[jax.ShapeDtypeStruct((rows, columns), bf16)] * groups,
        in_specs=[SMEM] + [VMEM] * (bals + len(pieces)),
        out_specs=[VMEM] * groups,
        cost_estimate=estimate(3),
        compiler_params=room(16),
    )(scalars, *plane_ids, *pieces)
    weights = jnp.concatenate([weight_in, weight_out], axis=1)
    weights = with_swapped(after(weights, found[0]), bals)
    block = [found[0]] + [emb_swap(found[step], step, embs) for step in range(1, groups)]

    pairs = slots * HEADS // 2
    terms = jax.ShapeDtypeStruct((weight_part, features + width), bf16)
    results = pl.pallas_call(
        functools.partial(layer_kernel, groups, slots, tables, bals, unit),
        out_shape=[jax.ShapeDtypeStruct((rows, width), bf16)]
        + [jax.ShapeDtypeStruct((rows, columns), bf16)] * groups
        + [terms] * bals,
        in_specs=[SMEM] + [VMEM] * (groups + bals + 1),
        out_specs=[VMEM] * (1 + groups + bals),
        scratch_shapes=[
            pltpu.VMEM((groups, rows, columns), bf16),
            pltpu.VMEM((bals, rows, weight_part), bf16),
            pltpu.VMEM((bals, rows, weight_part), f32),
            pltpu.VMEM((width, rows), bf16),
            pltpu.VMEM((width, rows), bf16),
            pltpu.VMEM((pairs, 2 * slot_rows, slot_rows), bf16),
            pltpu.VMEM((pairs, 2 * slot_rows, slot_rows), f32),
            pltpu.VMEM((rows, width), f32),
            pltpu.VMEM((rows, features - width), bf16),
            pltpu.VMEM((rows, features), f32),
            pltpu.VMEM((rows, features), bf16),
        ],
        cost_estimate=estimate(7),
        compiler_params=room(36),
    )(scalars, *block[::-1], *weights, wide_cot)
    layer_out, results = results[0], results[1:]
    grads, results = results[:groups], results[groups:]

    def over_cores(parts):
        return sum_rounded([parts[0]] + [bal_swap(parts[turn], turn, bals) for turn in range(1, bals)])

    def to_plane(value):
        return [value] + [emb_swap(value, step, embs) for step in range(1, groups)]

    def table_sums(plane_grads):
        return pl.pallas_call(
            functools.partial(scatter_kernel, groups, slots, bals),
            out_shape=[jax.ShapeDtypeStruct((tables, part, columns), bf16)] * bals,
            in_specs=[SMEM] + [VMEM] * (bals + groups),
            out_specs=[VMEM] * bals,
            cost_estimate=estimate(3),
            compiler_params=room(16),
        )(scalars, *plane_ids, *plane_grads[::-1])

    grad_scale = (rows * embs * bals) ** -0.5
    if owned:
        height, wide = weight_part // groups, features + width
        terms = [results[0]] + [bal_swap(results[turn], turn, bals) for turn in range(1, bals)]
        pieces = pl.pallas_call(
            functools.partial(pieces_kernel, bals),
            out_shape=[jax.ShapeDtypeStruct((height, wide), bf16)]
            + [jax.ShapeDtypeStruct((height, wide + rows // height * columns), bf16)] * (groups - 1),
            in_specs=[VMEM] * (bals + groups - 1),
            out_specs=[VMEM] * groups,
            compiler_params=room(12),
        )(*terms, *grads[1:])
        came = [emb_swap(pieces[step], step, embs) for step in range(1, groups)]
        mine = sum_rounded([value[:, :wide] for value in came[::-1]] + [pieces[0]])
        mine = mine.reshape(tables, unit, wide)
        sums = table_sums([grads[0]] + came)
        own_sums = over_cores(sums)
        came = [emb_swap(mine[step], step * groups, embs) for step in range(1, tables)]
        final = sum_rounded(came[-1:] + came[:-1] + [mine[0]])
        gathered = [final] + [emb_swap(final, step * groups, embs) for step in range(1, tables)]
        back = to_plane(jnp.concatenate(gathered, axis=0))
        later = after(own_sums, *gathered[1:])
        swapped = [emb_swap(later[step], step * groups, embs) for step in range(1, tables)]
        swapped = [after(value, *back[1:]) for value in swapped]
    else:
        sums = table_sums([grads[0]] + [emb_swap(grads[step], step, embs) for step in range(1, groups)])
        own_sums = over_cores(sums)
        swapped = [emb_swap(own_sums[step], step * groups, embs) for step in range(1, tables)]
    table_sum = swapped[-1].astype(f32)
    for value in swapped[:-1] + [own_sums[0]]:
        table_sum = table_sum + value.astype(f32)
    table_scale = (distinct / (bals * item_ids.shape[1])) ** 0.5

    if owned:
        totals = []
        for steps in ([0] + list(range(groups - 1, 1, -1))[: groups // 2 - 1], None):
            steps = steps or [step for step in range(1, groups) if step not in done]
            done = steps
            totals = pl.pallas_call(
                functools.partial(place_kernel, grad_scale, steps, slots, tables, bals, unit),
                out_shape=[
                    jax.ShapeDtypeStruct((weight_part, features), f32),
                    jax.ShapeDtypeStruct((weight_part, width), f32),
                ],
                in_specs=[SMEM] + [VMEM] * len(steps) + [HBM] * len(totals),
                out_specs=[HBM] * 2,
                scratch_shapes=[
                    pltpu.VMEM((len(steps) * tables * unit, features + width), f32),
                    pltpu.SemaphoreType.DMA((len(steps) * tables, 2)),
                ],
                input_output_aliases={1 + len(steps) + index: index for index in range(len(totals))},
                cost_estimate=estimate(1),
                compiler_params=room(12),
            )(scalars, *[back[step] for step in steps], *totals)
        total_in, total_out = totals
    else:
        total = lax.psum(over_cores(results).astype(f32), "emb") * grad_scale
        total_in, total_out = total[:, :features], total[:, features:]

    return layer_out[None], (table_sum * table_scale)[None], total_in, total_out


def solution(mesh):
    placed = (
        P("bal", None, None),
        P(None, "emb", None),
        P(None, "emb"),
        P(None, "emb"),
        P("emb", None, None),
        P("bal", None),
        P("bal", None),
        P("bal", "emb", None),
    )
    return jax.shard_map(
        on_device,
        mesh=mesh,
        in_specs=placed,
        out_specs=(P("bal", "emb", None), P("emb", "bal", None), P("bal", None), P("bal", None)),
        check_vma=False,
    )
```

```python
import functools

import jax
import jax.numpy as jnp
from jax import lax
from jax.experimental import pallas as pl
from jax.experimental.pallas import tpu as pltpu
from jax.sharding import PartitionSpec as P

HEADS = 8
EPS = 1e-05
LANES = 128

VMEM = pl.BlockSpec(memory_space=pltpu.VMEM)
SMEM = pl.BlockSpec(memory_space=pltpu.SMEM)
HBM = pl.BlockSpec(memory_space=pltpu.HBM)
f32 = jnp.float32
bf16 = jnp.bfloat16


def room(mib):
    return pltpu.CompilerParams(vmem_limit_bytes=mib * 1024 * 1024)


def estimate(microseconds):
    return pl.CostEstimate(flops=0, bytes_accessed=microseconds * 3_500_000, transcendentals=0)


def matmul(left, right):
    return lax.dot_general(left, right, (((1,), (0,)), ((), ())), preferred_element_type=f32)


def matmul_nt(left, right):
    return lax.dot_general(left, right, (((1,), (1,)), ((), ())), preferred_element_type=f32)


def matmul_tn(left, right):
    return lax.dot_general(left, right, (((0,), (0,)), ((), ())), preferred_element_type=f32)


def sigmoid(value):
    return 0.5 * jnp.tanh(0.5 * value) + 0.5


def bal_swap(value, step, count):
    return lax.ppermute(value, "bal", [(i, i ^ step) for i in range(count)])


def with_swapped(value, count):
    return [value] + [bal_swap(value, turn, count) for turn in range(1, count)]


def emb_swap(value, step, count):
    return lax.ppermute(value, "emb", [(i, i ^ step) for i in range(count)])


class Scalars:
    def __init__(self, ref, step, bals, slots):
        self.ref, self.step, self.bals, self.slots = ref, step, bals, slots

    def surplus(self, bal):
        return self.ref[self.step, bal]

    def source(self, bal):
        found = jnp.int32(0)
        for index in range(self.bals):
            found = found + jnp.where(self.ref[self.step, self.bals + index] == bal, index, 0)
        return found

    def length(self, bal, slot):
        return self.ref[self.step, 2 * self.bals + bal * self.slots + slot]

    def place(self):
        first = self.bals * (2 + self.slots)
        return self.ref[self.step, first], self.ref[self.step, first + 1], self.ref[self.step, first + 2]


def pick_ids(scalars, ids_refs, slots, tables):
    bal, group_here, _ = scalars[0].place()
    found = []
    for step, there in enumerate(scalars):
        group = group_here ^ step
        my_slot = there.surplus(bal)
        source = there.source(bal)
        from_slot = there.surplus(source)
        by_slot = [[] for _ in range(slots)]
        for table in tables:
            arrived = ids_refs[0][table, group * slots + from_slot]
            for turn in range(1, len(ids_refs)):
                other = ids_refs[turn][table, group * slots + from_slot]
                arrived = jnp.where(source ^ bal == turn, other, arrived)
            for slot in range(slots):
                own = ids_refs[0][table, group * slots + slot]
                by_slot[slot].append(jnp.where(my_slot == slot, arrived, own))
        found.append(by_slot)
    return found


def table_order(table_here, tables):
    return [table_here ^ step for step in range(tables)]


def lookup_kernel(groups, slots, tables, bals, *refs):
    refs = list(refs)
    take = lambda count: [refs.pop(0) for _ in range(count)]
    (scalar_ref,) = take(1)
    scalars = [Scalars(scalar_ref, step, bals, slots) for step in range(groups)]
    ids_refs = take(bals)
    pieces = [take(bals) for _ in range(tables)]
    out_refs = refs
    bal, _, table_here = scalars[0].place()
    part, columns = pieces[0][0].shape
    slot_rows = ids_refs[0].shape[3]
    lane = lax.broadcasted_iota(jnp.int32, (LANES, LANES), 1)
    ids = pick_ids(scalars, ids_refs, slots, table_order(table_here, tables))
    rows = out_refs[0].shape[0]
    total = jnp.zeros((groups * rows, columns), f32)
    for table in range(tables):
        found = []
        for group in range(groups):
            for slot in range(slots):
                for first in range(0, slot_rows, LANES):
                    row = ids[group][slot][table][:, first : first + LANES]
                    found.append(jnp.transpose(jnp.broadcast_to(row, (LANES, LANES))))
        column = jnp.concatenate(found, axis=0)
        for turn, ref in enumerate(pieces[table]):
            shifted = column - (bal ^ turn) * part
            hot = []
            for at in range(0, part, LANES):
                here = [shifted[row : row + LANES] == lane + at for row in range(0, groups * rows, LANES)]
                here = [jnp.where(one, 1.0, 0.0).astype(bf16) for one in here]
                hot.append(jnp.concatenate(here, axis=0))
            total = total + matmul(jnp.concatenate(hot, axis=1), ref[...])
    for group in range(groups):
        out_refs[group][...] = total[group * rows : (group + 1) * rows].astype(bf16)


def scatter_kernel(groups, slots, bals, *refs):
    refs = list(refs)
    take = lambda count: [refs.pop(0) for _ in range(count)]
    (scalar_ref,) = take(1)
    scalars = [Scalars(scalar_ref, step, bals, slots) for step in range(groups)]
    ids_refs, grad_refs, out_refs = take(bals), take(groups)[::-1], refs
    bal, _, table_here = scalars[0].place()
    tables, part, _ = out_refs[0].shape
    slot_rows = ids_refs[0].shape[3]
    height = min(part, 256)
    iota = lax.broadcasted_iota(jnp.int32, (height, slot_rows), 0)
    ids = pick_ids(scalars, ids_refs, slots, table_order(table_here, tables))
    columns = out_refs[0].shape[2]

    def rows_of(ref):
        height = ref.shape[0]
        first = ref.shape[1] - slots * slot_rows // height * columns
        return [ref[:, at : at + columns] for at in range(first, ref.shape[1], columns)]

    grads = jnp.concatenate([piece for ref in grad_refs for piece in rows_of(ref)], axis=0)
    for table in range(tables):
        for turn in range(bals):
            for at in range(0, part, height):
                start = (bal ^ turn) * part + at
                hot = jnp.concatenate(
                    [
                        jnp.where(iota == ids[group][slot][table] - start, 1.0, 0.0).astype(bf16)
                        for group in range(groups)
                        for slot in range(slots)
                    ],
                    axis=1,
                )
                out_refs[turn][table, at : at + height, :] = matmul(hot, grads).astype(bf16)


def norm(values):
    average = jnp.mean(values, axis=1, keepdims=True)
    centred = values - average
    inverse = lax.rsqrt(jnp.mean(centred * centred, axis=1, keepdims=True) + EPS)
    return centred * inverse, inverse


def norm_back(incoming, normed, inverse):
    first = jnp.mean(incoming, axis=1, keepdims=True)
    second = jnp.mean(incoming * normed, axis=1, keepdims=True)
    return inverse * (incoming - first - normed * second)


def layer_kernel(groups, slots, tables, bals, unit, scalar_ref, *refs):
    refs = list(refs)
    take = lambda count: [refs.pop(0) for _ in range(count)]
    block_refs = take(groups)[::-1]
    weight_refs = take(bals)
    (cot_ref,) = take(1)
    (layer_ref,) = take(1)
    grad_refs = take(groups)
    term_refs = take(bals)
    (x_ref, halves_ref, wide_ref, nt_ref, mt_ref, weights_ref, slope_ref, gate_ref, heads_ref, dsilu_ref, grads_ref) = refs

    scalars = Scalars(scalar_ref, 0, bals, slots)
    bal, group_here, table_here = scalars.place()
    rows, width = cot_ref.shape
    slot_rows = rows // slots
    head_width = width // HEADS
    score_scale = head_width**-0.5
    piece = block_refs[0].shape[1]
    part, features = weight_refs[0].shape[0], weight_refs[0].shape[1] - width

    def times_parts(value, first, last):
        for index in range(bals):
            halves_ref[index] = value[:, index * part : (index + 1) * part]
        found = matmul(halves_ref[bal], weight_refs[0][:, first:last])
        for turn in range(1, bals):
            found = found + matmul(halves_ref[bal ^ turn], weight_refs[turn][:, first:last])
        return found

    def times_parts_nt(value, first, last):
        for turn in range(bals):
            wide_ref[bal ^ turn] = matmul_nt(value, weight_refs[turn][:, first:last])
        return jnp.concatenate([wide_ref[index] for index in range(bals)], axis=1)

    my_slot = scalars.surplus(bal)
    source = scalars.source(bal)
    moved = scalars.length(source, scalars.surplus(source))
    lengths = [jnp.where(my_slot == slot, moved, scalars.length(bal, slot)) for slot in range(slots)]

    for step in range(groups):
        x_ref[group_here ^ step] = block_refs[step][...]
    x = jnp.concatenate([x_ref[group] for group in range(groups)], axis=1).astype(f32)
    normed_in, in_inverse = norm(x)
    nt_ref[...] = jnp.transpose(normed_in).astype(bf16)
    projected = times_parts(normed_in.astype(bf16), 0, features)
    logistic = sigmoid(projected)
    active = projected * logistic
    dsilu_ref[...] = logistic + active * (1.0 - logistic)
    gate_ref[...] = active[:, :width]
    heads_ref[...] = active[:, width:].astype(bf16)

    pair_width = 2 * head_width
    low = lax.broadcasted_iota(jnp.int32, (slot_rows, pair_width), 1) < head_width
    row_at = lax.broadcasted_iota(jnp.int32, (slot_rows, slot_rows), 0)
    col_at = lax.broadcasted_iota(jnp.int32, (slot_rows, slot_rows), 1)

    def split(value):
        zero = jnp.zeros_like(value)
        return jnp.concatenate([jnp.where(low, value, zero), jnp.where(low, zero, value)], axis=0)

    def side_by_side(value):
        return jnp.concatenate([value[:slot_rows], value[slot_rows:]], axis=1)

    def part_of(slot, pair, which):
        first = which * width + pair * pair_width
        return heads_ref[slot * slot_rows : (slot + 1) * slot_rows, first : first + pair_width]

    pairs = HEADS // 2
    attended = []
    for slot in range(slots):
        live = (col_at <= row_at) & (row_at < lengths[slot])
        allowed = jnp.where(live, 1.0 / slot_rows, 0.0)
        allowed = jnp.concatenate([allowed, allowed], axis=0)
        across = []
        for pair in range(pairs):
            value, query, key = (part_of(slot, pair, which) for which in range(3))
            scores = matmul_nt(split(query), key) * score_scale
            q = sigmoid(scores)
            sq = scores * q
            weights = (sq * allowed).astype(bf16)
            weights_ref[slot * pairs + pair] = weights
            slope_ref[slot * pairs + pair] = allowed * (q + sq * (1.0 - q))
            across.append(matmul(side_by_side(weights), split(value)))
        attended.append(jnp.concatenate(across, axis=1))
    normed_out, out_inverse = norm(jnp.concatenate(attended, axis=0))
    gate = gate_ref[...]
    mixed = normed_out * gate
    mt_ref[...] = jnp.transpose(mixed).astype(bf16)
    layer_ref[...] = (x + times_parts(mixed.astype(bf16), features, features + width)).astype(bf16)

    wide_cot = cot_ref[...]
    cot = wide_cot.astype(bf16)
    grad_mixed = times_parts_nt(cot, features, features + width)
    grad_attended = norm_back(grad_mixed * gate, normed_out, out_inverse).astype(bf16)
    grads_ref[:, :width] = (grad_mixed * normed_out * dsilu_ref[:, :width]).astype(bf16)

    def owner_order(ref, turn):
        start = (bal ^ turn) * part
        if part != groups * tables * unit:
            return ref[pl.ds(pl.multiple_of(start, part), part), :]
        found = []
        for group_step in range(groups):
            for table_step in range(tables):
                owner = (group_here ^ group_step) * tables + (table_here ^ table_step)
                at = pl.multiple_of(start + owner * unit, unit)
                found.append(ref[pl.ds(at, unit), :])
        return jnp.concatenate(found, axis=0)

    def emit_terms(ref, right, first):
        left = jnp.concatenate([owner_order(ref, turn) for turn in range(bals)], axis=0)
        found = matmul(left, right).astype(bf16)
        for turn in range(bals):
            rows_here = slice(turn * part, (turn + 1) * part)
            term_refs[turn][:, first : first + right.shape[1]] = found[rows_here]

    emit_terms(mt_ref, cot, features)

    for slot in range(slots):
        here = slice(slot * slot_rows, (slot + 1) * slot_rows)
        for pair in range(pairs):
            value, query, key = (part_of(slot, pair, which) for which in range(3))
            lanes = slice(pair * pair_width, (pair + 1) * pair_width)
            upper = split(grad_attended[here, lanes])
            grad_weights = matmul_nt(upper, value)
            grad_scores = (grad_weights * slope_ref[slot * pairs + pair]).astype(bf16)
            grad_value = matmul_tn(weights_ref[slot * pairs + pair], upper)
            grad_query = matmul(side_by_side(grad_scores), split(key)) * score_scale
            grad_key = matmul_tn(grad_scores, split(query)) * score_scale
            for which, found in enumerate((grad_value, grad_query, grad_key)):
                first = (1 + which) * width + pair * pair_width
                at = slice(first, first + pair_width)
                grads_ref[here, at] = (found * dsilu_ref[here, at]).astype(bf16)

    emit_terms(nt_ref, grads_ref[...], 0)

    grad_normed = times_parts_nt(grads_ref[...], 0, features)
    grad_rows = (wide_cot + norm_back(grad_normed, normed_in, in_inverse)).astype(bf16)
    for group in range(groups):
        x_ref[group] = grad_rows[:, group * piece : (group + 1) * piece]
    for step in range(groups):
        grad_refs[step][...] = x_ref[group_here ^ step]


def pieces_kernel(bals, *refs):
    count = len(refs) - bals
    groups = (count + 1) // 2
    term_refs, grad_refs = refs[:bals], refs[bals : bals + groups - 1]
    out_refs = refs[bals + groups - 1 :]
    height, width = out_refs[0].shape
    for step, out in enumerate(out_refs):
        rows = slice(step * height, (step + 1) * height)
        total = term_refs[0][rows, :].astype(f32)
        for ref in term_refs[1:]:
            total = total + ref[rows, :].astype(f32)
        out[:, :width] = total.astype(bf16)
        if step:
            grad = grad_refs[step - 1]
            columns = grad.shape[1]
            for index in range(grad.shape[0] // height):
                at = width + index * columns
                out[:, at : at + columns] = grad[index * height : (index + 1) * height, :]


def place_kernel(scale, steps, slots, tables, bals, unit, scalar_ref, *refs):
    pieces = refs[: len(steps)]
    in_ref, out_ref, scaled_ref, sems = refs[-4:]
    _, group_here, table_here = Scalars(scalar_ref, 0, bals, slots).place()
    features = in_ref.shape[1]
    copies = []
    for number, (group_step, piece) in enumerate(zip(steps, pieces)):
        for table_step in range(tables):
            index = number * tables + table_step
            at = index * unit
            from_rows = slice(table_step * unit, (table_step + 1) * unit)
            scaled_ref[at : at + unit, :] = piece[from_rows, :].astype(f32) * scale
            owner = (group_here ^ group_step) * tables + (table_here ^ table_step)
            to = pl.ds(pl.multiple_of(owner * unit, unit), unit)
            rows = scaled_ref.at[pl.ds(at, unit), :]
            sem = sems.at[index]
            copies.append(
                pltpu.make_async_copy(rows.at[:, pl.ds(0, features)], in_ref.at[to, :], sem.at[0])
            )
            copies.append(
                pltpu.make_async_copy(
                    rows.at[:, pl.ds(features, out_ref.shape[1])], out_ref.at[to, :], sem.at[1]
                )
            )
            copies[-2].start()
            copies[-1].start()
    for copy in copies:
        copy.wait()


def sum_rounded(terms):
    total = terms[0].astype(f32)
    for term in terms[1:]:
        total = total + term.astype(f32)
    return total.astype(bf16)


def after(value, *others):
    return lax.optimization_barrier((value,) + others)[0]


def on_device(
    item_ids, seq_lengths, surplus_slot, helper_map, embed_tables, weight_in, weight_out, cotangent
):
    bal = lax.axis_index("bal")
    emb = lax.axis_index("emb")
    bals = lax.axis_size("bal")
    embs = lax.axis_size("emb")
    tables = item_ids.shape[2]
    groups = embs // tables
    _, rows, width = cotangent.shape
    slots = seq_lengths.shape[2]
    slot_rows = rows // slots
    distinct, columns = embed_tables.shape[1:]
    part = distinct // bals
    weight_part = weight_in.shape[0]
    table_here = emb // groups
    group_here = emb % groups
    width, features = weight_out.shape[1], weight_in.shape[1]
    unit = weight_part // embs
    owned = unit % 16 == 0
    unit = unit if owned else 0
    first = bals * (2 + slots)
    lane = lax.broadcasted_iota(jnp.int32, (1, LANES), 1)
    scalars = jnp.where(lane == first, bal, 0)
    scalars = jnp.where(lane == first + 1, group_here, scalars)
    scalars = jnp.where(lane == first + 2, table_here, scalars)
    fields = [surplus_slot.T, helper_map.T] + [seq_lengths[index] for index in range(bals)]
    at = 0
    for field in fields:
        width_here = field.shape[1]
        scalars = scalars + jnp.pad(field, ((0, 0), (at, LANES - at - width_here)))
        at += width_here

    share = lax.dynamic_slice_in_dim(embed_tables[0], bal * part, part, 0)
    fetched = [emb_swap(share, step * groups, embs) for step in range(1, tables)]

    ids = lax.dynamic_slice_in_dim(
        jnp.transpose(after(item_ids[0], share)), table_here * groups * rows, groups * rows, 1
    )
    plane_ids = with_swapped(ids.reshape(tables, groups * slots, 1, slot_rows), bals)
    wide_cot = cotangent[0].astype(f32)
    scalars = after(scalars, share, wide_cot)
    for bit in range((groups - 1).bit_length()):
        scalars = jnp.concatenate([scalars, emb_swap(scalars, 1 << bit, embs)], axis=0)

    fetched[0] = after(fetched[0], scalars)
    pieces = [piece for one in [share] + fetched for piece in with_swapped(one, bals)]

    found = pl.pallas_call(
        functools.partial(lookup_kernel, groups, slots, tables, bals),
        out_shape=[jax.ShapeDtypeStruct((rows, columns), bf16)] * groups,
        in_specs=[SMEM] + [VMEM] * (bals + len(pieces)),
        out_specs=[VMEM] * groups,
        cost_estimate=estimate(3),
        compiler_params=room(16),
    )(scalars, *plane_ids, *pieces)
    weights = jnp.concatenate([weight_in, weight_out], axis=1)
    weights = with_swapped(after(weights, found[0]), bals)
    block = [found[0]] + [emb_swap(found[step], step, embs) for step in range(1, groups)]

    pairs = slots * HEADS // 2
    terms = jax.ShapeDtypeStruct((weight_part, features + width), bf16)
    results = pl.pallas_call(
        functools.partial(layer_kernel, groups, slots, tables, bals, unit),
        out_shape=[jax.ShapeDtypeStruct((rows, width), bf16)]
        + [jax.ShapeDtypeStruct((rows, columns), bf16)] * groups
        + [terms] * bals,
        in_specs=[SMEM] + [VMEM] * (groups + bals + 1),
        out_specs=[VMEM] * (1 + groups + bals),
        scratch_shapes=[
            pltpu.VMEM((groups, rows, columns), bf16),
            pltpu.VMEM((bals, rows, weight_part), bf16),
            pltpu.VMEM((bals, rows, weight_part), f32),
            pltpu.VMEM((width, rows), bf16),
            pltpu.VMEM((width, rows), bf16),
            pltpu.VMEM((pairs, 2 * slot_rows, slot_rows), bf16),
            pltpu.VMEM((pairs, 2 * slot_rows, slot_rows), f32),
            pltpu.VMEM((rows, width), f32),
            pltpu.VMEM((rows, features - width), bf16),
            pltpu.VMEM((rows, features), f32),
            pltpu.VMEM((rows, features), bf16),
        ],
        cost_estimate=estimate(7),
        compiler_params=room(36),
    )(scalars, *block[::-1], *weights, wide_cot)
    layer_out, results = results[0], results[1:]
    grads, results = results[:groups], results[groups:]

    def over_cores(parts):
        return sum_rounded([parts[0]] + [bal_swap(parts[turn], turn, bals) for turn in range(1, bals)])

    def to_plane(value):
        return [value] + [emb_swap(value, step, embs) for step in range(1, groups)]

    def table_sums(plane_grads):
        return pl.pallas_call(
            functools.partial(scatter_kernel, groups, slots, bals),
            out_shape=[jax.ShapeDtypeStruct((tables, part, columns), bf16)] * bals,
            in_specs=[SMEM] + [VMEM] * (bals + groups),
            out_specs=[VMEM] * bals,
            cost_estimate=estimate(3),
            compiler_params=room(16),
        )(scalars, *plane_ids, *plane_grads[::-1])

    grad_scale = (rows * embs * bals) ** -0.5
    if owned:
        height, wide = weight_part // groups, features + width
        terms = [results[0]] + [bal_swap(results[turn], turn, bals) for turn in range(1, bals)]
        pieces = pl.pallas_call(
            functools.partial(pieces_kernel, bals),
            out_shape=[jax.ShapeDtypeStruct((height, wide), bf16)]
            + [jax.ShapeDtypeStruct((height, wide + rows // height * columns), bf16)] * (groups - 1),
            in_specs=[VMEM] * (bals + groups - 1),
            out_specs=[VMEM] * groups,
            compiler_params=room(12),
        )(*terms, *grads[1:])
        came = [emb_swap(pieces[step], step, embs) for step in range(1, groups)]
        mine = sum_rounded([value[:, :wide] for value in came[::-1]] + [pieces[0]])
        mine = mine.reshape(tables, unit, wide)
        sums = table_sums([grads[0]] + came)
        own_sums = over_cores(sums)
        came = [emb_swap(mine[step], step * groups, embs) for step in range(1, tables)]
        final = sum_rounded(came[-1:] + came[:-1] + [mine[0]])
        gathered = [final] + [emb_swap(final, step * groups, embs) for step in range(1, tables)]
        back = to_plane(jnp.concatenate(gathered, axis=0))
        later = after(own_sums, *gathered[1:])
        swapped = [emb_swap(later[step], step * groups, embs) for step in range(1, tables)]
        swapped = [after(value, *back[1:]) for value in swapped]
    else:
        sums = table_sums([grads[0]] + [emb_swap(grads[step], step, embs) for step in range(1, groups)])
        own_sums = over_cores(sums)
        swapped = [emb_swap(own_sums[step], step * groups, embs) for step in range(1, tables)]
    table_sum = swapped[-1].astype(f32)
    for value in swapped[:-1] + [own_sums[0]]:
        table_sum = table_sum + value.astype(f32)
    table_scale = (distinct / (bals * item_ids.shape[1])) ** 0.5

    if owned:
        totals = []
        for steps in ([0] + list(range(groups - 1, 1, -1))[: groups // 2 - 1], None):
            steps = steps or [step for step in range(1, groups) if step not in done]
            done = steps
            totals = pl.pallas_call(
                functools.partial(place_kernel, grad_scale, steps, slots, tables, bals, unit),
                out_shape=[
                    jax.ShapeDtypeStruct((weight_part, features), f32),
                    jax.ShapeDtypeStruct((weight_part, width), f32),
                ],
                in_specs=[SMEM] + [VMEM] * len(steps) + [HBM] * len(totals),
                out_specs=[HBM] * 2,
                scratch_shapes=[
                    pltpu.VMEM((len(steps) * tables * unit, features + width), f32),
                    pltpu.SemaphoreType.DMA((len(steps) * tables, 2)),
                ],
                input_output_aliases={1 + len(steps) + index: index for index in range(len(totals))},
                cost_estimate=estimate(1),
                compiler_params=room(12),
            )(after(scalars, table_sum) if totals else scalars, *[back[step] for step in steps], *totals)
        total_in, total_out = totals
    else:
        total = lax.psum(over_cores(results).astype(f32), "emb") * grad_scale
        total_in, total_out = total[:, :features], total[:, features:]

    return layer_out[None], (table_sum * table_scale)[None], total_in, total_out


def solution(mesh):
    placed = (
        P("bal", None, None),
        P(None, "emb", None),
        P(None, "emb"),
        P(None, "emb"),
        P("emb", None, None),
        P("bal", None),
        P("bal", None),
        P("bal", "emb", None),
    )
    return jax.shard_map(
        on_device,
        mesh=mesh,
        in_specs=placed,
        out_specs=(P("bal", "emb", None), P("emb", "bal", None), P("bal", None), P("bal", None)),
        check_vma=False,
    )
```

```python
import functools

import jax
import jax.numpy as jnp
from jax import lax
from jax.experimental import pallas as pl
from jax.experimental.pallas import tpu as pltpu
from jax.sharding import PartitionSpec as P

HEADS = 8
EPS = 1e-05
LANES = 128

VMEM = pl.BlockSpec(memory_space=pltpu.VMEM)
SMEM = pl.BlockSpec(memory_space=pltpu.SMEM)
HBM = pl.BlockSpec(memory_space=pltpu.HBM)
f32 = jnp.float32
bf16 = jnp.bfloat16


def room(mib):
    return pltpu.CompilerParams(vmem_limit_bytes=mib * 1024 * 1024)


def estimate(microseconds):
    return pl.CostEstimate(flops=0, bytes_accessed=microseconds * 3_500_000, transcendentals=0)


def matmul(left, right):
    return lax.dot_general(left, right, (((1,), (0,)), ((), ())), preferred_element_type=f32)


def matmul_nt(left, right):
    return lax.dot_general(left, right, (((1,), (1,)), ((), ())), preferred_element_type=f32)


def matmul_tn(left, right):
    return lax.dot_general(left, right, (((0,), (0,)), ((), ())), preferred_element_type=f32)


def sigmoid(value):
    return 0.5 * jnp.tanh(0.5 * value) + 0.5


def bal_swap(value, step, count):
    return lax.ppermute(value, "bal", [(i, i ^ step) for i in range(count)])


def with_swapped(value, count):
    return [value] + [bal_swap(value, turn, count) for turn in range(1, count)]


def emb_swap(value, step, count):
    return lax.ppermute(value, "emb", [(i, i ^ step) for i in range(count)])


class Scalars:
    def __init__(self, ref, step, bals, slots):
        self.ref, self.step, self.bals, self.slots = ref, step, bals, slots

    def surplus(self, bal):
        return self.ref[self.step, bal]

    def source(self, bal):
        found = jnp.int32(0)
        for index in range(self.bals):
            found = found + jnp.where(self.ref[self.step, self.bals + index] == bal, index, 0)
        return found

    def length(self, bal, slot):
        return self.ref[self.step, 2 * self.bals + bal * self.slots + slot]

    def place(self):
        first = self.bals * (2 + self.slots)
        return self.ref[self.step, first], self.ref[self.step, first + 1], self.ref[self.step, first + 2]


def pick_ids(scalars, ids_refs, slots, tables):
    bal, group_here, _ = scalars[0].place()
    found = []
    for step, there in enumerate(scalars):
        group = group_here ^ step
        my_slot = there.surplus(bal)
        source = there.source(bal)
        from_slot = there.surplus(source)
        by_slot = [[] for _ in range(slots)]
        for table in tables:
            arrived = ids_refs[0][table, group * slots + from_slot]
            for turn in range(1, len(ids_refs)):
                other = ids_refs[turn][table, group * slots + from_slot]
                arrived = jnp.where(source ^ bal == turn, other, arrived)
            for slot in range(slots):
                own = ids_refs[0][table, group * slots + slot]
                by_slot[slot].append(jnp.where(my_slot == slot, arrived, own))
        found.append(by_slot)
    return found


def table_order(table_here, tables):
    return [table_here ^ step for step in range(tables)]


def lookup_kernel(groups, slots, tables, bals, *refs):
    refs = list(refs)
    take = lambda count: [refs.pop(0) for _ in range(count)]
    (scalar_ref,) = take(1)
    scalars = [Scalars(scalar_ref, step, bals, slots) for step in range(groups)]
    ids_refs = take(bals)
    pieces = [take(bals) for _ in range(tables)]
    out_refs = refs
    bal, _, table_here = scalars[0].place()
    part, columns = pieces[0][0].shape
    slot_rows = ids_refs[0].shape[3]
    lane = lax.broadcasted_iota(jnp.int32, (LANES, LANES), 1)
    ids = pick_ids(scalars, ids_refs, slots, table_order(table_here, tables))
    rows = out_refs[0].shape[0]
    total = jnp.zeros((groups * rows, columns), f32)
    for table in range(tables):
        found = []
        for group in range(groups):
            for slot in range(slots):
                for first in range(0, slot_rows, LANES):
                    row = ids[group][slot][table][:, first : first + LANES]
                    found.append(jnp.transpose(jnp.broadcast_to(row, (LANES, LANES))))
        column = jnp.concatenate(found, axis=0)
        for turn, ref in enumerate(pieces[table]):
            shifted = column - (bal ^ turn) * part
            hot = []
            for at in range(0, part, LANES):
                here = [shifted[row : row + LANES] == lane + at for row in range(0, groups * rows, LANES)]
                here = [jnp.where(one, 1.0, 0.0).astype(bf16) for one in here]
                hot.append(jnp.concatenate(here, axis=0))
            total = total + matmul(jnp.concatenate(hot, axis=1), ref[...])
    for group in range(groups):
        out_refs[group][...] = total[group * rows : (group + 1) * rows].astype(bf16)


def scatter_kernel(groups, slots, bals, waits, *refs):
    refs = list(refs)
    take = lambda count: [refs.pop(0) for _ in range(count)]
    (scalar_ref,) = take(1)
    scalars = [Scalars(scalar_ref, step, bals, slots) for step in range(groups)]
    ids_refs, grad_refs, _, out_refs = take(bals), take(groups)[::-1], take(waits), refs
    bal, _, table_here = scalars[0].place()
    tables, part, _ = out_refs[0].shape
    slot_rows = ids_refs[0].shape[3]
    height = min(part, 256)
    iota = lax.broadcasted_iota(jnp.int32, (height, slot_rows), 0)
    ids = pick_ids(scalars, ids_refs, slots, table_order(table_here, tables))
    columns = out_refs[0].shape[2]

    def rows_of(ref):
        height = ref.shape[0]
        first = ref.shape[1] - slots * slot_rows // height * columns
        return [ref[:, at : at + columns] for at in range(first, ref.shape[1], columns)]

    grads = jnp.concatenate([piece for ref in grad_refs for piece in rows_of(ref)], axis=0)
    for table in range(tables):
        for turn in range(bals):
            for at in range(0, part, height):
                start = (bal ^ turn) * part + at
                hot = jnp.concatenate(
                    [
                        jnp.where(iota == ids[group][slot][table] - start, 1.0, 0.0).astype(bf16)
                        for group in range(groups)
                        for slot in range(slots)
                    ],
                    axis=1,
                )
                out_refs[turn][table, at : at + height, :] = matmul(hot, grads).astype(bf16)


def norm(values):
    average = jnp.mean(values, axis=1, keepdims=True)
    centred = values - average
    inverse = lax.rsqrt(jnp.mean(centred * centred, axis=1, keepdims=True) + EPS)
    return centred * inverse, inverse


def norm_back(incoming, normed, inverse):
    first = jnp.mean(incoming, axis=1, keepdims=True)
    second = jnp.mean(incoming * normed, axis=1, keepdims=True)
    return inverse * (incoming - first - normed * second)


def layer_kernel(groups, slots, tables, bals, unit, scalar_ref, *refs):
    refs = list(refs)
    take = lambda count: [refs.pop(0) for _ in range(count)]
    block_refs = take(groups)[::-1]
    weight_refs = take(bals)
    (cot_ref,) = take(1)
    (layer_ref,) = take(1)
    grad_refs = take(groups)
    term_refs = take(bals)
    (x_ref, halves_ref, wide_ref, nt_ref, mt_ref, weights_ref, slope_ref, gate_ref, heads_ref, dsilu_ref, grads_ref) = refs

    scalars = Scalars(scalar_ref, 0, bals, slots)
    bal, group_here, table_here = scalars.place()
    rows, width = cot_ref.shape
    slot_rows = rows // slots
    head_width = width // HEADS
    score_scale = head_width**-0.5
    piece = block_refs[0].shape[1]
    part, features = weight_refs[0].shape[0], weight_refs[0].shape[1] - width

    def times_parts(value, first, last):
        for index in range(bals):
            halves_ref[index] = value[:, index * part : (index + 1) * part]
        found = matmul(halves_ref[bal], weight_refs[0][:, first:last])
        for turn in range(1, bals):
            found = found + matmul(halves_ref[bal ^ turn], weight_refs[turn][:, first:last])
        return found

    def times_parts_nt(value, first, last):
        for turn in range(bals):
            wide_ref[bal ^ turn] = matmul_nt(value, weight_refs[turn][:, first:last])
        return jnp.concatenate([wide_ref[index] for index in range(bals)], axis=1)

    my_slot = scalars.surplus(bal)
    source = scalars.source(bal)
    moved = scalars.length(source, scalars.surplus(source))
    lengths = [jnp.where(my_slot == slot, moved, scalars.length(bal, slot)) for slot in range(slots)]

    for step in range(groups):
        x_ref[group_here ^ step] = block_refs[step][...]
    x = jnp.concatenate([x_ref[group] for group in range(groups)], axis=1).astype(f32)
    normed_in, in_inverse = norm(x)
    nt_ref[...] = jnp.transpose(normed_in).astype(bf16)
    projected = times_parts(normed_in.astype(bf16), 0, features)
    logistic = sigmoid(projected)
    active = projected * logistic
    dsilu_ref[...] = logistic + active * (1.0 - logistic)
    gate_ref[...] = active[:, :width]
    heads_ref[...] = active[:, width:].astype(bf16)

    pair_width = 2 * head_width
    low = lax.broadcasted_iota(jnp.int32, (slot_rows, pair_width), 1) < head_width
    row_at = lax.broadcasted_iota(jnp.int32, (slot_rows, slot_rows), 0)
    col_at = lax.broadcasted_iota(jnp.int32, (slot_rows, slot_rows), 1)

    def split(value):
        zero = jnp.zeros_like(value)
        return jnp.concatenate([jnp.where(low, value, zero), jnp.where(low, zero, value)], axis=0)

    def side_by_side(value):
        return jnp.concatenate([value[:slot_rows], value[slot_rows:]], axis=1)

    def part_of(slot, pair, which):
        first = which * width + pair * pair_width
        return heads_ref[slot * slot_rows : (slot + 1) * slot_rows, first : first + pair_width]

    pairs = HEADS // 2
    attended = []
    for slot in range(slots):
        live = (col_at <= row_at) & (row_at < lengths[slot])
        allowed = jnp.where(live, 1.0 / slot_rows, 0.0)
        allowed = jnp.concatenate([allowed, allowed], axis=0)
        across = []
        for pair in range(pairs):
            value, query, key = (part_of(slot, pair, which) for which in range(3))
            scores = matmul_nt(split(query), key) * score_scale
            q = sigmoid(scores)
            sq = scores * q
            weights = (sq * allowed).astype(bf16)
            weights_ref[slot * pairs + pair] = weights
            slope_ref[slot * pairs + pair] = allowed * (q + sq * (1.0 - q))
            across.append(matmul(side_by_side(weights), split(value)))
        attended.append(jnp.concatenate(across, axis=1))
    normed_out, out_inverse = norm(jnp.concatenate(attended, axis=0))
    gate = gate_ref[...]
    mixed = normed_out * gate
    mt_ref[...] = jnp.transpose(mixed).astype(bf16)
    layer_ref[...] = (x + times_parts(mixed.astype(bf16), features, features + width)).astype(bf16)

    wide_cot = cot_ref[...]
    cot = wide_cot.astype(bf16)
    grad_mixed = times_parts_nt(cot, features, features + width)
    grad_attended = norm_back(grad_mixed * gate, normed_out, out_inverse).astype(bf16)
    grads_ref[:, :width] = (grad_mixed * normed_out * dsilu_ref[:, :width]).astype(bf16)

    def owner_order(ref, turn):
        start = (bal ^ turn) * part
        if part != groups * tables * unit:
            return ref[pl.ds(pl.multiple_of(start, part), part), :]
        found = []
        for group_step in range(groups):
            for table_step in range(tables):
                owner = (group_here ^ group_step) * tables + (table_here ^ table_step)
                at = pl.multiple_of(start + owner * unit, unit)
                found.append(ref[pl.ds(at, unit), :])
        return jnp.concatenate(found, axis=0)

    def emit_terms(ref, right, first):
        left = jnp.concatenate([owner_order(ref, turn) for turn in range(bals)], axis=0)
        found = matmul(left, right).astype(bf16)
        for turn in range(bals):
            rows_here = slice(turn * part, (turn + 1) * part)
            term_refs[turn][:, first : first + right.shape[1]] = found[rows_here]

    emit_terms(mt_ref, cot, features)

    for slot in range(slots):
        here = slice(slot * slot_rows, (slot + 1) * slot_rows)
        for pair in range(pairs):
            value, query, key = (part_of(slot, pair, which) for which in range(3))
            lanes = slice(pair * pair_width, (pair + 1) * pair_width)
            upper = split(grad_attended[here, lanes])
            grad_weights = matmul_nt(upper, value)
            grad_scores = (grad_weights * slope_ref[slot * pairs + pair]).astype(bf16)
            grad_value = matmul_tn(weights_ref[slot * pairs + pair], upper)
            grad_query = matmul(side_by_side(grad_scores), split(key)) * score_scale
            grad_key = matmul_tn(grad_scores, split(query)) * score_scale
            for which, found in enumerate((grad_value, grad_query, grad_key)):
                first = (1 + which) * width + pair * pair_width
                at = slice(first, first + pair_width)
                grads_ref[here, at] = (found * dsilu_ref[here, at]).astype(bf16)

    emit_terms(nt_ref, grads_ref[...], 0)

    grad_normed = times_parts_nt(grads_ref[...], 0, features)
    grad_rows = (wide_cot + norm_back(grad_normed, normed_in, in_inverse)).astype(bf16)
    for group in range(groups):
        x_ref[group] = grad_rows[:, group * piece : (group + 1) * piece]
    for step in range(groups):
        grad_refs[step][...] = x_ref[group_here ^ step]


def pieces_kernel(tables, groups, bals, *refs):
    term_refs, grad_refs = refs[:bals], refs[bals : bals + groups - 1]
    plane_refs = refs[bals + groups - 1 : bals + 2 * groups - 1]
    table_refs = refs[bals + 2 * groups - 1 :]
    height, width = plane_refs[0].shape
    unit = height // tables

    def total(rows, columns):
        found = term_refs[0][rows, columns].astype(f32)
        for ref in term_refs[1:]:
            found = found + ref[rows, columns].astype(f32)
        return found.astype(bf16)

    for step, out in enumerate(plane_refs):
        rows = slice(step * height, (step + 1) * height)
        out[:, :width] = total(rows, slice(0, width))
        if step:
            grad = grad_refs[step - 1]
            columns = grad.shape[1]
            for index in range(grad.shape[0] // height):
                at = width + index * columns
                out[:, at : at + columns] = grad[index * height : (index + 1) * height, :]
    for table_step, out in enumerate(table_refs):
        for step in range(groups):
            first = step * height + table_step * unit
            rows = slice(first, first + unit)
            columns = slice(width, width + out.shape[1])
            out[step * unit : (step + 1) * unit, :] = total(rows, columns)


def ordered(plane, table, first):
    rest = [("plane", step) for step in plane] + [("table", step) for step in table]
    rest.remove(first)
    rest.sort(key=lambda one: (-one[1], one[0] if first[0] == "table" else one[0] != "table"))
    return [first] + rest


def first_sums_kernel(order, tables, groups, plane_ref, table_ref, *refs):
    came, outs = refs[: len(order)], refs[len(order) :]
    unit, width = outs[0].shape
    plane, table = plane_ref[...].astype(f32), table_ref[...].astype(f32)
    for (kind, _), ref in zip(order, came):
        if kind == "plane":
            plane = plane + ref[:, :width].astype(f32)
        else:
            table = table + ref[...].astype(f32)
    for step in range(tables):
        outs[step][...] = plane[step * unit : (step + 1) * unit].astype(bf16)
    for step in range(groups):
        outs[tables + step][...] = table[step * unit : (step + 1) * unit].astype(bf16)


def second_sums_kernel(order, first_ref, last_ref, *refs):
    came, out = refs[:-1], refs[-1]
    width = first_ref.shape[1]
    first, last = first_ref[...].astype(f32), last_ref[...].astype(f32)
    for (kind, _), ref in zip(order, came):
        if kind == "table":
            first = first + ref[...].astype(f32)
        else:
            last = last + ref[...].astype(f32)
    out[:, :width] = first.astype(bf16)
    out[:, width:] = last.astype(bf16)


def place_kernel(scale, steps, slots, tables, bals, unit, scalar_ref, *refs):
    pieces = refs[: len(steps)]
    in_ref, out_ref, scaled_ref, sems = refs[-4:]
    _, group_here, table_here = Scalars(scalar_ref, 0, bals, slots).place()
    features = in_ref.shape[1]
    copies = []
    for number, (group_step, piece) in enumerate(zip(steps, pieces)):
        for table_step in range(tables):
            index = number * tables + table_step
            at = index * unit
            from_rows = slice(table_step * unit, (table_step + 1) * unit)
            scaled_ref[at : at + unit, :] = piece[from_rows, :].astype(f32) * scale
            owner = (group_here ^ group_step) * tables + (table_here ^ table_step)
            to = pl.ds(pl.multiple_of(owner * unit, unit), unit)
            rows = scaled_ref.at[pl.ds(at, unit), :]
            sem = sems.at[index]
            copies.append(
                pltpu.make_async_copy(rows.at[:, pl.ds(0, features)], in_ref.at[to, :], sem.at[0])
            )
            copies.append(
                pltpu.make_async_copy(
                    rows.at[:, pl.ds(features, out_ref.shape[1])], out_ref.at[to, :], sem.at[1]
                )
            )
            copies[-2].start()
            copies[-1].start()
    for copy in copies:
        copy.wait()


def sum_rounded(terms):
    total = terms[0].astype(f32)
    for term in terms[1:]:
        total = total + term.astype(f32)
    return total.astype(bf16)


def after(value, *others):
    return lax.optimization_barrier((value,) + others)[0]


def on_device(
    item_ids, seq_lengths, surplus_slot, helper_map, embed_tables, weight_in, weight_out, cotangent
):
    bal = lax.axis_index("bal")
    emb = lax.axis_index("emb")
    bals = lax.axis_size("bal")
    embs = lax.axis_size("emb")
    tables = item_ids.shape[2]
    groups = embs // tables
    _, rows, width = cotangent.shape
    slots = seq_lengths.shape[2]
    slot_rows = rows // slots
    distinct, columns = embed_tables.shape[1:]
    part = distinct // bals
    weight_part = weight_in.shape[0]
    table_here = emb // groups
    group_here = emb % groups
    width, features = weight_out.shape[1], weight_in.shape[1]
    unit = weight_part // embs
    owned = unit % 16 == 0
    unit = unit if owned else 0
    first = bals * (2 + slots)
    lane = lax.broadcasted_iota(jnp.int32, (1, LANES), 1)
    scalars = jnp.where(lane == first, bal, 0)
    scalars = jnp.where(lane == first + 1, group_here, scalars)
    scalars = jnp.where(lane == first + 2, table_here, scalars)
    fields = [surplus_slot.T, helper_map.T] + [seq_lengths[index] for index in range(bals)]
    at = 0
    for field in fields:
        width_here = field.shape[1]
        scalars = scalars + jnp.pad(field, ((0, 0), (at, LANES - at - width_here)))
        at += width_here

    plane_steps, table_steps = range(1, groups), range(1, tables)
    share = lax.dynamic_slice_in_dim(embed_tables[0], bal * part, part, 0)
    fetched = [emb_swap(share, step * groups, embs) for step in range(1, tables)]

    ids = lax.dynamic_slice_in_dim(
        jnp.transpose(after(item_ids[0], share)), table_here * groups * rows, groups * rows, 1
    )
    plane_ids = with_swapped(ids.reshape(tables, groups * slots, 1, slot_rows), bals)
    wide_cot = cotangent[0].astype(f32)
    scalars = after(scalars, share, wide_cot)
    for bit in range((groups - 1).bit_length()):
        scalars = jnp.concatenate([scalars, emb_swap(scalars, 1 << bit, embs)], axis=0)

    fetched[0] = after(fetched[0], scalars)
    pieces = [piece for one in [share] + fetched for piece in with_swapped(one, bals)]

    found = pl.pallas_call(
        functools.partial(lookup_kernel, groups, slots, tables, bals),
        out_shape=[jax.ShapeDtypeStruct((rows, columns), bf16)] * groups,
        in_specs=[SMEM] + [VMEM] * (bals + len(pieces)),
        out_specs=[VMEM] * groups,
        cost_estimate=estimate(3),
        compiler_params=room(16),
    )(scalars, *plane_ids, *pieces)
    weights = jnp.concatenate([weight_in, weight_out], axis=1)
    weights = with_swapped(after(weights, found[0]), bals)
    block = [found[0]] + [emb_swap(found[step], step, embs) for step in range(1, groups)]

    pairs = slots * HEADS // 2
    terms = jax.ShapeDtypeStruct((weight_part, features + width), bf16)
    results = pl.pallas_call(
        functools.partial(layer_kernel, groups, slots, tables, bals, unit),
        out_shape=[jax.ShapeDtypeStruct((rows, width), bf16)]
        + [jax.ShapeDtypeStruct((rows, columns), bf16)] * groups
        + [terms] * bals,
        in_specs=[SMEM] + [VMEM] * (groups + bals + 1),
        out_specs=[VMEM] * (1 + groups + bals),
        scratch_shapes=[
            pltpu.VMEM((groups, rows, columns), bf16),
            pltpu.VMEM((bals, rows, weight_part), bf16),
            pltpu.VMEM((bals, rows, weight_part), f32),
            pltpu.VMEM((width, rows), bf16),
            pltpu.VMEM((width, rows), bf16),
            pltpu.VMEM((pairs, 2 * slot_rows, slot_rows), bf16),
            pltpu.VMEM((pairs, 2 * slot_rows, slot_rows), f32),
            pltpu.VMEM((rows, width), f32),
            pltpu.VMEM((rows, features - width), bf16),
            pltpu.VMEM((rows, features), f32),
            pltpu.VMEM((rows, features), bf16),
        ],
        cost_estimate=estimate(7),
        compiler_params=room(36),
    )(scalars, *block[::-1], *weights, wide_cot)
    layer_out, results = results[0], results[1:]
    grads, results = results[:groups], results[groups:]

    def over_cores(parts):
        return sum_rounded([parts[0]] + [bal_swap(parts[turn], turn, bals) for turn in range(1, bals)])

    def to_plane(value):
        return [value] + [emb_swap(value, step, embs) for step in range(1, groups)]

    def table_sums(plane_grads, *others):
        return pl.pallas_call(
            functools.partial(scatter_kernel, groups, slots, bals, len(others)),
            out_shape=[jax.ShapeDtypeStruct((tables, part, columns), bf16)] * bals,
            in_specs=[SMEM] + [VMEM] * (bals + groups) + [HBM] * len(others),
            out_specs=[VMEM] * bals,
            cost_estimate=estimate(3),
            compiler_params=room(16),
        )(scalars, *plane_ids, *plane_grads[::-1], *others)

    grad_scale = (rows * embs * bals) ** -0.5
    if owned:
        height, wide = weight_part // groups, features + width
        terms = [results[0]] + [bal_swap(results[turn], turn, bals) for turn in range(1, bals)]
        last = 2 * width
        first = wide - last
        shape = lambda *dims: jax.ShapeDtypeStruct(dims, bf16)
        pieces = pl.pallas_call(
            functools.partial(pieces_kernel, tables, groups, bals),
            out_shape=[shape(height, first)]
            + [shape(height, first + rows // height * columns)] * (groups - 1)
            + [shape(height, last)] * tables,
            in_specs=[VMEM] * (bals + groups - 1),
            out_specs=[VMEM] * (groups + tables),
            compiler_params=room(12),
        )(*terms, *grads[1:])
        plane_pieces, table_pieces = pieces[:groups], pieces[groups:]
        order = ordered(plane_steps, table_steps, ("table", 1))
        came = {("plane", step): emb_swap(plane_pieces[step], step, embs) for step in plane_steps}
        for step in table_steps:
            came["table", step] = emb_swap(table_pieces[step], step * groups, embs)
        mine = pl.pallas_call(
            functools.partial(first_sums_kernel, order, tables, groups),
            out_shape=[shape(unit, first)] * tables + [shape(unit, last)] * groups,
            in_specs=[VMEM] * (2 + len(order)),
            out_specs=[VMEM] * (tables + groups),
            compiler_params=room(12),
        )(plane_pieces[0], table_pieces[0], *[came[one] for one in order])
        plane_grads = [grads[0]] + [came["plane", step] for step in range(1, groups)]
        order = ordered(plane_steps, table_steps, ("plane", 1))
        came = {("plane", step): emb_swap(mine[tables + step], step, embs) for step in plane_steps}
        for step in table_steps:
            came["table", step] = emb_swap(mine[step], step * groups, embs)
        final = pl.pallas_call(
            functools.partial(second_sums_kernel, order),
            out_shape=shape(unit, wide),
            in_specs=[VMEM] * (2 + len(order)),
            out_specs=VMEM,
            compiler_params=room(12),
        )(mine[0], mine[tables], *[came[one] for one in order])
        own_sums = over_cores(table_sums(plane_grads, final))
        gathered = [final] + [emb_swap(final, step * groups, embs) for step in range(1, tables)]
        back = to_plane(jnp.concatenate(gathered, axis=0))
        later = after(own_sums, *gathered[1:])
        swapped = [emb_swap(later[step], step * groups, embs) for step in range(1, tables)]
        swapped = [after(value, *back[1:]) for value in swapped]
    else:
        sums = table_sums([grads[0]] + [emb_swap(grads[step], step, embs) for step in range(1, groups)])
        own_sums = over_cores(sums)
        swapped = [emb_swap(own_sums[step], step * groups, embs) for step in range(1, tables)]
    table_sum = swapped[-1].astype(f32)
    for value in swapped[:-1] + [own_sums[0]]:
        table_sum = table_sum + value.astype(f32)
    table_scale = (distinct / (bals * item_ids.shape[1])) ** 0.5

    if owned:
        totals = []
        for steps in ([0] + list(range(groups - 1, 1, -1))[: groups // 2 - 1], None):
            steps = steps or [step for step in range(1, groups) if step not in done]
            done = steps
            totals = pl.pallas_call(
                functools.partial(place_kernel, grad_scale, steps, slots, tables, bals, unit),
                out_shape=[
                    jax.ShapeDtypeStruct((weight_part, features), f32),
                    jax.ShapeDtypeStruct((weight_part, width), f32),
                ],
                in_specs=[SMEM] + [VMEM] * len(steps) + [HBM] * len(totals),
                out_specs=[HBM] * 2,
                scratch_shapes=[
                    pltpu.VMEM((len(steps) * tables * unit, features + width), f32),
                    pltpu.SemaphoreType.DMA((len(steps) * tables, 2)),
                ],
                input_output_aliases={1 + len(steps) + index: index for index in range(len(totals))},
                cost_estimate=estimate(1),
                compiler_params=room(12),
            )(after(scalars, table_sum) if totals else scalars, *[back[step] for step in steps], *totals)
        total_in, total_out = totals
    else:
        total = lax.psum(over_cores(results).astype(f32), "emb") * grad_scale
        total_in, total_out = total[:, :features], total[:, features:]

    return layer_out[None], (table_sum * table_scale)[None], total_in, total_out


def solution(mesh):
    placed = (
        P("bal", None, None),
        P(None, "emb", None),
        P(None, "emb"),
        P(None, "emb"),
        P("emb", None, None),
        P("bal", None),
        P("bal", None),
        P("bal", "emb", None),
    )
    return jax.shard_map(
        on_device,
        mesh=mesh,
        in_specs=placed,
        out_specs=(P("bal", "emb", None), P("emb", "bal", None), P("bal", None), P("bal", None)),
        check_vma=False,
    )
```

```python
import functools

import jax
import jax.numpy as jnp
from jax import lax
from jax.experimental import pallas as pl
from jax.experimental.pallas import tpu as pltpu
from jax.sharding import PartitionSpec as P

HEADS = 8
EPS = 1e-05
LANES = 128

VMEM = pl.BlockSpec(memory_space=pltpu.VMEM)
SMEM = pl.BlockSpec(memory_space=pltpu.SMEM)
HBM = pl.BlockSpec(memory_space=pltpu.HBM)
f32 = jnp.float32
bf16 = jnp.bfloat16


def room(mib):
    return pltpu.CompilerParams(vmem_limit_bytes=mib * 1024 * 1024)


def estimate(microseconds):
    return pl.CostEstimate(flops=0, bytes_accessed=microseconds * 3_500_000, transcendentals=0)


def matmul(left, right):
    return lax.dot_general(left, right, (((1,), (0,)), ((), ())), preferred_element_type=f32)


def matmul_nt(left, right):
    return lax.dot_general(left, right, (((1,), (1,)), ((), ())), preferred_element_type=f32)


def matmul_tn(left, right):
    return lax.dot_general(left, right, (((0,), (0,)), ((), ())), preferred_element_type=f32)


def sigmoid(value):
    return 0.5 * jnp.tanh(0.5 * value) + 0.5


def bal_swap(value, step, count):
    return lax.ppermute(value, "bal", [(i, i ^ step) for i in range(count)])


def with_swapped(value, count):
    return [value] + [bal_swap(value, turn, count) for turn in range(1, count)]


def emb_swap(value, step, count):
    return lax.ppermute(value, "emb", [(i, i ^ step) for i in range(count)])


class Scalars:
    def __init__(self, ref, step, bals, slots):
        self.ref, self.step, self.bals, self.slots = ref, step, bals, slots

    def surplus(self, bal):
        return self.ref[self.step, bal]

    def source(self, bal):
        found = jnp.int32(0)
        for index in range(self.bals):
            found = found + jnp.where(self.ref[self.step, self.bals + index] == bal, index, 0)
        return found

    def length(self, bal, slot):
        return self.ref[self.step, 2 * self.bals + bal * self.slots + slot]

    def place(self):
        first = self.bals * (2 + self.slots)
        return self.ref[self.step, first], self.ref[self.step, first + 1], self.ref[self.step, first + 2]


def pick_ids(scalars, ids_refs, slots, tables):
    bal, group_here, _ = scalars[0].place()
    found = []
    for step, there in enumerate(scalars):
        group = group_here ^ step
        my_slot = there.surplus(bal)
        source = there.source(bal)
        from_slot = there.surplus(source)
        by_slot = [[] for _ in range(slots)]
        for table in tables:
            arrived = ids_refs[0][table, group * slots + from_slot]
            for turn in range(1, len(ids_refs)):
                other = ids_refs[turn][table, group * slots + from_slot]
                arrived = jnp.where(source ^ bal == turn, other, arrived)
            for slot in range(slots):
                own = ids_refs[0][table, group * slots + slot]
                by_slot[slot].append(jnp.where(my_slot == slot, arrived, own))
        found.append(by_slot)
    return found


def table_order(table_here, tables):
    return [table_here ^ step for step in range(tables)]


def lookup_kernel(groups, slots, tables, bals, *refs):
    refs = list(refs)
    take = lambda count: [refs.pop(0) for _ in range(count)]
    (scalar_ref,) = take(1)
    scalars = [Scalars(scalar_ref, step, bals, slots) for step in range(groups)]
    ids_refs = take(bals)
    pieces = [take(bals) for _ in range(tables)]
    out_refs = refs
    bal, _, table_here = scalars[0].place()
    part, columns = pieces[0][0].shape
    slot_rows = ids_refs[0].shape[3]
    lane = lax.broadcasted_iota(jnp.int32, (LANES, LANES), 1)
    ids = pick_ids(scalars, ids_refs, slots, table_order(table_here, tables))
    rows = out_refs[0].shape[0]
    total = jnp.zeros((groups * rows, columns), f32)
    for table in range(tables):
        found = []
        for group in range(groups):
            for slot in range(slots):
                for first in range(0, slot_rows, LANES):
                    row = ids[group][slot][table][:, first : first + LANES]
                    found.append(jnp.transpose(jnp.broadcast_to(row, (LANES, LANES))))
        column = jnp.concatenate(found, axis=0)
        for turn, ref in enumerate(pieces[table]):
            shifted = column - (bal ^ turn) * part
            hot = []
            for at in range(0, part, LANES):
                here = [shifted[row : row + LANES] == lane + at for row in range(0, groups * rows, LANES)]
                here = [jnp.where(one, 1.0, 0.0).astype(bf16) for one in here]
                hot.append(jnp.concatenate(here, axis=0))
            total = total + matmul(jnp.concatenate(hot, axis=1), ref[...])
    for group in range(groups):
        out_refs[group][...] = total[group * rows : (group + 1) * rows].astype(bf16)


def scatter_kernel(groups, slots, bals, *refs):
    refs = list(refs)
    take = lambda count: [refs.pop(0) for _ in range(count)]
    (scalar_ref,) = take(1)
    scalars = [Scalars(scalar_ref, step, bals, slots) for step in range(groups)]
    ids_refs, grad_refs, out_refs = take(bals), take(groups)[::-1], refs
    bal, _, table_here = scalars[0].place()
    tables, part, _ = out_refs[0].shape
    slot_rows = ids_refs[0].shape[3]
    height = min(part, 256)
    iota = lax.broadcasted_iota(jnp.int32, (height, slot_rows), 0)
    ids = pick_ids(scalars, ids_refs, slots, table_order(table_here, tables))
    columns = out_refs[0].shape[2]

    def rows_of(ref):
        height = ref.shape[0]
        first = ref.shape[1] - slots * slot_rows // height * columns
        return [ref[:, at : at + columns] for at in range(first, ref.shape[1], columns)]

    grads = jnp.concatenate([piece for ref in grad_refs for piece in rows_of(ref)], axis=0)
    for table in range(tables):
        for turn in range(bals):
            for at in range(0, part, height):
                start = (bal ^ turn) * part + at
                hot = jnp.concatenate(
                    [
                        jnp.where(iota == ids[group][slot][table] - start, 1.0, 0.0).astype(bf16)
                        for group in range(groups)
                        for slot in range(slots)
                    ],
                    axis=1,
                )
                out_refs[turn][table, at : at + height, :] = matmul(hot, grads).astype(bf16)


def norm(values):
    average = jnp.mean(values, axis=1, keepdims=True)
    centred = values - average
    inverse = lax.rsqrt(jnp.mean(centred * centred, axis=1, keepdims=True) + EPS)
    return centred * inverse, inverse


def norm_back(incoming, normed, inverse):
    first = jnp.mean(incoming, axis=1, keepdims=True)
    second = jnp.mean(incoming * normed, axis=1, keepdims=True)
    return inverse * (incoming - first - normed * second)


def times_parts_nt(value, weight_refs, first, last, bal, wide_ref):
    for turn, ref in enumerate(weight_refs):
        wide_ref[bal ^ turn] = matmul_nt(value, ref[:, first:last])
    return jnp.concatenate([wide_ref[index] for index in range(len(weight_refs))], axis=1)


def layer_kernel(groups, slots, tables, bals, unit, scalar_ref, *refs):
    refs = list(refs)
    take = lambda count: [refs.pop(0) for _ in range(count)]
    block_refs = take(groups)[::-1]
    weight_refs = take(bals)
    (cot_ref,) = take(1)
    (layer_ref,) = take(1)
    grads_ref, normed_ref, inverse_ref = take(3)
    term_refs = take(bals)
    (x_ref, halves_ref, wide_ref, nt_ref, mt_ref, weights_ref, slope_ref, gate_ref, heads_ref, dsilu_ref) = refs

    scalars = Scalars(scalar_ref, 0, bals, slots)
    bal, group_here, table_here = scalars.place()
    rows, width = cot_ref.shape
    slot_rows = rows // slots
    head_width = width // HEADS
    score_scale = head_width**-0.5
    piece = block_refs[0].shape[1]
    part, features = weight_refs[0].shape[0], weight_refs[0].shape[1] - width

    def times_parts(value, first, last):
        for index in range(bals):
            halves_ref[index] = value[:, index * part : (index + 1) * part]
        found = matmul(halves_ref[bal], weight_refs[0][:, first:last])
        for turn in range(1, bals):
            found = found + matmul(halves_ref[bal ^ turn], weight_refs[turn][:, first:last])
        return found

    my_slot = scalars.surplus(bal)
    source = scalars.source(bal)
    moved = scalars.length(source, scalars.surplus(source))
    lengths = [jnp.where(my_slot == slot, moved, scalars.length(bal, slot)) for slot in range(slots)]

    for step in range(groups):
        x_ref[group_here ^ step] = block_refs[step][...]
    x = jnp.concatenate([x_ref[group] for group in range(groups)], axis=1).astype(f32)
    normed_in, in_inverse = norm(x)
    normed_ref[...] = normed_in
    inverse_ref[...] = jnp.broadcast_to(in_inverse, inverse_ref.shape)
    nt_ref[...] = jnp.transpose(normed_in).astype(bf16)
    projected = times_parts(normed_in.astype(bf16), 0, features)
    logistic = sigmoid(projected)
    active = projected * logistic
    dsilu_ref[...] = logistic + active * (1.0 - logistic)
    gate_ref[...] = active[:, :width]
    heads_ref[...] = active[:, width:].astype(bf16)

    pair_width = 2 * head_width
    low = lax.broadcasted_iota(jnp.int32, (slot_rows, pair_width), 1) < head_width
    row_at = lax.broadcasted_iota(jnp.int32, (slot_rows, slot_rows), 0)
    col_at = lax.broadcasted_iota(jnp.int32, (slot_rows, slot_rows), 1)

    def split(value):
        zero = jnp.zeros_like(value)
        return jnp.concatenate([jnp.where(low, value, zero), jnp.where(low, zero, value)], axis=0)

    def side_by_side(value):
        return jnp.concatenate([value[:slot_rows], value[slot_rows:]], axis=1)

    def part_of(slot, pair, which):
        first = which * width + pair * pair_width
        return heads_ref[slot * slot_rows : (slot + 1) * slot_rows, first : first + pair_width]

    pairs = HEADS // 2
    attended = []
    for slot in range(slots):
        live = (col_at <= row_at) & (row_at < lengths[slot])
        allowed = jnp.where(live, 1.0 / slot_rows, 0.0)
        allowed = jnp.concatenate([allowed, allowed], axis=0)
        across = []
        for pair in range(pairs):
            value, query, key = (part_of(slot, pair, which) for which in range(3))
            scores = matmul_nt(split(query), key) * score_scale
            q = sigmoid(scores)
            sq = scores * q
            weights = (sq * allowed).astype(bf16)
            weights_ref[slot * pairs + pair] = weights
            slope_ref[slot * pairs + pair] = allowed * (q + sq * (1.0 - q))
            across.append(matmul(side_by_side(weights), split(value)))
        attended.append(jnp.concatenate(across, axis=1))
    normed_out, out_inverse = norm(jnp.concatenate(attended, axis=0))
    gate = gate_ref[...]
    mixed = normed_out * gate
    mt_ref[...] = jnp.transpose(mixed).astype(bf16)
    layer_ref[...] = (x + times_parts(mixed.astype(bf16), features, features + width)).astype(bf16)

    wide_cot = cot_ref[...]
    cot = wide_cot.astype(bf16)
    grad_mixed = times_parts_nt(cot, weight_refs, features, features + width, bal, wide_ref)
    grad_attended = norm_back(grad_mixed * gate, normed_out, out_inverse).astype(bf16)
    grads_ref[:, :width] = (grad_mixed * normed_out * dsilu_ref[:, :width]).astype(bf16)

    def owner_order(ref, turn):
        start = (bal ^ turn) * part
        if part != groups * tables * unit:
            return ref[pl.ds(pl.multiple_of(start, part), part), :]
        found = []
        for group_step in range(groups):
            for table_step in range(tables):
                owner = (group_here ^ group_step) * tables + (table_here ^ table_step)
                at = pl.multiple_of(start + owner * unit, unit)
                found.append(ref[pl.ds(at, unit), :])
        return jnp.concatenate(found, axis=0)

    def emit_terms(ref, right, first):
        left = jnp.concatenate([owner_order(ref, turn) for turn in range(bals)], axis=0)
        found = matmul(left, right).astype(bf16)
        for turn in range(bals):
            rows_here = slice(turn * part, (turn + 1) * part)
            term_refs[turn][:, first : first + right.shape[1]] = found[rows_here]

    emit_terms(mt_ref, cot, features)

    for slot in range(slots):
        here = slice(slot * slot_rows, (slot + 1) * slot_rows)
        for pair in range(pairs):
            value, query, key = (part_of(slot, pair, which) for which in range(3))
            lanes = slice(pair * pair_width, (pair + 1) * pair_width)
            upper = split(grad_attended[here, lanes])
            grad_weights = matmul_nt(upper, value)
            grad_scores = (grad_weights * slope_ref[slot * pairs + pair]).astype(bf16)
            grad_value = matmul_tn(weights_ref[slot * pairs + pair], upper)
            grad_query = matmul(side_by_side(grad_scores), split(key)) * score_scale
            grad_key = matmul_tn(grad_scores, split(query)) * score_scale
            for which, found in enumerate((grad_value, grad_query, grad_key)):
                first = (1 + which) * width + pair * pair_width
                at = slice(first, first + pair_width)
                grads_ref[here, at] = (found * dsilu_ref[here, at]).astype(bf16)

    emit_terms(nt_ref, grads_ref[...], 0)


def rows_kernel(groups, slots, bals, scalar_ref, *refs):
    refs = list(refs)
    take = lambda count: [refs.pop(0) for _ in range(count)]
    grads_ref, normed_ref, inverse_ref, cot_ref = take(4)
    weight_refs, grad_refs = take(bals), take(groups)
    x_ref, wide_ref = refs
    bal, group_here, _ = Scalars(scalar_ref, 0, bals, slots).place()
    features = grads_ref.shape[1]
    piece = grad_refs[0].shape[1]
    grad_normed = times_parts_nt(grads_ref[...], weight_refs, 0, features, bal, wide_ref)
    back = norm_back(grad_normed, normed_ref[...], inverse_ref[:, :1])
    grad_rows = (cot_ref[...] + back).astype(bf16)
    for group in range(groups):
        x_ref[group] = grad_rows[:, group * piece : (group + 1) * piece]
    for step in range(groups):
        grad_refs[step][...] = x_ref[group_here ^ step]


def pieces_kernel(bals, *refs):
    count = len(refs) - bals
    groups = (count + 1) // 2
    term_refs, grad_refs = refs[:bals], refs[bals : bals + groups - 1]
    out_refs = refs[bals + groups - 1 :]
    height, width = out_refs[0].shape
    for step, out in enumerate(out_refs):
        rows = slice(step * height, (step + 1) * height)
        total = term_refs[0][rows, :].astype(f32)
        for ref in term_refs[1:]:
            total = total + ref[rows, :].astype(f32)
        out[:, :width] = total.astype(bf16)
        if step:
            grad = grad_refs[step - 1]
            columns = grad.shape[1]
            for index in range(grad.shape[0] // height):
                at = width + index * columns
                out[:, at : at + columns] = grad[index * height : (index + 1) * height, :]


def place_kernel(scale, steps, slots, tables, bals, unit, scalar_ref, *refs):
    pieces = refs[: len(steps)]
    in_ref, out_ref, scaled_ref, sems = refs[-4:]
    _, group_here, table_here = Scalars(scalar_ref, 0, bals, slots).place()
    features = in_ref.shape[1]
    copies = []
    for number, (group_step, piece) in enumerate(zip(steps, pieces)):
        for table_step in range(tables):
            index = number * tables + table_step
            at = index * unit
            from_rows = slice(table_step * unit, (table_step + 1) * unit)
            scaled_ref[at : at + unit, :] = piece[from_rows, :].astype(f32) * scale
            owner = (group_here ^ group_step) * tables + (table_here ^ table_step)
            to = pl.ds(pl.multiple_of(owner * unit, unit), unit)
            rows = scaled_ref.at[pl.ds(at, unit), :]
            sem = sems.at[index]
            copies.append(
                pltpu.make_async_copy(rows.at[:, pl.ds(0, features)], in_ref.at[to, :], sem.at[0])
            )
            copies.append(
                pltpu.make_async_copy(
                    rows.at[:, pl.ds(features, out_ref.shape[1])], out_ref.at[to, :], sem.at[1]
                )
            )
            copies[-2].start()
            copies[-1].start()
    for copy in copies:
        copy.wait()


def sum_rounded(terms):
    total = terms[0].astype(f32)
    for term in terms[1:]:
        total = total + term.astype(f32)
    return total.astype(bf16)


def after(value, *others):
    return lax.optimization_barrier((value,) + others)[0]


def on_device(
    item_ids, seq_lengths, surplus_slot, helper_map, embed_tables, weight_in, weight_out, cotangent
):
    bal = lax.axis_index("bal")
    emb = lax.axis_index("emb")
    bals = lax.axis_size("bal")
    embs = lax.axis_size("emb")
    tables = item_ids.shape[2]
    groups = embs // tables
    _, rows, width = cotangent.shape
    slots = seq_lengths.shape[2]
    slot_rows = rows // slots
    distinct, columns = embed_tables.shape[1:]
    part = distinct // bals
    weight_part = weight_in.shape[0]
    table_here = emb // groups
    group_here = emb % groups
    width, features = weight_out.shape[1], weight_in.shape[1]
    unit = weight_part // embs
    owned = unit % 16 == 0
    unit = unit if owned else 0
    first = bals * (2 + slots)
    lane = lax.broadcasted_iota(jnp.int32, (1, LANES), 1)
    scalars = jnp.where(lane == first, bal, 0)
    scalars = jnp.where(lane == first + 1, group_here, scalars)
    scalars = jnp.where(lane == first + 2, table_here, scalars)
    fields = [surplus_slot.T, helper_map.T] + [seq_lengths[index] for index in range(bals)]
    at = 0
    for field in fields:
        width_here = field.shape[1]
        scalars = scalars + jnp.pad(field, ((0, 0), (at, LANES - at - width_here)))
        at += width_here

    share = lax.dynamic_slice_in_dim(embed_tables[0], bal * part, part, 0)
    fetched = [emb_swap(share, step * groups, embs) for step in range(1, tables)]

    ids = lax.dynamic_slice_in_dim(
        jnp.transpose(after(item_ids[0], share)), table_here * groups * rows, groups * rows, 1
    )
    plane_ids = with_swapped(ids.reshape(tables, groups * slots, 1, slot_rows), bals)
    wide_cot = cotangent[0].astype(f32)
    scalars = after(scalars, share, wide_cot)
    for bit in range((groups - 1).bit_length()):
        scalars = jnp.concatenate([scalars, emb_swap(scalars, 1 << bit, embs)], axis=0)

    fetched[0] = after(fetched[0], scalars)
    pieces = [piece for one in [share] + fetched for piece in with_swapped(one, bals)]

    found = pl.pallas_call(
        functools.partial(lookup_kernel, groups, slots, tables, bals),
        out_shape=[jax.ShapeDtypeStruct((rows, columns), bf16)] * groups,
        in_specs=[SMEM] + [VMEM] * (bals + len(pieces)),
        out_specs=[VMEM] * groups,
        cost_estimate=estimate(3),
        compiler_params=room(16),
    )(scalars, *plane_ids, *pieces)
    weights = jnp.concatenate([weight_in, weight_out], axis=1)
    weights = with_swapped(after(weights, found[0]), bals)
    block = [found[0]] + [emb_swap(found[step], step, embs) for step in range(1, groups)]

    pairs = slots * HEADS // 2
    terms = jax.ShapeDtypeStruct((weight_part, features + width), bf16)
    results = pl.pallas_call(
        functools.partial(layer_kernel, groups, slots, tables, bals, unit),
        out_shape=[jax.ShapeDtypeStruct((rows, width), bf16)]
        + [jax.ShapeDtypeStruct((rows, features), bf16)]
        + [jax.ShapeDtypeStruct((rows, columns_here), f32) for columns_here in (width, LANES)]
        + [terms] * bals,
        in_specs=[SMEM] + [VMEM] * (groups + bals + 1),
        out_specs=[VMEM] * (4 + bals),
        scratch_shapes=[
            pltpu.VMEM((groups, rows, columns), bf16),
            pltpu.VMEM((bals, rows, weight_part), bf16),
            pltpu.VMEM((bals, rows, weight_part), f32),
            pltpu.VMEM((width, rows), bf16),
            pltpu.VMEM((width, rows), bf16),
            pltpu.VMEM((pairs, 2 * slot_rows, slot_rows), bf16),
            pltpu.VMEM((pairs, 2 * slot_rows, slot_rows), f32),
            pltpu.VMEM((rows, width), f32),
            pltpu.VMEM((rows, features - width), bf16),
            pltpu.VMEM((rows, features), f32),
        ],
        cost_estimate=estimate(7),
        compiler_params=room(36),
    )(scalars, *block[::-1], *weights, wide_cot)
    layer_out, for_rows, results = results[0], results[1:4], results[4:]
    grads = pl.pallas_call(
        functools.partial(rows_kernel, groups, slots, bals),
        out_shape=[jax.ShapeDtypeStruct((rows, columns), bf16)] * groups,
        in_specs=[SMEM] + [VMEM] * (4 + bals),
        out_specs=[VMEM] * groups,
        scratch_shapes=[
            pltpu.VMEM((groups, rows, columns), bf16),
            pltpu.VMEM((bals, rows, weight_part), f32),
        ],
        cost_estimate=estimate(2),
        compiler_params=room(16),
    )(scalars, *for_rows, wide_cot, *weights)

    def over_cores(parts):
        return sum_rounded([parts[0]] + [bal_swap(parts[turn], turn, bals) for turn in range(1, bals)])

    def to_plane(value):
        return [value] + [emb_swap(value, step, embs) for step in range(1, groups)]

    def table_sums(plane_grads):
        return pl.pallas_call(
            functools.partial(scatter_kernel, groups, slots, bals),
            out_shape=[jax.ShapeDtypeStruct((tables, part, columns), bf16)] * bals,
            in_specs=[SMEM] + [VMEM] * (bals + groups),
            out_specs=[VMEM] * bals,
            cost_estimate=estimate(3),
            compiler_params=room(16),
        )(scalars, *plane_ids, *plane_grads[::-1])

    grad_scale = (rows * embs * bals) ** -0.5
    if owned:
        height, wide = weight_part // groups, features + width
        terms = [results[0]] + [bal_swap(results[turn], turn, bals) for turn in range(1, bals)]
        pieces = pl.pallas_call(
            functools.partial(pieces_kernel, bals),
            out_shape=[jax.ShapeDtypeStruct((height, wide), bf16)]
            + [jax.ShapeDtypeStruct((height, wide + rows // height * columns), bf16)] * (groups - 1),
            in_specs=[VMEM] * (bals + groups - 1),
            out_specs=[VMEM] * groups,
            compiler_params=room(12),
        )(*terms, *grads[1:])
        came = [emb_swap(pieces[step], step, embs) for step in range(1, groups)]
        mine = sum_rounded([value[:, :wide] for value in came[::-1]] + [pieces[0]])
        mine = mine.reshape(tables, unit, wide)
        sums = table_sums([grads[0]] + came)
        own_sums = over_cores(sums)
        came = [emb_swap(mine[step], step * groups, embs) for step in range(1, tables)]
        final = sum_rounded(came[-1:] + came[:-1] + [mine[0]])
        gathered = [final] + [emb_swap(final, step * groups, embs) for step in range(1, tables)]
        back = to_plane(jnp.concatenate(gathered, axis=0))
        later = after(own_sums, *gathered[1:])
        swapped = [emb_swap(later[step], step * groups, embs) for step in range(1, tables)]
        swapped = [after(value, *back[1:]) for value in swapped]
    else:
        sums = table_sums([grads[0]] + [emb_swap(grads[step], step, embs) for step in range(1, groups)])
        own_sums = over_cores(sums)
        swapped = [emb_swap(own_sums[step], step * groups, embs) for step in range(1, tables)]
    table_sum = swapped[-1].astype(f32)
    for value in swapped[:-1] + [own_sums[0]]:
        table_sum = table_sum + value.astype(f32)
    table_scale = (distinct / (bals * item_ids.shape[1])) ** 0.5

    if owned:
        totals = []
        for steps in ([0] + list(range(groups - 1, 1, -1))[: groups // 2 - 1], None):
            steps = steps or [step for step in range(1, groups) if step not in done]
            done = steps
            totals = pl.pallas_call(
                functools.partial(place_kernel, grad_scale, steps, slots, tables, bals, unit),
                out_shape=[
                    jax.ShapeDtypeStruct((weight_part, features), f32),
                    jax.ShapeDtypeStruct((weight_part, width), f32),
                ],
                in_specs=[SMEM] + [VMEM] * len(steps) + [HBM] * len(totals),
                out_specs=[HBM] * 2,
                scratch_shapes=[
                    pltpu.VMEM((len(steps) * tables * unit, features + width), f32),
                    pltpu.SemaphoreType.DMA((len(steps) * tables, 2)),
                ],
                input_output_aliases={1 + len(steps) + index: index for index in range(len(totals))},
                cost_estimate=estimate(1),
                compiler_params=room(12),
            )(scalars, *[back[step] for step in steps], *totals)
        total_in, total_out = totals
    else:
        total = lax.psum(over_cores(results).astype(f32), "emb") * grad_scale
        total_in, total_out = total[:, :features], total[:, features:]

    return layer_out[None], (table_sum * table_scale)[None], total_in, total_out


def solution(mesh):
    placed = (
        P("bal", None, None),
        P(None, "emb", None),
        P(None, "emb"),
        P(None, "emb"),
        P("emb", None, None),
        P("bal", None),
        P("bal", None),
        P("bal", "emb", None),
    )
    return jax.shard_map(
        on_device,
        mesh=mesh,
        in_specs=placed,
        out_specs=(P("bal", "emb", None), P("emb", "bal", None), P("bal", None), P("bal", None)),
        check_vma=False,
    )
```

```python
import functools

import jax
import jax.numpy as jnp
from jax import lax
from jax.experimental import pallas as pl
from jax.experimental.pallas import tpu as pltpu
from jax.sharding import PartitionSpec as P

HEADS = 8
EPS = 1e-05
LANES = 128
BLOCK_ROWS = 64
BLOCK_COLUMNS = 256

VMEM = pl.BlockSpec(memory_space=pltpu.VMEM)
SMEM = pl.BlockSpec(memory_space=pltpu.SMEM)
HBM = pl.BlockSpec(memory_space=pltpu.HBM)
f32 = jnp.float32
bf16 = jnp.bfloat16


def room(mib):
    return pltpu.CompilerParams(vmem_limit_bytes=mib * 1024 * 1024)


def estimate(microseconds):
    return pl.CostEstimate(flops=0, bytes_accessed=microseconds * 3_500_000, transcendentals=0)


def matmul(left, right):
    return lax.dot_general(left, right, (((1,), (0,)), ((), ())), preferred_element_type=f32)


def matmul_nt(left, right):
    return lax.dot_general(left, right, (((1,), (1,)), ((), ())), preferred_element_type=f32)


def matmul_tn(left, right):
    return lax.dot_general(left, right, (((0,), (0,)), ((), ())), preferred_element_type=f32)


def sigmoid(value):
    return 0.5 * jnp.tanh(0.5 * value) + 0.5


def bal_swap(value, step, count):
    return lax.ppermute(value, "bal", [(i, i ^ step) for i in range(count)])


def with_swapped(value, count):
    return [value] + [bal_swap(value, turn, count) for turn in range(1, count)]


def emb_swap(value, step, count):
    return lax.ppermute(value, "emb", [(i, i ^ step) for i in range(count)])


class Scalars:
    def __init__(self, ref, step, bals, slots):
        self.ref, self.step, self.bals, self.slots = ref, step, bals, slots

    def surplus(self, bal):
        return self.ref[self.step, bal]

    def source(self, bal):
        found = jnp.int32(0)
        for index in range(self.bals):
            found = found + jnp.where(self.ref[self.step, self.bals + index] == bal, index, 0)
        return found

    def length(self, bal, slot):
        return self.ref[self.step, 2 * self.bals + bal * self.slots + slot]

    def place(self):
        first = self.bals * (2 + self.slots)
        return self.ref[self.step, first], self.ref[self.step, first + 1], self.ref[self.step, first + 2]


def pick_ids(scalars, ids_refs, slots, tables):
    bal, group_here, _ = scalars[0].place()
    found = []
    for step, there in enumerate(scalars):
        group = group_here ^ step
        my_slot = there.surplus(bal)
        source = there.source(bal)
        from_slot = there.surplus(source)
        by_slot = [[] for _ in range(slots)]
        for table in tables:
            arrived = ids_refs[0][table, group * slots + from_slot]
            for turn in range(1, len(ids_refs)):
                other = ids_refs[turn][table, group * slots + from_slot]
                arrived = jnp.where(source ^ bal == turn, other, arrived)
            for slot in range(slots):
                own = ids_refs[0][table, group * slots + slot]
                by_slot[slot].append(jnp.where(my_slot == slot, arrived, own))
        found.append(by_slot)
    return found


def table_order(table_here, tables):
    return [table_here ^ step for step in range(tables)]


def lookup_kernel(groups, slots, tables, bals, *refs):
    refs = list(refs)
    take = lambda count: [refs.pop(0) for _ in range(count)]
    (scalar_ref,) = take(1)
    scalars = [Scalars(scalar_ref, step, bals, slots) for step in range(groups)]
    ids_refs = take(bals)
    pieces = [take(bals) for _ in range(tables)]
    out_refs = refs
    bal, _, table_here = scalars[0].place()
    part, columns = pieces[0][0].shape
    slot_rows = ids_refs[0].shape[3]
    lane = lax.broadcasted_iota(jnp.int32, (LANES, LANES), 1)
    ids = pick_ids(scalars, ids_refs, slots, table_order(table_here, tables))
    rows = out_refs[0].shape[0]
    total = jnp.zeros((groups * rows, columns), f32)
    for table in range(tables):
        found = []
        for group in range(groups):
            for slot in range(slots):
                for first in range(0, slot_rows, LANES):
                    row = ids[group][slot][table][:, first : first + LANES]
                    found.append(jnp.transpose(jnp.broadcast_to(row, (LANES, LANES))))
        column = jnp.concatenate(found, axis=0)
        for turn, ref in enumerate(pieces[table]):
            shifted = column - (bal ^ turn) * part
            hot = []
            for at in range(0, part, LANES):
                here = [shifted[row : row + LANES] == lane + at for row in range(0, groups * rows, LANES)]
                here = [jnp.where(one, 1.0, 0.0).astype(bf16) for one in here]
                hot.append(jnp.concatenate(here, axis=0))
            total = total + matmul(jnp.concatenate(hot, axis=1), ref[...])
    for group in range(groups):
        out_refs[group][...] = total[group * rows : (group + 1) * rows].astype(bf16)


def scatter_kernel(groups, slots, bals, *refs):
    refs = list(refs)
    take = lambda count: [refs.pop(0) for _ in range(count)]
    (scalar_ref,) = take(1)
    scalars = [Scalars(scalar_ref, step, bals, slots) for step in range(groups)]
    ids_refs, grad_refs, out_refs = take(bals), take(groups)[::-1], refs
    bal, _, table_here = scalars[0].place()
    tables, part, _ = out_refs[0].shape
    slot_rows = ids_refs[0].shape[3]
    height = min(part, 256)
    iota = lax.broadcasted_iota(jnp.int32, (height, slot_rows), 0)
    ids = pick_ids(scalars, ids_refs, slots, table_order(table_here, tables))
    columns = out_refs[0].shape[2]

    def rows_of(ref):
        height = ref.shape[0]
        first = ref.shape[1] - slots * slot_rows // height * columns
        return [ref[:, at : at + columns] for at in range(first, ref.shape[1], columns)]

    grads = jnp.concatenate([piece for ref in grad_refs for piece in rows_of(ref)], axis=0)
    for table in range(tables):
        for turn in range(bals):
            for at in range(0, part, height):
                start = (bal ^ turn) * part + at
                hot = jnp.concatenate(
                    [
                        jnp.where(iota == ids[group][slot][table] - start, 1.0, 0.0).astype(bf16)
                        for group in range(groups)
                        for slot in range(slots)
                    ],
                    axis=1,
                )
                out_refs[turn][table, at : at + height, :] = matmul(hot, grads).astype(bf16)


def norm(values):
    average = jnp.mean(values, axis=1, keepdims=True)
    centred = values - average
    inverse = lax.rsqrt(jnp.mean(centred * centred, axis=1, keepdims=True) + EPS)
    return centred * inverse, inverse


def norm_back(incoming, normed, inverse):
    first = jnp.mean(incoming, axis=1, keepdims=True)
    second = jnp.mean(incoming * normed, axis=1, keepdims=True)
    return inverse * (incoming - first - normed * second)


def times_parts_nt(value, weight_refs, first, last, bal, wide_ref):
    for turn, ref in enumerate(weight_refs):
        wide_ref[bal ^ turn] = matmul_nt(value, ref[:, first:last])
    return jnp.concatenate([wide_ref[index] for index in range(len(weight_refs))], axis=1)


def layer_kernel(groups, slots, tables, bals, unit, scalar_ref, *refs):
    refs = list(refs)
    take = lambda count: [refs.pop(0) for _ in range(count)]
    block_refs = take(groups)[::-1]
    weight_refs = take(bals)
    (cot_ref,) = take(1)
    (layer_ref,) = take(1)
    grads_ref, normed_ref, inverse_ref = take(3)
    term_refs = take(bals)
    (x_ref, halves_ref, wide_ref, nt_ref, mt_ref, weights_ref, slope_ref, gate_ref, heads_ref, dsilu_ref, out_ref, mixed_ref, back_ref) = refs

    scalars = Scalars(scalar_ref, 0, bals, slots)
    bal, group_here, table_here = scalars.place()
    rows, width = cot_ref.shape
    slot_rows = rows // slots
    head_width = width // HEADS
    score_scale = head_width**-0.5
    piece = block_refs[0].shape[1]
    part, features = weight_refs[0].shape[0], weight_refs[0].shape[1] - width

    blocks = [slice(at, at + BLOCK_ROWS) for at in range(0, rows, BLOCK_ROWS)]

    def keep_parts(here, value):
        for index in range(bals):
            halves_ref[index, here, :] = value[:, index * part : (index + 1) * part].astype(bf16)

    def times_parts(first, last):
        found = matmul(halves_ref[bal], weight_refs[0][:, first:last])
        for turn in range(1, bals):
            found = found + matmul(halves_ref[bal ^ turn], weight_refs[turn][:, first:last])
        return found

    my_slot = scalars.surplus(bal)
    source = scalars.source(bal)
    moved = scalars.length(source, scalars.surplus(source))
    lengths = [jnp.where(my_slot == slot, moved, scalars.length(bal, slot)) for slot in range(slots)]

    for step in range(groups):
        x_ref[group_here ^ step] = block_refs[step][...]

    def x_rows(here):
        return jnp.concatenate([x_ref[group, here, :] for group in range(groups)], axis=1).astype(f32)

    for here in blocks:
        normed, inverse = norm(x_rows(here))
        normed_ref[here, :] = normed
        inverse_ref[here, :] = jnp.broadcast_to(inverse, (BLOCK_ROWS, inverse_ref.shape[1]))
        keep_parts(here, normed)
    for at in range(0, features, width):
        dsilu_ref[:, at : at + width] = times_parts(at, at + width)
        for here in blocks:
            for first in range(at, at + width, BLOCK_COLUMNS):
                columns = slice(first, first + BLOCK_COLUMNS)
                projected = dsilu_ref[here, columns]
                logistic = sigmoid(projected)
                active = projected * logistic
                dsilu_ref[here, columns] = logistic + active * (1.0 - logistic)
                if at < width:
                    gate_ref[here, columns] = active
                else:
                    heads_ref[here, first - width : first - width + BLOCK_COLUMNS] = active.astype(bf16)
    nt_ref[...] = jnp.transpose(normed_ref[...]).astype(bf16)

    pair_width = 2 * head_width
    low = lax.broadcasted_iota(jnp.int32, (slot_rows, pair_width), 1) < head_width
    row_at = lax.broadcasted_iota(jnp.int32, (slot_rows, slot_rows), 0)
    col_at = lax.broadcasted_iota(jnp.int32, (slot_rows, slot_rows), 1)

    def split(value):
        zero = jnp.zeros_like(value)
        return jnp.concatenate([jnp.where(low, value, zero), jnp.where(low, zero, value)], axis=0)

    def side_by_side(value):
        return jnp.concatenate([value[:slot_rows], value[slot_rows:]], axis=1)

    def part_of(slot, pair, which):
        first = which * width + pair * pair_width
        return heads_ref[slot * slot_rows : (slot + 1) * slot_rows, first : first + pair_width]

    pairs = HEADS // 2
    for slot in range(slots):
        live = (col_at <= row_at) & (row_at < lengths[slot])
        allowed = jnp.where(live, 1.0 / slot_rows, 0.0)
        slot_here = slice(slot * slot_rows, (slot + 1) * slot_rows)
        for pair in range(pairs):
            value, query, key = (part_of(slot, pair, which) for which in range(3))
            scores = matmul_nt(split(query), key) * score_scale
            both = []
            for head in range(2):
                half = slice(head * slot_rows, (head + 1) * slot_rows)
                q = sigmoid(scores[half])
                sq = scores[half] * q
                both.append((sq * allowed).astype(bf16))
                weights_ref[slot * pairs + pair, half, :] = both[-1]
                slope_ref[slot * pairs + pair, half, :] = allowed * (q + sq * (1.0 - q))
            lanes = slice(pair * pair_width, (pair + 1) * pair_width)
            out_ref[slot_here, lanes] = matmul(jnp.concatenate(both, axis=1), split(value))

    cot = cot_ref[...].astype(bf16)
    mixed_ref[...] = times_parts_nt(cot, weight_refs, features, features + width, bal, wide_ref)
    for here in blocks:
        normed, inverse = norm(out_ref[here, :])
        gate = gate_ref[here, :]
        grad_mixed = mixed_ref[here, :]
        back_ref[here, :] = norm_back(grad_mixed * gate, normed, inverse).astype(bf16)
        grads_ref[here, :width] = (grad_mixed * normed * dsilu_ref[here, :width]).astype(bf16)
        mixed = normed * gate
        mixed_ref[here, :] = mixed
        keep_parts(here, mixed)
    mt_ref[...] = jnp.transpose(mixed_ref[...]).astype(bf16)
    mixed_ref[...] = times_parts(features, features + width)
    for here in blocks:
        layer_ref[here, :] = (x_rows(here) + mixed_ref[here, :]).astype(bf16)

    def owner_order(ref, turn):
        start = (bal ^ turn) * part
        if part != groups * tables * unit:
            return ref[pl.ds(pl.multiple_of(start, part), part), :]
        found = []
        for group_step in range(groups):
            for table_step in range(tables):
                owner = (group_here ^ group_step) * tables + (table_here ^ table_step)
                at = pl.multiple_of(start + owner * unit, unit)
                found.append(ref[pl.ds(at, unit), :])
        return jnp.concatenate(found, axis=0)

    def emit_terms(ref, right, first):
        left = jnp.concatenate([owner_order(ref, turn) for turn in range(bals)], axis=0)
        found = matmul(left, right).astype(bf16)
        for turn in range(bals):
            rows_here = slice(turn * part, (turn + 1) * part)
            term_refs[turn][:, first : first + right.shape[1]] = found[rows_here]

    emit_terms(mt_ref, cot, features)

    for slot in range(slots):
        here = slice(slot * slot_rows, (slot + 1) * slot_rows)
        for pair in range(pairs):
            value, query, key = (part_of(slot, pair, which) for which in range(3))
            lanes = slice(pair * pair_width, (pair + 1) * pair_width)
            upper = split(back_ref[here, lanes])
            grad_weights = matmul_nt(upper, value)
            grad_scores = (grad_weights * slope_ref[slot * pairs + pair]).astype(bf16)
            grad_value = matmul_tn(weights_ref[slot * pairs + pair], upper)
            grad_query = matmul(side_by_side(grad_scores), split(key)) * score_scale
            grad_key = matmul_tn(grad_scores, split(query)) * score_scale
            for which, found in enumerate((grad_value, grad_query, grad_key)):
                first = (1 + which) * width + pair * pair_width
                at = slice(first, first + pair_width)
                grads_ref[here, at] = (found * dsilu_ref[here, at]).astype(bf16)

    emit_terms(nt_ref, grads_ref[...], 0)


def rows_kernel(groups, slots, bals, scalar_ref, *refs):
    refs = list(refs)
    take = lambda count: [refs.pop(0) for _ in range(count)]
    grads_ref, normed_ref, inverse_ref, cot_ref = take(4)
    weight_refs, grad_refs = take(bals), take(groups)
    x_ref, wide_ref = refs
    bal, group_here, _ = Scalars(scalar_ref, 0, bals, slots).place()
    features = grads_ref.shape[1]
    piece = grad_refs[0].shape[1]
    grad_normed = times_parts_nt(grads_ref[...], weight_refs, 0, features, bal, wide_ref)
    back = norm_back(grad_normed, normed_ref[...], inverse_ref[:, :1])
    grad_rows = (cot_ref[...] + back).astype(bf16)
    for group in range(groups):
        x_ref[group] = grad_rows[:, group * piece : (group + 1) * piece]
    for step in range(groups):
        grad_refs[step][...] = x_ref[group_here ^ step]


def pieces_kernel(bals, *refs):
    count = len(refs) - bals
    groups = (count + 1) // 2
    term_refs, grad_refs = refs[:bals], refs[bals : bals + groups - 1]
    out_refs = refs[bals + groups - 1 :]
    height, width = out_refs[0].shape
    for step, out in enumerate(out_refs):
        rows = slice(step * height, (step + 1) * height)
        total = term_refs[0][rows, :].astype(f32)
        for ref in term_refs[1:]:
            total = total + ref[rows, :].astype(f32)
        out[:, :width] = total.astype(bf16)
        if step:
            grad = grad_refs[step - 1]
            columns = grad.shape[1]
            for index in range(grad.shape[0] // height):
                at = width + index * columns
                out[:, at : at + columns] = grad[index * height : (index + 1) * height, :]


def place_kernel(scale, steps, slots, tables, bals, unit, scalar_ref, *refs):
    pieces = refs[: len(steps)]
    in_ref, out_ref, scaled_ref, sems = refs[-4:]
    _, group_here, table_here = Scalars(scalar_ref, 0, bals, slots).place()
    features = in_ref.shape[1]
    copies = []
    for number, (group_step, piece) in enumerate(zip(steps, pieces)):
        for table_step in range(tables):
            index = number * tables + table_step
            at = index * unit
            from_rows = slice(table_step * unit, (table_step + 1) * unit)
            scaled_ref[at : at + unit, :] = piece[from_rows, :].astype(f32) * scale
            owner = (group_here ^ group_step) * tables + (table_here ^ table_step)
            to = pl.ds(pl.multiple_of(owner * unit, unit), unit)
            rows = scaled_ref.at[pl.ds(at, unit), :]
            sem = sems.at[index]
            copies.append(
                pltpu.make_async_copy(rows.at[:, pl.ds(0, features)], in_ref.at[to, :], sem.at[0])
            )
            copies.append(
                pltpu.make_async_copy(
                    rows.at[:, pl.ds(features, out_ref.shape[1])], out_ref.at[to, :], sem.at[1]
                )
            )
            copies[-2].start()
            copies[-1].start()
    for copy in copies:
        copy.wait()


def sum_rounded(terms):
    total = terms[0].astype(f32)
    for term in terms[1:]:
        total = total + term.astype(f32)
    return total.astype(bf16)


def after(value, *others):
    return lax.optimization_barrier((value,) + others)[0]


def on_device(
    item_ids, seq_lengths, surplus_slot, helper_map, embed_tables, weight_in, weight_out, cotangent
):
    bal = lax.axis_index("bal")
    emb = lax.axis_index("emb")
    bals = lax.axis_size("bal")
    embs = lax.axis_size("emb")
    tables = item_ids.shape[2]
    groups = embs // tables
    _, rows, width = cotangent.shape
    slots = seq_lengths.shape[2]
    slot_rows = rows // slots
    distinct, columns = embed_tables.shape[1:]
    part = distinct // bals
    weight_part = weight_in.shape[0]
    table_here = emb // groups
    group_here = emb % groups
    width, features = weight_out.shape[1], weight_in.shape[1]
    unit = weight_part // embs
    owned = unit % 16 == 0
    unit = unit if owned else 0
    first = bals * (2 + slots)
    lane = lax.broadcasted_iota(jnp.int32, (1, LANES), 1)
    scalars = jnp.where(lane == first, bal, 0)
    scalars = jnp.where(lane == first + 1, group_here, scalars)
    scalars = jnp.where(lane == first + 2, table_here, scalars)
    fields = [surplus_slot.T, helper_map.T] + [seq_lengths[index] for index in range(bals)]
    at = 0
    for field in fields:
        width_here = field.shape[1]
        scalars = scalars + jnp.pad(field, ((0, 0), (at, LANES - at - width_here)))
        at += width_here

    share = lax.dynamic_slice_in_dim(embed_tables[0], bal * part, part, 0)
    fetched = [emb_swap(share, step * groups, embs) for step in range(1, tables)]

    ids = lax.dynamic_slice_in_dim(
        jnp.transpose(after(item_ids[0], share)), table_here * groups * rows, groups * rows, 1
    )
    plane_ids = with_swapped(ids.reshape(tables, groups * slots, 1, slot_rows), bals)
    wide_cot = cotangent[0].astype(f32)
    scalars = after(scalars, share, wide_cot)
    for bit in range((groups - 1).bit_length()):
        scalars = jnp.concatenate([scalars, emb_swap(scalars, 1 << bit, embs)], axis=0)

    fetched[0] = after(fetched[0], scalars)
    pieces = [piece for one in [share] + fetched for piece in with_swapped(one, bals)]

    found = pl.pallas_call(
        functools.partial(lookup_kernel, groups, slots, tables, bals),
        out_shape=[jax.ShapeDtypeStruct((rows, columns), bf16)] * groups,
        in_specs=[SMEM] + [VMEM] * (bals + len(pieces)),
        out_specs=[VMEM] * groups,
        cost_estimate=estimate(3),
        compiler_params=room(16),
    )(scalars, *plane_ids, *pieces)
    weights = jnp.concatenate([weight_in, weight_out], axis=1)
    weights = with_swapped(after(weights, found[0]), bals)
    block = [found[0]] + [emb_swap(found[step], step, embs) for step in range(1, groups)]

    pairs = slots * HEADS // 2
    terms = jax.ShapeDtypeStruct((weight_part, features + width), bf16)
    results = pl.pallas_call(
        functools.partial(layer_kernel, groups, slots, tables, bals, unit),
        out_shape=[jax.ShapeDtypeStruct((rows, width), bf16)]
        + [jax.ShapeDtypeStruct((rows, features), bf16)]
        + [jax.ShapeDtypeStruct((rows, columns_here), f32) for columns_here in (width, LANES)]
        + [terms] * bals,
        in_specs=[SMEM] + [VMEM] * (groups + bals + 1),
        out_specs=[VMEM] * (4 + bals),
        scratch_shapes=[
            pltpu.VMEM((groups, rows, columns), bf16),
            pltpu.VMEM((bals, rows, weight_part), bf16),
            pltpu.VMEM((bals, rows, weight_part), f32),
            pltpu.VMEM((width, rows), bf16),
            pltpu.VMEM((width, rows), bf16),
            pltpu.VMEM((pairs, 2 * slot_rows, slot_rows), bf16),
            pltpu.VMEM((pairs, 2 * slot_rows, slot_rows), f32),
            pltpu.VMEM((rows, width), f32),
            pltpu.VMEM((rows, features - width), bf16),
            pltpu.VMEM((rows, features), f32),
            pltpu.VMEM((rows, width), f32),
            pltpu.VMEM((rows, width), f32),
            pltpu.VMEM((rows, width), bf16),
        ],
        cost_estimate=estimate(7),
        compiler_params=room(36),
    )(scalars, *block[::-1], *weights, wide_cot)
    layer_out, for_rows, results = results[0], results[1:4], results[4:]
    grads = pl.pallas_call(
        functools.partial(rows_kernel, groups, slots, bals),
        out_shape=[jax.ShapeDtypeStruct((rows, columns), bf16)] * groups,
        in_specs=[SMEM] + [VMEM] * (4 + bals),
        out_specs=[VMEM] * groups,
        scratch_shapes=[
            pltpu.VMEM((groups, rows, columns), bf16),
            pltpu.VMEM((bals, rows, weight_part), f32),
        ],
        cost_estimate=estimate(2),
        compiler_params=room(16),
    )(scalars, *for_rows, wide_cot, *weights)

    def over_cores(parts):
        return sum_rounded([parts[0]] + [bal_swap(parts[turn], turn, bals) for turn in range(1, bals)])

    def to_plane(value):
        return [value] + [emb_swap(value, step, embs) for step in range(1, groups)]

    def table_sums(plane_grads):
        return pl.pallas_call(
            functools.partial(scatter_kernel, groups, slots, bals),
            out_shape=[jax.ShapeDtypeStruct((tables, part, columns), bf16)] * bals,
            in_specs=[SMEM] + [VMEM] * (bals + groups),
            out_specs=[VMEM] * bals,
            cost_estimate=estimate(3),
            compiler_params=room(16),
        )(scalars, *plane_ids, *plane_grads[::-1])

    grad_scale = (rows * embs * bals) ** -0.5
    if owned:
        height, wide = weight_part // groups, features + width
        terms = [results[0]] + [bal_swap(results[turn], turn, bals) for turn in range(1, bals)]
        pieces = pl.pallas_call(
            functools.partial(pieces_kernel, bals),
            out_shape=[jax.ShapeDtypeStruct((height, wide), bf16)]
            + [jax.ShapeDtypeStruct((height, wide + rows // height * columns), bf16)] * (groups - 1),
            in_specs=[VMEM] * (bals + groups - 1),
            out_specs=[VMEM] * groups,
            compiler_params=room(12),
        )(*terms, *grads[1:])
        came = [emb_swap(pieces[step], step, embs) for step in range(1, groups)]
        mine = sum_rounded([value[:, :wide] for value in came[::-1]] + [pieces[0]])
        mine = mine.reshape(tables, unit, wide)
        sums = table_sums([grads[0]] + came)
        own_sums = over_cores(sums)
        came = [emb_swap(mine[step], step * groups, embs) for step in range(1, tables)]
        final = sum_rounded(came[-1:] + came[:-1] + [mine[0]])
        gathered = [final] + [emb_swap(final, step * groups, embs) for step in range(1, tables)]
        back = to_plane(jnp.concatenate(gathered, axis=0))
        later = after(own_sums, *gathered[1:])
        swapped = [emb_swap(later[step], step * groups, embs) for step in range(1, tables)]
        swapped = [after(value, *back[1:]) for value in swapped]
    else:
        sums = table_sums([grads[0]] + [emb_swap(grads[step], step, embs) for step in range(1, groups)])
        own_sums = over_cores(sums)
        swapped = [emb_swap(own_sums[step], step * groups, embs) for step in range(1, tables)]
    table_sum = swapped[-1].astype(f32)
    for value in swapped[:-1] + [own_sums[0]]:
        table_sum = table_sum + value.astype(f32)
    table_scale = (distinct / (bals * item_ids.shape[1])) ** 0.5

    if owned:
        totals = []
        for steps in ([0] + list(range(groups - 1, 1, -1))[: groups // 2 - 1], None):
            steps = steps or [step for step in range(1, groups) if step not in done]
            done = steps
            totals = pl.pallas_call(
                functools.partial(place_kernel, grad_scale, steps, slots, tables, bals, unit),
                out_shape=[
                    jax.ShapeDtypeStruct((weight_part, features), f32),
                    jax.ShapeDtypeStruct((weight_part, width), f32),
                ],
                in_specs=[SMEM] + [VMEM] * len(steps) + [HBM] * len(totals),
                out_specs=[HBM] * 2,
                scratch_shapes=[
                    pltpu.VMEM((len(steps) * tables * unit, features + width), f32),
                    pltpu.SemaphoreType.DMA((len(steps) * tables, 2)),
                ],
                input_output_aliases={1 + len(steps) + index: index for index in range(len(totals))},
                cost_estimate=estimate(1),
                compiler_params=room(12),
            )(scalars, *[back[step] for step in steps], *totals)
        total_in, total_out = totals
    else:
        total = lax.psum(over_cores(results).astype(f32), "emb") * grad_scale
        total_in, total_out = total[:, :features], total[:, features:]

    return layer_out[None], (table_sum * table_scale)[None], total_in, total_out


def solution(mesh):
    placed = (
        P("bal", None, None),
        P(None, "emb", None),
        P(None, "emb"),
        P(None, "emb"),
        P("emb", None, None),
        P("bal", None),
        P("bal", None),
        P("bal", "emb", None),
    )
    return jax.shard_map(
        on_device,
        mesh=mesh,
        in_specs=placed,
        out_specs=(P("bal", "emb", None), P("emb", "bal", None), P("bal", None), P("bal", None)),
        check_vma=False,
    )
```

```python
import functools

import jax
import jax.numpy as jnp
from jax import lax
from jax.experimental import pallas as pl
from jax.experimental.pallas import tpu as pltpu
from jax.sharding import PartitionSpec as P

HEADS = 8
EPS = 1e-05
LANES = 128
BLOCK_ROWS = 64
BLOCK_COLUMNS = 256

VMEM = pl.BlockSpec(memory_space=pltpu.VMEM)
SMEM = pl.BlockSpec(memory_space=pltpu.SMEM)
HBM = pl.BlockSpec(memory_space=pltpu.HBM)
f32 = jnp.float32
bf16 = jnp.bfloat16


def room(mib):
    return pltpu.CompilerParams(vmem_limit_bytes=mib * 1024 * 1024)


def estimate(microseconds):
    return pl.CostEstimate(flops=0, bytes_accessed=microseconds * 3_500_000, transcendentals=0)


def matmul(left, right):
    return lax.dot_general(left, right, (((1,), (0,)), ((), ())), preferred_element_type=f32)


def matmul_nt(left, right):
    return lax.dot_general(left, right, (((1,), (1,)), ((), ())), preferred_element_type=f32)


def matmul_tn(left, right):
    return lax.dot_general(left, right, (((0,), (0,)), ((), ())), preferred_element_type=f32)


def sigmoid(value):
    return 0.5 * jnp.tanh(0.5 * value) + 0.5


def bal_swap(value, step, count):
    return lax.ppermute(value, "bal", [(i, i ^ step) for i in range(count)])


def with_swapped(value, count):
    return [value] + [bal_swap(value, turn, count) for turn in range(1, count)]


def emb_swap(value, step, count):
    return lax.ppermute(value, "emb", [(i, i ^ step) for i in range(count)])


class Scalars:
    def __init__(self, ref, step, bals, slots):
        self.ref, self.step, self.bals, self.slots = ref, step, bals, slots

    def surplus(self, bal):
        return self.ref[self.step, bal]

    def source(self, bal):
        found = jnp.int32(0)
        for index in range(self.bals):
            found = found + jnp.where(self.ref[self.step, self.bals + index] == bal, index, 0)
        return found

    def length(self, bal, slot):
        return self.ref[self.step, 2 * self.bals + bal * self.slots + slot]

    def place(self):
        first = self.bals * (2 + self.slots)
        return self.ref[self.step, first], self.ref[self.step, first + 1], self.ref[self.step, first + 2]


def pick_ids(scalars, ids_refs, slots, tables):
    bal, group_here, _ = scalars[0].place()
    found = []
    for step, there in enumerate(scalars):
        group = group_here ^ step
        my_slot = there.surplus(bal)
        source = there.source(bal)
        from_slot = there.surplus(source)
        by_slot = [[] for _ in range(slots)]
        for table in tables:
            arrived = ids_refs[0][table, group * slots + from_slot]
            for turn in range(1, len(ids_refs)):
                other = ids_refs[turn][table, group * slots + from_slot]
                arrived = jnp.where(source ^ bal == turn, other, arrived)
            for slot in range(slots):
                own = ids_refs[0][table, group * slots + slot]
                by_slot[slot].append(jnp.where(my_slot == slot, arrived, own))
        found.append(by_slot)
    return found


def table_order(table_here, tables):
    return [table_here ^ step for step in range(tables)]


def lookup_kernel(groups, slots, tables, bals, *refs):
    refs = list(refs)
    take = lambda count: [refs.pop(0) for _ in range(count)]
    (scalar_ref,) = take(1)
    scalars = [Scalars(scalar_ref, step, bals, slots) for step in range(groups)]
    ids_refs = take(bals)
    pieces = [take(bals) for _ in range(tables)]
    out_refs = refs
    bal, _, table_here = scalars[0].place()
    part, columns = pieces[0][0].shape
    slot_rows = ids_refs[0].shape[3]
    lane = lax.broadcasted_iota(jnp.int32, (LANES, LANES), 1)
    ids = pick_ids(scalars, ids_refs, slots, table_order(table_here, tables))
    rows = out_refs[0].shape[0]
    total = jnp.zeros((groups * rows, columns), f32)
    for table in range(tables):
        found = []
        for group in range(groups):
            for slot in range(slots):
                for first in range(0, slot_rows, LANES):
                    row = ids[group][slot][table][:, first : first + LANES]
                    found.append(jnp.transpose(jnp.broadcast_to(row, (LANES, LANES))))
        column = jnp.concatenate(found, axis=0)
        for turn, ref in enumerate(pieces[table]):
            shifted = column - (bal ^ turn) * part
            hot = []
            for at in range(0, part, LANES):
                here = [shifted[row : row + LANES] == lane + at for row in range(0, groups * rows, LANES)]
                here = [jnp.where(one, 1.0, 0.0).astype(bf16) for one in here]
                hot.append(jnp.concatenate(here, axis=0))
            total = total + matmul(jnp.concatenate(hot, axis=1), ref[...])
    for group in range(groups):
        out_refs[group][...] = total[group * rows : (group + 1) * rows].astype(bf16)


def scatter_kernel(groups, slots, bals, *refs):
    refs = list(refs)
    take = lambda count: [refs.pop(0) for _ in range(count)]
    (scalar_ref,) = take(1)
    scalars = [Scalars(scalar_ref, step, bals, slots) for step in range(groups)]
    ids_refs, grad_refs, out_refs = take(bals), take(groups)[::-1], refs
    bal, _, table_here = scalars[0].place()
    tables, part, _ = out_refs[0].shape
    slot_rows = ids_refs[0].shape[3]
    height = min(part, 256)
    iota = lax.broadcasted_iota(jnp.int32, (height, slot_rows), 0)
    ids = pick_ids(scalars, ids_refs, slots, table_order(table_here, tables))
    columns = out_refs[0].shape[2]

    def rows_of(ref):
        height = ref.shape[0]
        first = ref.shape[1] - slots * slot_rows // height * columns
        return [ref[:, at : at + columns] for at in range(first, ref.shape[1], columns)]

    grads = jnp.concatenate([piece for ref in grad_refs for piece in rows_of(ref)], axis=0)
    for table in range(tables):
        for turn in range(bals):
            for at in range(0, part, height):
                start = (bal ^ turn) * part + at
                hot = jnp.concatenate(
                    [
                        jnp.where(iota == ids[group][slot][table] - start, 1.0, 0.0).astype(bf16)
                        for group in range(groups)
                        for slot in range(slots)
                    ],
                    axis=1,
                )
                out_refs[turn][table, at : at + height, :] = matmul(hot, grads).astype(bf16)


def norm(values):
    average = jnp.mean(values, axis=1, keepdims=True)
    centred = values - average
    inverse = lax.rsqrt(jnp.mean(centred * centred, axis=1, keepdims=True) + EPS)
    return centred * inverse, inverse


def norm_back(incoming, normed, inverse):
    first = jnp.mean(incoming, axis=1, keepdims=True)
    second = jnp.mean(incoming * normed, axis=1, keepdims=True)
    return inverse * (incoming - first - normed * second)


def times_parts_nt(value, weight_refs, first, last, bal, wide_ref):
    for turn, ref in enumerate(weight_refs):
        wide_ref[bal ^ turn] = matmul_nt(value, ref[:, first:last])
    return jnp.concatenate([wide_ref[index] for index in range(len(weight_refs))], axis=1)


def layer_kernel(groups, slots, tables, bals, unit, scalar_ref, *refs):
    refs = list(refs)
    take = lambda count: [refs.pop(0) for _ in range(count)]
    block_refs = take(groups)[::-1]
    weight_refs = take(bals)
    (cot_ref,) = take(1)
    grads_ref, normed_ref, inverse_ref, keep_mixed_ref = take(4)
    term_refs = take(bals)
    (x_ref, halves_ref, wide_ref, nt_ref, mt_ref, weights_ref, slope_ref, gate_ref, heads_ref, dsilu_ref, out_ref, mixed_ref, back_ref) = refs

    scalars = Scalars(scalar_ref, 0, bals, slots)
    bal, group_here, table_here = scalars.place()
    rows, width = cot_ref.shape
    slot_rows = rows // slots
    head_width = width // HEADS
    score_scale = head_width**-0.5
    piece = block_refs[0].shape[1]
    part, features = weight_refs[0].shape[0], weight_refs[0].shape[1] - width

    blocks = [slice(at, at + BLOCK_ROWS) for at in range(0, rows, BLOCK_ROWS)]

    def keep_parts(here, value):
        for index in range(bals):
            halves_ref[index, here, :] = value[:, index * part : (index + 1) * part].astype(bf16)

    def times_parts(first, last):
        found = matmul(halves_ref[bal], weight_refs[0][:, first:last])
        for turn in range(1, bals):
            found = found + matmul(halves_ref[bal ^ turn], weight_refs[turn][:, first:last])
        return found

    my_slot = scalars.surplus(bal)
    source = scalars.source(bal)
    moved = scalars.length(source, scalars.surplus(source))
    lengths = [jnp.where(my_slot == slot, moved, scalars.length(bal, slot)) for slot in range(slots)]

    for step in range(groups):
        x_ref[group_here ^ step] = block_refs[step][...]

    def x_rows(here):
        return jnp.concatenate([x_ref[group, here, :] for group in range(groups)], axis=1).astype(f32)

    for here in blocks:
        normed, inverse = norm(x_rows(here))
        normed_ref[here, :] = normed
        inverse_ref[here, :] = jnp.broadcast_to(inverse, (BLOCK_ROWS, inverse_ref.shape[1]))
        keep_parts(here, normed)
    for at in range(0, features, width):
        dsilu_ref[:, at : at + width] = times_parts(at, at + width)
        for here in blocks:
            for first in range(at, at + width, BLOCK_COLUMNS):
                columns = slice(first, first + BLOCK_COLUMNS)
                projected = dsilu_ref[here, columns]
                logistic = sigmoid(projected)
                active = projected * logistic
                dsilu_ref[here, columns] = logistic + active * (1.0 - logistic)
                if at < width:
                    gate_ref[here, columns] = active
                else:
                    heads_ref[here, first - width : first - width + BLOCK_COLUMNS] = active.astype(bf16)
    nt_ref[...] = jnp.transpose(normed_ref[...]).astype(bf16)

    pair_width = 2 * head_width
    low = lax.broadcasted_iota(jnp.int32, (slot_rows, pair_width), 1) < head_width
    row_at = lax.broadcasted_iota(jnp.int32, (slot_rows, slot_rows), 0)
    col_at = lax.broadcasted_iota(jnp.int32, (slot_rows, slot_rows), 1)

    def split(value):
        zero = jnp.zeros_like(value)
        return jnp.concatenate([jnp.where(low, value, zero), jnp.where(low, zero, value)], axis=0)

    def side_by_side(value):
        return jnp.concatenate([value[:slot_rows], value[slot_rows:]], axis=1)

    def part_of(slot, pair, which):
        first = which * width + pair * pair_width
        return heads_ref[slot * slot_rows : (slot + 1) * slot_rows, first : first + pair_width]

    pairs = HEADS // 2
    for slot in range(slots):
        live = (col_at <= row_at) & (row_at < lengths[slot])
        allowed = jnp.where(live, 1.0 / slot_rows, 0.0)
        slot_here = slice(slot * slot_rows, (slot + 1) * slot_rows)
        for pair in range(pairs):
            value, query, key = (part_of(slot, pair, which) for which in range(3))
            scores = matmul_nt(split(query), key) * score_scale
            both = []
            for head in range(2):
                half = slice(head * slot_rows, (head + 1) * slot_rows)
                q = sigmoid(scores[half])
                sq = scores[half] * q
                both.append((sq * allowed).astype(bf16))
                weights_ref[slot * pairs + pair, half, :] = both[-1]
                slope_ref[slot * pairs + pair, half, :] = allowed * (q + sq * (1.0 - q))
            lanes = slice(pair * pair_width, (pair + 1) * pair_width)
            out_ref[slot_here, lanes] = matmul(jnp.concatenate(both, axis=1), split(value))

    cot = cot_ref[...].astype(bf16)
    mixed_ref[...] = times_parts_nt(cot, weight_refs, features, features + width, bal, wide_ref)
    for here in blocks:
        normed, inverse = norm(out_ref[here, :])
        gate = gate_ref[here, :]
        grad_mixed = mixed_ref[here, :]
        back_ref[here, :] = norm_back(grad_mixed * gate, normed, inverse).astype(bf16)
        grads_ref[here, :width] = (grad_mixed * normed * dsilu_ref[here, :width]).astype(bf16)
        mixed = normed * gate
        mixed_ref[here, :] = mixed
        keep_mixed_ref[here, :] = mixed.astype(bf16)
    mt_ref[...] = jnp.transpose(mixed_ref[...]).astype(bf16)

    def owner_order(ref, turn):
        start = (bal ^ turn) * part
        if part != groups * tables * unit:
            return ref[pl.ds(pl.multiple_of(start, part), part), :]
        found = []
        for group_step in range(groups):
            for table_step in range(tables):
                owner = (group_here ^ group_step) * tables + (table_here ^ table_step)
                at = pl.multiple_of(start + owner * unit, unit)
                found.append(ref[pl.ds(at, unit), :])
        return jnp.concatenate(found, axis=0)

    def emit_terms(ref, right, first):
        left = jnp.concatenate([owner_order(ref, turn) for turn in range(bals)], axis=0)
        found = matmul(left, right).astype(bf16)
        for turn in range(bals):
            rows_here = slice(turn * part, (turn + 1) * part)
            term_refs[turn][:, first : first + right.shape[1]] = found[rows_here]

    emit_terms(mt_ref, cot, features)

    for slot in range(slots):
        here = slice(slot * slot_rows, (slot + 1) * slot_rows)
        for pair in range(pairs):
            value, query, key = (part_of(slot, pair, which) for which in range(3))
            lanes = slice(pair * pair_width, (pair + 1) * pair_width)
            upper = split(back_ref[here, lanes])
            grad_weights = matmul_nt(upper, value)
            grad_scores = (grad_weights * slope_ref[slot * pairs + pair]).astype(bf16)
            grad_value = matmul_tn(weights_ref[slot * pairs + pair], upper)
            grad_query = matmul(side_by_side(grad_scores), split(key)) * score_scale
            grad_key = matmul_tn(grad_scores, split(query)) * score_scale
            for which, found in enumerate((grad_value, grad_query, grad_key)):
                first = (1 + which) * width + pair * pair_width
                at = slice(first, first + pair_width)
                grads_ref[here, at] = (found * dsilu_ref[here, at]).astype(bf16)

    emit_terms(nt_ref, grads_ref[...], 0)


def rows_kernel(groups, slots, bals, scalar_ref, *refs):
    refs = list(refs)
    take = lambda count: [refs.pop(0) for _ in range(count)]
    grads_ref, normed_ref, inverse_ref, mixed_ref, cot_ref = take(5)
    weight_refs, block_refs = take(bals), take(groups)
    (layer_ref,) = take(1)
    grad_refs = take(groups)
    x_ref, wide_ref, halves_ref = refs
    bal, group_here, _ = Scalars(scalar_ref, 0, bals, slots).place()
    features = grads_ref.shape[1]
    piece = grad_refs[0].shape[1]
    part = weight_refs[0].shape[0]
    for step in range(groups):
        x_ref[group_here ^ step] = block_refs[step][...]
    x = jnp.concatenate([x_ref[group] for group in range(groups)], axis=1).astype(f32)
    for index in range(bals):
        halves_ref[index] = mixed_ref[:, index * part : (index + 1) * part]
    for turn in range(bals):
        x = x + matmul(halves_ref[bal ^ turn], weight_refs[turn][:, features:])
    layer_ref[...] = x.astype(bf16)
    grad_normed = times_parts_nt(grads_ref[...], weight_refs, 0, features, bal, wide_ref)
    back = norm_back(grad_normed, normed_ref[...], inverse_ref[:, :1])
    grad_rows = (cot_ref[...] + back).astype(bf16)
    for group in range(groups):
        x_ref[group] = grad_rows[:, group * piece : (group + 1) * piece]
    for step in range(groups):
        grad_refs[step][...] = x_ref[group_here ^ step]


def pieces_kernel(bals, *refs):
    count = len(refs) - bals
    groups = (count + 1) // 2
    term_refs, grad_refs = refs[:bals], refs[bals : bals + groups - 1]
    out_refs = refs[bals + groups - 1 :]
    height, width = out_refs[0].shape
    for step, out in enumerate(out_refs):
        rows = slice(step * height, (step + 1) * height)
        total = term_refs[0][rows, :].astype(f32)
        for ref in term_refs[1:]:
            total = total + ref[rows, :].astype(f32)
        out[:, :width] = total.astype(bf16)
        if step:
            grad = grad_refs[step - 1]
            columns = grad.shape[1]
            for index in range(grad.shape[0] // height):
                at = width + index * columns
                out[:, at : at + columns] = grad[index * height : (index + 1) * height, :]


def place_kernel(scale, steps, slots, tables, bals, unit, scalar_ref, *refs):
    pieces = refs[: len(steps)]
    in_ref, out_ref, scaled_ref, sems = refs[-4:]
    _, group_here, table_here = Scalars(scalar_ref, 0, bals, slots).place()
    features = in_ref.shape[1]
    copies = []
    height = tables * unit
    for number, (group_step, piece) in enumerate(zip(steps, pieces)):
        for table_step in range(tables):
            to = pl.multiple_of(number * height + (table_here ^ table_step) * unit, unit)
            value = piece[table_step * unit : (table_step + 1) * unit, :]
            scaled_ref[pl.ds(to, unit), :] = value.astype(f32) * scale
        from_rows = scaled_ref.at[pl.ds(number * height, height), :]
        to = pl.ds(pl.multiple_of((group_here ^ group_step) * height, height), height)
        for index, (first, out) in enumerate(((0, in_ref), (features, out_ref))):
            copies.append(
                pltpu.make_async_copy(
                    from_rows.at[:, pl.ds(first, out.shape[1])], out.at[to, :], sems.at[number, index]
                )
            )
            copies[-1].start()
    for copy in copies:
        copy.wait()


def sum_rounded(terms):
    total = terms[0].astype(f32)
    for term in terms[1:]:
        total = total + term.astype(f32)
    return total.astype(bf16)


def after(value, *others):
    return lax.optimization_barrier((value,) + others)[0]


def on_device(
    item_ids, seq_lengths, surplus_slot, helper_map, embed_tables, weight_in, weight_out, cotangent
):
    bal = lax.axis_index("bal")
    emb = lax.axis_index("emb")
    bals = lax.axis_size("bal")
    embs = lax.axis_size("emb")
    tables = item_ids.shape[2]
    groups = embs // tables
    _, rows, width = cotangent.shape
    slots = seq_lengths.shape[2]
    slot_rows = rows // slots
    distinct, columns = embed_tables.shape[1:]
    part = distinct // bals
    weight_part = weight_in.shape[0]
    table_here = emb // groups
    group_here = emb % groups
    width, features = weight_out.shape[1], weight_in.shape[1]
    unit = weight_part // embs
    owned = unit % 16 == 0
    unit = unit if owned else 0
    first = bals * (2 + slots)
    lane = lax.broadcasted_iota(jnp.int32, (1, LANES), 1)
    scalars = jnp.where(lane == first, bal, 0)
    scalars = jnp.where(lane == first + 1, group_here, scalars)
    scalars = jnp.where(lane == first + 2, table_here, scalars)
    fields = [surplus_slot.T, helper_map.T] + [seq_lengths[index] for index in range(bals)]
    at = 0
    for field in fields:
        width_here = field.shape[1]
        scalars = scalars + jnp.pad(field, ((0, 0), (at, LANES - at - width_here)))
        at += width_here

    share = lax.dynamic_slice_in_dim(embed_tables[0], bal * part, part, 0)
    fetched = [emb_swap(share, step * groups, embs) for step in range(1, tables)]

    ids = lax.dynamic_slice_in_dim(
        jnp.transpose(after(item_ids[0], share)), table_here * groups * rows, groups * rows, 1
    )
    plane_ids = with_swapped(ids.reshape(tables, groups * slots, 1, slot_rows), bals)
    wide_cot = cotangent[0].astype(f32)
    scalars = after(scalars, share, wide_cot)
    for bit in range((groups - 1).bit_length()):
        scalars = jnp.concatenate([scalars, emb_swap(scalars, 1 << bit, embs)], axis=0)

    fetched[0] = after(fetched[0], scalars)
    pieces = [piece for one in [share] + fetched for piece in with_swapped(one, bals)]

    found = pl.pallas_call(
        functools.partial(lookup_kernel, groups, slots, tables, bals),
        out_shape=[jax.ShapeDtypeStruct((rows, columns), bf16)] * groups,
        in_specs=[SMEM] + [VMEM] * (bals + len(pieces)),
        out_specs=[VMEM] * groups,
        cost_estimate=estimate(3),
        compiler_params=room(16),
    )(scalars, *plane_ids, *pieces)
    weights = jnp.concatenate([weight_in, weight_out], axis=1)
    weights = with_swapped(after(weights, found[0]), bals)
    block = [found[0]] + [emb_swap(found[step], step, embs) for step in range(1, groups)]

    pairs = slots * HEADS // 2
    terms = jax.ShapeDtypeStruct((weight_part, features + width), bf16)
    results = pl.pallas_call(
        functools.partial(layer_kernel, groups, slots, tables, bals, unit),
        out_shape=[jax.ShapeDtypeStruct((rows, features), bf16)]
        + [jax.ShapeDtypeStruct((rows, columns_here), f32) for columns_here in (width, LANES)]
        + [jax.ShapeDtypeStruct((rows, width), bf16)]
        + [terms] * bals,
        in_specs=[SMEM] + [VMEM] * (groups + bals + 1),
        out_specs=[VMEM] * (4 + bals),
        scratch_shapes=[
            pltpu.VMEM((groups, rows, columns), bf16),
            pltpu.VMEM((bals, rows, weight_part), bf16),
            pltpu.VMEM((bals, rows, weight_part), f32),
            pltpu.VMEM((width, rows), bf16),
            pltpu.VMEM((width, rows), bf16),
            pltpu.VMEM((pairs, 2 * slot_rows, slot_rows), bf16),
            pltpu.VMEM((pairs, 2 * slot_rows, slot_rows), f32),
            pltpu.VMEM((rows, width), f32),
            pltpu.VMEM((rows, features - width), bf16),
            pltpu.VMEM((rows, features), f32),
            pltpu.VMEM((rows, width), f32),
            pltpu.VMEM((rows, width), f32),
            pltpu.VMEM((rows, width), bf16),
        ],
        cost_estimate=estimate(7),
        compiler_params=room(36),
    )(scalars, *block[::-1], *weights, wide_cot)
    for_rows, results = results[:4], results[4:]
    layer_out, *grads = pl.pallas_call(
        functools.partial(rows_kernel, groups, slots, bals),
        out_shape=[jax.ShapeDtypeStruct((rows, width), bf16)]
        + [jax.ShapeDtypeStruct((rows, columns), bf16)] * groups,
        in_specs=[SMEM] + [VMEM] * (5 + bals + groups),
        out_specs=[VMEM] * (1 + groups),
        scratch_shapes=[
            pltpu.VMEM((groups, rows, columns), bf16),
            pltpu.VMEM((bals, rows, weight_part), f32),
            pltpu.VMEM((bals, rows, weight_part), bf16),
        ],
        cost_estimate=estimate(2),
        compiler_params=room(16),
    )(scalars, *for_rows, wide_cot, *weights, *block)

    def over_cores(parts):
        return sum_rounded([parts[0]] + [bal_swap(parts[turn], turn, bals) for turn in range(1, bals)])

    def to_plane(value):
        return [value] + [emb_swap(value, step, embs) for step in range(1, groups)]

    def table_sums(plane_grads):
        return pl.pallas_call(
            functools.partial(scatter_kernel, groups, slots, bals),
            out_shape=[jax.ShapeDtypeStruct((tables, part, columns), bf16)] * bals,
            in_specs=[SMEM] + [VMEM] * (bals + groups),
            out_specs=[VMEM] * bals,
            cost_estimate=estimate(3),
            compiler_params=room(16),
        )(scalars, *plane_ids, *plane_grads[::-1])

    grad_scale = (rows * embs * bals) ** -0.5
    if owned:
        height, wide = weight_part // groups, features + width
        terms = [results[0]] + [bal_swap(results[turn], turn, bals) for turn in range(1, bals)]
        pieces = pl.pallas_call(
            functools.partial(pieces_kernel, bals),
            out_shape=[jax.ShapeDtypeStruct((height, wide), bf16)]
            + [jax.ShapeDtypeStruct((height, wide + rows // height * columns), bf16)] * (groups - 1),
            in_specs=[VMEM] * (bals + groups - 1),
            out_specs=[VMEM] * groups,
            compiler_params=room(12),
        )(*terms, *grads[1:])
        came = [emb_swap(pieces[step], step, embs) for step in range(1, groups)]
        mine = sum_rounded([value[:, :wide] for value in came[::-1]] + [pieces[0]])
        mine = mine.reshape(tables, unit, wide)
        sums = table_sums([grads[0]] + came)
        own_sums = over_cores(sums)
        came = [emb_swap(mine[step], step * groups, embs) for step in range(1, tables)]
        final = sum_rounded(came[-1:] + came[:-1] + [mine[0]])
        gathered = [final] + [emb_swap(final, step * groups, embs) for step in range(1, tables)]
        back = to_plane(jnp.concatenate(gathered, axis=0))
        later = after(own_sums, *gathered[1:])
        swapped = [emb_swap(later[step], step * groups, embs) for step in range(1, tables)]
        swapped = [after(value, *back[1:]) for value in swapped]
    else:
        sums = table_sums([grads[0]] + [emb_swap(grads[step], step, embs) for step in range(1, groups)])
        own_sums = over_cores(sums)
        swapped = [emb_swap(own_sums[step], step * groups, embs) for step in range(1, tables)]
    table_sum = swapped[-1].astype(f32)
    for value in swapped[:-1] + [own_sums[0]]:
        table_sum = table_sum + value.astype(f32)
    table_scale = (distinct / (bals * item_ids.shape[1])) ** 0.5

    if owned:
        totals = []
        for steps in ([0] + list(range(groups - 1, 1, -1))[: groups // 2 - 1], None):
            steps = steps or [step for step in range(1, groups) if step not in done]
            done = steps
            totals = pl.pallas_call(
                functools.partial(place_kernel, grad_scale, steps, slots, tables, bals, unit),
                out_shape=[
                    jax.ShapeDtypeStruct((weight_part, features), f32),
                    jax.ShapeDtypeStruct((weight_part, width), f32),
                ],
                in_specs=[SMEM] + [VMEM] * len(steps) + [HBM] * len(totals),
                out_specs=[HBM] * 2,
                scratch_shapes=[
                    pltpu.VMEM((len(steps) * tables * unit, features + width), f32),
                    pltpu.SemaphoreType.DMA((len(steps), 2)),
                ],
                input_output_aliases={1 + len(steps) + index: index for index in range(len(totals))},
                cost_estimate=estimate(1),
                compiler_params=room(12),
            )(scalars, *[back[step] for step in steps], *totals)
        total_in, total_out = totals
    else:
        total = lax.psum(over_cores(results).astype(f32), "emb") * grad_scale
        total_in, total_out = total[:, :features], total[:, features:]

    return layer_out[None], (table_sum * table_scale)[None], total_in, total_out


def solution(mesh):
    placed = (
        P("bal", None, None),
        P(None, "emb", None),
        P(None, "emb"),
        P(None, "emb"),
        P("emb", None, None),
        P("bal", None),
        P("bal", None),
        P("bal", "emb", None),
    )
    return jax.shard_map(
        on_device,
        mesh=mesh,
        in_specs=placed,
        out_specs=(P("bal", "emb", None), P("emb", "bal", None), P("bal", None), P("bal", None)),
        check_vma=False,
    )
```

```python
import functools

import jax
import jax.numpy as jnp
from jax import lax
from jax.experimental import pallas as pl
from jax.experimental.pallas import tpu as pltpu
from jax.sharding import PartitionSpec as P

HEADS = 8
EPS = 1e-05
LANES = 128
BLOCK_ROWS = 64
BLOCK_COLUMNS = 256

VMEM = pl.BlockSpec(memory_space=pltpu.VMEM)
SMEM = pl.BlockSpec(memory_space=pltpu.SMEM)
HBM = pl.BlockSpec(memory_space=pltpu.HBM)
f32 = jnp.float32
bf16 = jnp.bfloat16


def room(mib):
    return pltpu.CompilerParams(vmem_limit_bytes=mib * 1024 * 1024)


def estimate(microseconds):
    return pl.CostEstimate(flops=0, bytes_accessed=microseconds * 3_500_000, transcendentals=0)


def matmul(left, right):
    return lax.dot_general(left, right, (((1,), (0,)), ((), ())), preferred_element_type=f32)


def matmul_nt(left, right):
    return lax.dot_general(left, right, (((1,), (1,)), ((), ())), preferred_element_type=f32)


def matmul_tn(left, right):
    return lax.dot_general(left, right, (((0,), (0,)), ((), ())), preferred_element_type=f32)


def sigmoid(value):
    return 0.5 * jnp.tanh(0.5 * value) + 0.5


def bal_swap(value, step, count):
    return lax.ppermute(value, "bal", [(i, i ^ step) for i in range(count)])


def with_swapped(value, count):
    return [value] + [bal_swap(value, turn, count) for turn in range(1, count)]


def emb_swap(value, step, count):
    return lax.ppermute(value, "emb", [(i, i ^ step) for i in range(count)])


class Scalars:
    def __init__(self, ref, step, bals, slots):
        self.ref, self.step, self.bals, self.slots = ref, step, bals, slots

    def surplus(self, bal):
        return self.ref[self.step, bal]

    def source(self, bal):
        found = jnp.int32(0)
        for index in range(self.bals):
            found = found + jnp.where(self.ref[self.step, self.bals + index] == bal, index, 0)
        return found

    def length(self, bal, slot):
        return self.ref[self.step, 2 * self.bals + bal * self.slots + slot]

    def place(self):
        first = self.bals * (2 + self.slots)
        return self.ref[self.step, first], self.ref[self.step, first + 1], self.ref[self.step, first + 2]


def pick_ids(scalars, ids_refs, slots, tables):
    bal, group_here, _ = scalars[0].place()
    found = []
    for step, there in enumerate(scalars):
        group = group_here ^ step
        my_slot = there.surplus(bal)
        source = there.source(bal)
        from_slot = there.surplus(source)
        by_slot = [[] for _ in range(slots)]
        for table in tables:
            arrived = ids_refs[0][table, group * slots + from_slot]
            for turn in range(1, len(ids_refs)):
                other = ids_refs[turn][table, group * slots + from_slot]
                arrived = jnp.where(source ^ bal == turn, other, arrived)
            for slot in range(slots):
                own = ids_refs[0][table, group * slots + slot]
                by_slot[slot].append(jnp.where(my_slot == slot, arrived, own))
        found.append(by_slot)
    return found


def table_order(table_here, tables):
    return [table_here ^ step for step in range(tables)]


def lookup_kernel(groups, slots, tables, bals, *refs):
    refs = list(refs)
    take = lambda count: [refs.pop(0) for _ in range(count)]
    (scalar_ref,) = take(1)
    scalars = [Scalars(scalar_ref, step, bals, slots) for step in range(groups)]
    ids_refs = take(bals)
    pieces = [take(bals) for _ in range(tables)]
    out_refs = refs
    bal, _, table_here = scalars[0].place()
    part, columns = pieces[0][0].shape
    slot_rows = ids_refs[0].shape[3]
    lane = lax.broadcasted_iota(jnp.int32, (LANES, LANES), 1)
    ids = pick_ids(scalars, ids_refs, slots, table_order(table_here, tables))
    rows = out_refs[0].shape[0]
    total = jnp.zeros((groups * rows, columns), f32)
    for table in range(tables):
        found = []
        for group in range(groups):
            for slot in range(slots):
                for first in range(0, slot_rows, LANES):
                    row = ids[group][slot][table][:, first : first + LANES]
                    found.append(jnp.transpose(jnp.broadcast_to(row, (LANES, LANES))))
        column = jnp.concatenate(found, axis=0)
        for turn, ref in enumerate(pieces[table]):
            shifted = column - (bal ^ turn) * part
            hot = []
            for at in range(0, part, LANES):
                here = [shifted[row : row + LANES] == lane + at for row in range(0, groups * rows, LANES)]
                here = [jnp.where(one, 1.0, 0.0).astype(bf16) for one in here]
                hot.append(jnp.concatenate(here, axis=0))
            total = total + matmul(jnp.concatenate(hot, axis=1), ref[...])
    for group in range(groups):
        out_refs[group][...] = total[group * rows : (group + 1) * rows].astype(bf16)


def scatter_kernel(groups, slots, bals, *refs):
    refs = list(refs)
    take = lambda count: [refs.pop(0) for _ in range(count)]
    (scalar_ref,) = take(1)
    scalars = [Scalars(scalar_ref, step, bals, slots) for step in range(groups)]
    ids_refs, grad_refs, out_refs = take(bals), take(groups)[::-1], refs
    bal, _, table_here = scalars[0].place()
    tables, part, _ = out_refs[0].shape
    slot_rows = ids_refs[0].shape[3]
    height = min(part, 256)
    iota = lax.broadcasted_iota(jnp.int32, (height, slot_rows), 0)
    ids = pick_ids(scalars, ids_refs, slots, table_order(table_here, tables))
    columns = out_refs[0].shape[2]

    def rows_of(ref):
        height = ref.shape[0]
        first = ref.shape[1] - slots * slot_rows // height * columns
        return [ref[:, at : at + columns] for at in range(first, ref.shape[1], columns)]

    grads = jnp.concatenate([piece for ref in grad_refs for piece in rows_of(ref)], axis=0)
    for table in range(tables):
        for turn in range(bals):
            for at in range(0, part, height):
                start = (bal ^ turn) * part + at
                hot = jnp.concatenate(
                    [
                        jnp.where(iota == ids[group][slot][table] - start, 1.0, 0.0).astype(bf16)
                        for group in range(groups)
                        for slot in range(slots)
                    ],
                    axis=1,
                )
                out_refs[turn][table, at : at + height, :] = matmul(hot, grads).astype(bf16)


def norm(values):
    average = jnp.mean(values, axis=1, keepdims=True)
    centred = values - average
    inverse = lax.rsqrt(jnp.mean(centred * centred, axis=1, keepdims=True) + EPS)
    return centred * inverse, inverse


def norm_back(incoming, normed, inverse):
    first = jnp.mean(incoming, axis=1, keepdims=True)
    second = jnp.mean(incoming * normed, axis=1, keepdims=True)
    return inverse * (incoming - first - normed * second)


def times_parts_nt(value, weight_refs, first, last, bal, wide_ref):
    for turn, ref in enumerate(weight_refs):
        wide_ref[bal ^ turn] = matmul_nt(value, ref[:, first:last])
    return jnp.concatenate([wide_ref[index] for index in range(len(weight_refs))], axis=1)


def layer_kernel(groups, slots, tables, bals, unit, scalar_ref, *refs):
    refs = list(refs)
    take = lambda count: [refs.pop(0) for _ in range(count)]
    block_refs = take(groups)[::-1]
    weight_refs = take(bals)
    (cot_ref,) = take(1)
    grads_ref, normed_ref, inverse_ref, keep_mixed_ref = take(4)
    term_refs = take(bals)
    (x_ref, halves_ref, wide_ref, nt_ref, mt_ref, weights_ref, slope_ref, gate_ref, heads_ref, dsilu_ref, out_ref, mixed_ref, back_ref) = refs

    scalars = Scalars(scalar_ref, 0, bals, slots)
    bal, group_here, table_here = scalars.place()
    rows, width = cot_ref.shape
    slot_rows = rows // slots
    head_width = width // HEADS
    score_scale = head_width**-0.5
    piece = block_refs[0].shape[1]
    part, features = weight_refs[0].shape[0], weight_refs[0].shape[1] - width

    blocks = [slice(at, at + BLOCK_ROWS) for at in range(0, rows, BLOCK_ROWS)]

    def keep_parts(here, value):
        for index in range(bals):
            halves_ref[index, here, :] = value[:, index * part : (index + 1) * part].astype(bf16)

    def times_parts(first, last):
        found = matmul(halves_ref[bal], weight_refs[0][:, first:last])
        for turn in range(1, bals):
            found = found + matmul(halves_ref[bal ^ turn], weight_refs[turn][:, first:last])
        return found

    my_slot = scalars.surplus(bal)
    source = scalars.source(bal)
    moved = scalars.length(source, scalars.surplus(source))
    lengths = [jnp.where(my_slot == slot, moved, scalars.length(bal, slot)) for slot in range(slots)]

    for step in range(groups):
        x_ref[group_here ^ step] = block_refs[step][...]

    def x_rows(here):
        return jnp.concatenate([x_ref[group, here, :] for group in range(groups)], axis=1).astype(f32)

    for here in blocks:
        normed, inverse = norm(x_rows(here))
        normed_ref[here, :] = normed
        inverse_ref[here, :] = jnp.broadcast_to(inverse, (BLOCK_ROWS, inverse_ref.shape[1]))
        keep_parts(here, normed)
    for at in range(0, features, width):
        dsilu_ref[:, at : at + width] = times_parts(at, at + width)
        for here in blocks:
            for first in range(at, at + width, BLOCK_COLUMNS):
                columns = slice(first, first + BLOCK_COLUMNS)
                projected = dsilu_ref[here, columns]
                logistic = sigmoid(projected)
                active = projected * logistic
                dsilu_ref[here, columns] = logistic + active * (1.0 - logistic)
                if at < width:
                    gate_ref[here, columns] = active
                else:
                    heads_ref[here, first - width : first - width + BLOCK_COLUMNS] = active.astype(bf16)
    nt_ref[...] = jnp.transpose(normed_ref[...]).astype(bf16)

    pair_width = 2 * head_width
    low = lax.broadcasted_iota(jnp.int32, (slot_rows, pair_width), 1) < head_width
    row_at = lax.broadcasted_iota(jnp.int32, (slot_rows, slot_rows), 0)
    col_at = lax.broadcasted_iota(jnp.int32, (slot_rows, slot_rows), 1)

    def split(value):
        zero = jnp.zeros_like(value)
        return jnp.concatenate([jnp.where(low, value, zero), jnp.where(low, zero, value)], axis=0)

    def side_by_side(value):
        return jnp.concatenate([value[:slot_rows], value[slot_rows:]], axis=1)

    def part_of(slot, pair, which):
        first = which * width + pair * pair_width
        return heads_ref[slot * slot_rows : (slot + 1) * slot_rows, first : first + pair_width]

    pairs = HEADS // 2
    for slot in range(slots):
        live = (col_at <= row_at) & (row_at < lengths[slot])
        allowed = jnp.where(live, 1.0 / slot_rows, 0.0)
        slot_here = slice(slot * slot_rows, (slot + 1) * slot_rows)
        for pair in range(pairs):
            value, query, key = (part_of(slot, pair, which) for which in range(3))
            scores = matmul_nt(split(query), key) * score_scale
            both = []
            for head in range(2):
                half = slice(head * slot_rows, (head + 1) * slot_rows)
                q = sigmoid(scores[half])
                sq = scores[half] * q
                both.append((sq * allowed).astype(bf16))
                weights_ref[slot * pairs + pair, half, :] = both[-1]
                slope_ref[slot * pairs + pair, half, :] = allowed * (q + sq * (1.0 - q))
            lanes = slice(pair * pair_width, (pair + 1) * pair_width)
            out_ref[slot_here, lanes] = matmul(jnp.concatenate(both, axis=1), split(value))

    cot = cot_ref[...].astype(bf16)
    mixed_ref[...] = times_parts_nt(cot, weight_refs, features, features + width, bal, wide_ref)
    for here in blocks:
        normed, inverse = norm(out_ref[here, :])
        gate = gate_ref[here, :]
        grad_mixed = mixed_ref[here, :]
        back_ref[here, :] = norm_back(grad_mixed * gate, normed, inverse).astype(bf16)
        grads_ref[here, :width] = (grad_mixed * normed * dsilu_ref[here, :width]).astype(bf16)
        mixed = normed * gate
        mixed_ref[here, :] = mixed
        keep_mixed_ref[here, :] = mixed.astype(bf16)
    mt_ref[...] = jnp.transpose(mixed_ref[...]).astype(bf16)

    def owner_order(ref, turn):
        start = (bal ^ turn) * part
        if part != groups * tables * unit:
            return ref[pl.ds(pl.multiple_of(start, part), part), :]
        found = []
        for group_step in range(groups):
            for table_step in range(tables):
                owner = (group_here ^ group_step) * tables + (table_here ^ table_step)
                at = pl.multiple_of(start + owner * unit, unit)
                found.append(ref[pl.ds(at, unit), :])
        return jnp.concatenate(found, axis=0)

    def emit_terms(ref, right, first):
        left = jnp.concatenate([owner_order(ref, turn) for turn in range(bals)], axis=0)
        found = matmul(left, right).astype(bf16)
        for turn in range(bals):
            rows_here = slice(turn * part, (turn + 1) * part)
            term_refs[turn][:, first : first + right.shape[1]] = found[rows_here]

    emit_terms(mt_ref, cot, features)

    for slot in range(slots):
        here = slice(slot * slot_rows, (slot + 1) * slot_rows)
        for pair in range(pairs):
            value, query, key = (part_of(slot, pair, which) for which in range(3))
            lanes = slice(pair * pair_width, (pair + 1) * pair_width)
            upper = split(back_ref[here, lanes])
            grad_weights = matmul_nt(upper, value)
            grad_scores = (grad_weights * slope_ref[slot * pairs + pair]).astype(bf16)
            grad_value = matmul_tn(weights_ref[slot * pairs + pair], upper)
            grad_query = matmul(side_by_side(grad_scores), split(key)) * score_scale
            grad_key = matmul_tn(grad_scores, split(query)) * score_scale
            for which, found in enumerate((grad_value, grad_query, grad_key)):
                first = (1 + which) * width + pair * pair_width
                at = slice(first, first + pair_width)
                grads_ref[here, at] = (found * dsilu_ref[here, at]).astype(bf16)

    emit_terms(nt_ref, grads_ref[...], 0)


def rows_kernel(groups, slots, bals, scalar_ref, *refs):
    refs = list(refs)
    take = lambda count: [refs.pop(0) for _ in range(count)]
    grads_ref, normed_ref, inverse_ref, mixed_ref, cot_ref = take(5)
    weight_refs, block_refs = take(bals), take(groups)
    (layer_ref,) = take(1)
    grad_refs = take(groups)
    x_ref, wide_ref, halves_ref = refs
    bal, group_here, _ = Scalars(scalar_ref, 0, bals, slots).place()
    features = grads_ref.shape[1]
    piece = grad_refs[0].shape[1]
    part = weight_refs[0].shape[0]
    for step in range(groups):
        x_ref[group_here ^ step] = block_refs[step][...]
    x = jnp.concatenate([x_ref[group] for group in range(groups)], axis=1).astype(f32)
    for index in range(bals):
        halves_ref[index] = mixed_ref[:, index * part : (index + 1) * part]
    for turn in range(bals):
        x = x + matmul(halves_ref[bal ^ turn], weight_refs[turn][:, features:])
    layer_ref[...] = x.astype(bf16)
    grad_normed = times_parts_nt(grads_ref[...], weight_refs, 0, features, bal, wide_ref)
    back = norm_back(grad_normed, normed_ref[...], inverse_ref[:, :1])
    grad_rows = (cot_ref[...] + back).astype(bf16)
    for group in range(groups):
        x_ref[group] = grad_rows[:, group * piece : (group + 1) * piece]
    for step in range(groups):
        grad_refs[step][...] = x_ref[group_here ^ step]


def pieces_kernel(bals, *refs):
    count = len(refs) - bals
    groups = (count + 1) // 2
    term_refs, grad_refs = refs[:bals], refs[bals : bals + groups - 1]
    out_refs = refs[bals + groups - 1 :]
    height, width = out_refs[0].shape
    for step, out in enumerate(out_refs):
        rows = slice(step * height, (step + 1) * height)
        total = term_refs[0][rows, :].astype(f32)
        for ref in term_refs[1:]:
            total = total + ref[rows, :].astype(f32)
        out[:, :width] = total.astype(bf16)
        if step:
            grad = grad_refs[step - 1]
            columns = grad.shape[1]
            for index in range(grad.shape[0] // height):
                at = width + index * columns
                out[:, at : at + columns] = grad[index * height : (index + 1) * height, :]


def place_kernel(scale, steps, slots, tables, bals, unit, scalar_ref, *refs):
    pieces = refs[: len(steps)]
    in_ref, out_ref, scaled_ref, sems = refs[-4:]
    _, group_here, table_here = Scalars(scalar_ref, 0, bals, slots).place()
    features = in_ref.shape[1]
    copies = []
    height = tables * unit
    for number, (group_step, piece) in enumerate(zip(steps, pieces)):
        for table_step in range(tables):
            to = pl.multiple_of(number * height + (table_here ^ table_step) * unit, unit)
            value = piece[table_step * unit : (table_step + 1) * unit, :]
            scaled_ref[pl.ds(to, unit), :] = value.astype(f32) * scale
        from_rows = scaled_ref.at[pl.ds(number * height, height), :]
        to = pl.ds(pl.multiple_of((group_here ^ group_step) * height, height), height)
        for index, (first, out) in enumerate(((0, in_ref), (features, out_ref))):
            copies.append(
                pltpu.make_async_copy(
                    from_rows.at[:, pl.ds(first, out.shape[1])], out.at[to, :], sems.at[number, index]
                )
            )
            copies[-1].start()
    for copy in copies:
        copy.wait()


def sum_rounded(terms):
    total = terms[0].astype(f32)
    for term in terms[1:]:
        total = total + term.astype(f32)
    return total.astype(bf16)


def after(value, *others):
    return lax.optimization_barrier((value,) + others)[0]


def on_device(
    item_ids, seq_lengths, surplus_slot, helper_map, embed_tables, weight_in, weight_out, cotangent
):
    bal = lax.axis_index("bal")
    emb = lax.axis_index("emb")
    bals = lax.axis_size("bal")
    embs = lax.axis_size("emb")
    tables = item_ids.shape[2]
    groups = embs // tables
    _, rows, width = cotangent.shape
    slots = seq_lengths.shape[2]
    slot_rows = rows // slots
    distinct, columns = embed_tables.shape[1:]
    part = distinct // bals
    weight_part = weight_in.shape[0]
    table_here = emb // groups
    group_here = emb % groups
    width, features = weight_out.shape[1], weight_in.shape[1]
    unit = weight_part // embs
    owned = unit % 16 == 0
    unit = unit if owned else 0
    first = bals * (2 + slots)
    lane = lax.broadcasted_iota(jnp.int32, (1, LANES), 1)
    scalars = jnp.where(lane == first, bal, 0)
    scalars = jnp.where(lane == first + 1, group_here, scalars)
    scalars = jnp.where(lane == first + 2, table_here, scalars)
    fields = [surplus_slot.T, helper_map.T] + [seq_lengths[index] for index in range(bals)]
    at = 0
    for field in fields:
        width_here = field.shape[1]
        scalars = scalars + jnp.pad(field, ((0, 0), (at, LANES - at - width_here)))
        at += width_here

    share = lax.dynamic_slice_in_dim(embed_tables[0], bal * part, part, 0)
    fetched = [emb_swap(share, step * groups, embs) for step in range(1, tables)]

    ids = lax.dynamic_slice_in_dim(
        jnp.transpose(after(item_ids[0], share)), table_here * groups * rows, groups * rows, 1
    )
    plane_ids = with_swapped(ids.reshape(tables, groups * slots, 1, slot_rows), bals)
    wide_cot = cotangent[0].astype(f32)
    scalars = after(scalars, share)
    for bit in range((groups - 1).bit_length()):
        scalars = jnp.concatenate([scalars, emb_swap(scalars, 1 << bit, embs)], axis=0)
        scalars = after(scalars, wide_cot)

    fetched[0] = after(fetched[0], scalars)
    pieces = [piece for one in [share] + fetched for piece in with_swapped(one, bals)]

    found = pl.pallas_call(
        functools.partial(lookup_kernel, groups, slots, tables, bals),
        out_shape=[jax.ShapeDtypeStruct((rows, columns), bf16)] * groups,
        in_specs=[SMEM] + [VMEM] * (bals + len(pieces)),
        out_specs=[VMEM] * groups,
        cost_estimate=estimate(3),
        compiler_params=room(16),
    )(scalars, *plane_ids, *pieces)
    weights = jnp.concatenate([weight_in, weight_out], axis=1)
    weights = with_swapped(after(weights, found[0]), bals)
    block = [found[0]] + [emb_swap(found[step], step, embs) for step in range(1, groups)]

    pairs = slots * HEADS // 2
    terms = jax.ShapeDtypeStruct((weight_part, features + width), bf16)
    results = pl.pallas_call(
        functools.partial(layer_kernel, groups, slots, tables, bals, unit),
        out_shape=[jax.ShapeDtypeStruct((rows, features), bf16)]
        + [jax.ShapeDtypeStruct((rows, columns_here), f32) for columns_here in (width, LANES)]
        + [jax.ShapeDtypeStruct((rows, width), bf16)]
        + [terms] * bals,
        in_specs=[SMEM] + [VMEM] * (groups + bals + 1),
        out_specs=[VMEM] * (4 + bals),
        scratch_shapes=[
            pltpu.VMEM((groups, rows, columns), bf16),
            pltpu.VMEM((bals, rows, weight_part), bf16),
            pltpu.VMEM((bals, rows, weight_part), f32),
            pltpu.VMEM((width, rows), bf16),
            pltpu.VMEM((width, rows), bf16),
            pltpu.VMEM((pairs, 2 * slot_rows, slot_rows), bf16),
            pltpu.VMEM((pairs, 2 * slot_rows, slot_rows), f32),
            pltpu.VMEM((rows, width), f32),
            pltpu.VMEM((rows, features - width), bf16),
            pltpu.VMEM((rows, features), f32),
            pltpu.VMEM((rows, width), f32),
            pltpu.VMEM((rows, width), f32),
            pltpu.VMEM((rows, width), bf16),
        ],
        cost_estimate=estimate(7),
        compiler_params=room(36),
    )(scalars, *block[::-1], *weights, wide_cot)
    for_rows, results = results[:4], results[4:]
    layer_out, *grads = pl.pallas_call(
        functools.partial(rows_kernel, groups, slots, bals),
        out_shape=[jax.ShapeDtypeStruct((rows, width), bf16)]
        + [jax.ShapeDtypeStruct((rows, columns), bf16)] * groups,
        in_specs=[SMEM] + [VMEM] * (5 + bals + groups),
        out_specs=[VMEM] * (1 + groups),
        scratch_shapes=[
            pltpu.VMEM((groups, rows, columns), bf16),
            pltpu.VMEM((bals, rows, weight_part), f32),
            pltpu.VMEM((bals, rows, weight_part), bf16),
        ],
        cost_estimate=estimate(2),
        compiler_params=room(16),
    )(scalars, *for_rows, wide_cot, *weights, *block)

    def over_cores(parts):
        return sum_rounded([parts[0]] + [bal_swap(parts[turn], turn, bals) for turn in range(1, bals)])

    def to_plane(value):
        return [value] + [emb_swap(value, step, embs) for step in range(1, groups)]

    def table_sums(plane_grads):
        return pl.pallas_call(
            functools.partial(scatter_kernel, groups, slots, bals),
            out_shape=[jax.ShapeDtypeStruct((tables, part, columns), bf16)] * bals,
            in_specs=[SMEM] + [VMEM] * (bals + groups),
            out_specs=[VMEM] * bals,
            cost_estimate=estimate(3),
            compiler_params=room(16),
        )(scalars, *plane_ids, *plane_grads[::-1])

    grad_scale = (rows * embs * bals) ** -0.5
    if owned:
        height, wide = weight_part // groups, features + width
        terms = [results[0]] + [bal_swap(results[turn], turn, bals) for turn in range(1, bals)]
        pieces = pl.pallas_call(
            functools.partial(pieces_kernel, bals),
            out_shape=[jax.ShapeDtypeStruct((height, wide), bf16)]
            + [jax.ShapeDtypeStruct((height, wide + rows // height * columns), bf16)] * (groups - 1),
            in_specs=[VMEM] * (bals + groups - 1),
            out_specs=[VMEM] * groups,
            compiler_params=room(12),
        )(*terms, *grads[1:])
        came = [emb_swap(pieces[step], step, embs) for step in range(1, groups)]
        mine = sum_rounded([value[:, :wide] for value in came[::-1]] + [pieces[0]])
        mine = mine.reshape(tables, unit, wide)
        sums = table_sums([grads[0]] + came)
        own_sums = over_cores(sums)
        came = [emb_swap(mine[step], step * groups, embs) for step in range(1, tables)]
        final = sum_rounded(came[-1:] + came[:-1] + [mine[0]])
        gathered = [final] + [emb_swap(final, step * groups, embs) for step in range(1, tables)]
        back = to_plane(jnp.concatenate(gathered, axis=0))
        later = after(own_sums, *gathered[1:])
        swapped = [emb_swap(later[step], step * groups, embs) for step in range(1, tables)]
        swapped = [after(value, *back[1:]) for value in swapped]
    else:
        sums = table_sums([grads[0]] + [emb_swap(grads[step], step, embs) for step in range(1, groups)])
        own_sums = over_cores(sums)
        swapped = [emb_swap(own_sums[step], step * groups, embs) for step in range(1, tables)]
    table_sum = swapped[-1].astype(f32)
    for value in swapped[:-1] + [own_sums[0]]:
        table_sum = table_sum + value.astype(f32)
    table_scale = (distinct / (bals * item_ids.shape[1])) ** 0.5

    if owned:
        totals = []
        for steps in ([0] + list(range(groups - 1, 1, -1))[: groups // 2 - 1], None):
            steps = steps or [step for step in range(1, groups) if step not in done]
            done = steps
            totals = pl.pallas_call(
                functools.partial(place_kernel, grad_scale, steps, slots, tables, bals, unit),
                out_shape=[
                    jax.ShapeDtypeStruct((weight_part, features), f32),
                    jax.ShapeDtypeStruct((weight_part, width), f32),
                ],
                in_specs=[SMEM] + [VMEM] * len(steps) + [HBM] * len(totals),
                out_specs=[HBM] * 2,
                scratch_shapes=[
                    pltpu.VMEM((len(steps) * tables * unit, features + width), f32),
                    pltpu.SemaphoreType.DMA((len(steps), 2)),
                ],
                input_output_aliases={1 + len(steps) + index: index for index in range(len(totals))},
                cost_estimate=estimate(1),
                compiler_params=room(12),
            )(scalars, *[back[step] for step in steps], *totals)
        total_in, total_out = totals
    else:
        total = lax.psum(over_cores(results).astype(f32), "emb") * grad_scale
        total_in, total_out = total[:, :features], total[:, features:]

    return layer_out[None], (table_sum * table_scale)[None], total_in, total_out


def solution(mesh):
    placed = (
        P("bal", None, None),
        P(None, "emb", None),
        P(None, "emb"),
        P(None, "emb"),
        P("emb", None, None),
        P("bal", None),
        P("bal", None),
        P("bal", "emb", None),
    )
    return jax.shard_map(
        on_device,
        mesh=mesh,
        in_specs=placed,
        out_specs=(P("bal", "emb", None), P("emb", "bal", None), P("bal", None), P("bal", None)),
        check_vma=False,
    )
```

```python
import functools

import jax
import jax.numpy as jnp
from jax import lax
from jax.experimental import pallas as pl
from jax.experimental.pallas import tpu as pltpu
from jax.sharding import PartitionSpec as P

HEADS = 8
EPS = 1e-05
LANES = 128
BLOCK_ROWS = 64
BLOCK_COLUMNS = 256

VMEM = pl.BlockSpec(memory_space=pltpu.VMEM)
SMEM = pl.BlockSpec(memory_space=pltpu.SMEM)
HBM = pl.BlockSpec(memory_space=pltpu.HBM)
f32 = jnp.float32
bf16 = jnp.bfloat16


def room(mib):
    return pltpu.CompilerParams(vmem_limit_bytes=mib * 1024 * 1024)


def estimate(microseconds):
    return pl.CostEstimate(flops=0, bytes_accessed=microseconds * 3_500_000, transcendentals=0)


def matmul(left, right):
    return lax.dot_general(left, right, (((1,), (0,)), ((), ())), preferred_element_type=f32)


def matmul_nt(left, right):
    return lax.dot_general(left, right, (((1,), (1,)), ((), ())), preferred_element_type=f32)


def matmul_tn(left, right):
    return lax.dot_general(left, right, (((0,), (0,)), ((), ())), preferred_element_type=f32)


def sigmoid(value):
    return 0.5 * jnp.tanh(0.5 * value) + 0.5


def bal_swap(value, step, count):
    return lax.ppermute(value, "bal", [(i, i ^ step) for i in range(count)])


def with_swapped(value, count):
    return [value] + [bal_swap(value, turn, count) for turn in range(1, count)]


def emb_swap(value, step, count):
    return lax.ppermute(value, "emb", [(i, i ^ step) for i in range(count)])


class Scalars:
    def __init__(self, ref, step, bals, slots):
        self.ref, self.step, self.bals, self.slots = ref, step, bals, slots

    def surplus(self, bal):
        return self.ref[self.step, bal]

    def source(self, bal):
        found = jnp.int32(0)
        for index in range(self.bals):
            found = found + jnp.where(self.ref[self.step, self.bals + index] == bal, index, 0)
        return found

    def length(self, bal, slot):
        return self.ref[self.step, 2 * self.bals + bal * self.slots + slot]

    def place(self):
        first = self.bals * (2 + self.slots)
        return self.ref[self.step, first], self.ref[self.step, first + 1], self.ref[self.step, first + 2]


def pick_ids(scalars, ids_refs, slots, tables):
    bal, group_here, _ = scalars[0].place()
    found = []
    for step, there in enumerate(scalars):
        group = group_here ^ step
        my_slot = there.surplus(bal)
        source = there.source(bal)
        from_slot = there.surplus(source)
        by_slot = [[] for _ in range(slots)]
        for table in tables:
            arrived = ids_refs[0][table, group * slots + from_slot]
            for turn in range(1, len(ids_refs)):
                other = ids_refs[turn][table, group * slots + from_slot]
                arrived = jnp.where(source ^ bal == turn, other, arrived)
            for slot in range(slots):
                own = ids_refs[0][table, group * slots + slot]
                by_slot[slot].append(jnp.where(my_slot == slot, arrived, own))
        found.append(by_slot)
    return found


def table_order(table_here, tables):
    return [table_here ^ step for step in range(tables)]


def lookup_kernel(groups, slots, tables, bals, *refs):
    refs = list(refs)
    take = lambda count: [refs.pop(0) for _ in range(count)]
    (scalar_ref,) = take(1)
    scalars = [Scalars(scalar_ref, step, bals, slots) for step in range(groups)]
    ids_refs = take(bals)
    pieces = [take(bals) for _ in range(tables)]
    out_refs = refs
    bal, _, table_here = scalars[0].place()
    part, columns = pieces[0][0].shape
    slot_rows = ids_refs[0].shape[3]
    lane = lax.broadcasted_iota(jnp.int32, (LANES, LANES), 1)
    ids = pick_ids(scalars, ids_refs, slots, table_order(table_here, tables))
    rows = out_refs[0].shape[0]
    total = jnp.zeros((groups * rows, columns), f32)
    for table in range(tables):
        found = []
        for group in range(groups):
            for slot in range(slots):
                for first in range(0, slot_rows, LANES):
                    row = ids[group][slot][table][:, first : first + LANES]
                    found.append(jnp.transpose(jnp.broadcast_to(row, (LANES, LANES))))
        column = jnp.concatenate(found, axis=0)
        for turn, ref in enumerate(pieces[table]):
            shifted = column - (bal ^ turn) * part
            hot = []
            for at in range(0, part, LANES):
                here = [shifted[row : row + LANES] == lane + at for row in range(0, groups * rows, LANES)]
                here = [jnp.where(one, 1.0, 0.0).astype(bf16) for one in here]
                hot.append(jnp.concatenate(here, axis=0))
            total = total + matmul(jnp.concatenate(hot, axis=1), ref[...])
    for group in range(groups):
        out_refs[group][...] = total[group * rows : (group + 1) * rows].astype(bf16)


def scatter_kernel(groups, slots, bals, *refs):
    refs = list(refs)
    take = lambda count: [refs.pop(0) for _ in range(count)]
    (scalar_ref,) = take(1)
    scalars = [Scalars(scalar_ref, step, bals, slots) for step in range(groups)]
    ids_refs, grad_refs, out_refs = take(bals), take(groups)[::-1], refs
    bal, _, table_here = scalars[0].place()
    tables, part, _ = out_refs[0].shape
    slot_rows = ids_refs[0].shape[3]
    height = min(part, 256)
    iota = lax.broadcasted_iota(jnp.int32, (height, slot_rows), 0)
    ids = pick_ids(scalars, ids_refs, slots, table_order(table_here, tables))
    columns = out_refs[0].shape[2]

    def rows_of(ref):
        height = ref.shape[0]
        first = ref.shape[1] - slots * slot_rows // height * columns
        return [ref[:, at : at + columns] for at in range(first, ref.shape[1], columns)]

    grads = jnp.concatenate([piece for ref in grad_refs for piece in rows_of(ref)], axis=0)
    for table in range(tables):
        for turn in range(bals):
            for at in range(0, part, height):
                start = (bal ^ turn) * part + at
                hot = jnp.concatenate(
                    [
                        jnp.where(iota == ids[group][slot][table] - start, 1.0, 0.0).astype(bf16)
                        for group in range(groups)
                        for slot in range(slots)
                    ],
                    axis=1,
                )
                out_refs[turn][table, at : at + height, :] = matmul(hot, grads).astype(bf16)


def norm(values):
    average = jnp.mean(values, axis=1, keepdims=True)
    centred = values - average
    inverse = lax.rsqrt(jnp.mean(centred * centred, axis=1, keepdims=True) + EPS)
    return centred * inverse, inverse


def norm_back(incoming, normed, inverse):
    first = jnp.mean(incoming, axis=1, keepdims=True)
    second = jnp.mean(incoming * normed, axis=1, keepdims=True)
    return inverse * (incoming - first - normed * second)


def times_parts_nt(value, weight_refs, first, last, bal, wide_ref):
    for turn, ref in enumerate(weight_refs):
        wide_ref[bal ^ turn] = matmul_nt(value, ref[:, first:last])
    return jnp.concatenate([wide_ref[index] for index in range(len(weight_refs))], axis=1)


def layer_kernel(groups, slots, tables, bals, unit, scalar_ref, *refs):
    refs = list(refs)
    take = lambda count: [refs.pop(0) for _ in range(count)]
    block_refs = take(groups)[::-1]
    weight_refs = take(bals)
    (cot_ref,) = take(1)
    grads_ref, normed_ref, inverse_ref, keep_mixed_ref = take(4)
    term_refs = take(bals)
    (x_ref, halves_ref, wide_ref, nt_ref, mt_ref, weights_ref, slope_ref, gate_ref, heads_ref, dsilu_ref, out_ref, mixed_ref, back_ref) = refs

    scalars = Scalars(scalar_ref, 0, bals, slots)
    bal, group_here, table_here = scalars.place()
    rows, width = cot_ref.shape
    slot_rows = rows // slots
    head_width = width // HEADS
    score_scale = head_width**-0.5
    piece = block_refs[0].shape[1]
    part, features = weight_refs[0].shape[0], weight_refs[0].shape[1] - width

    blocks = [slice(at, at + BLOCK_ROWS) for at in range(0, rows, BLOCK_ROWS)]

    def keep_parts(here, value):
        for index in range(bals):
            halves_ref[index, here, :] = value[:, index * part : (index + 1) * part].astype(bf16)

    def times_parts(first, last):
        found = matmul(halves_ref[bal], weight_refs[0][:, first:last])
        for turn in range(1, bals):
            found = found + matmul(halves_ref[bal ^ turn], weight_refs[turn][:, first:last])
        return found

    my_slot = scalars.surplus(bal)
    source = scalars.source(bal)
    moved = scalars.length(source, scalars.surplus(source))
    lengths = [jnp.where(my_slot == slot, moved, scalars.length(bal, slot)) for slot in range(slots)]

    for step in range(groups):
        x_ref[group_here ^ step] = block_refs[step][...]

    def x_rows(here):
        return jnp.concatenate([x_ref[group, here, :] for group in range(groups)], axis=1).astype(f32)

    for here in blocks:
        normed, inverse = norm(x_rows(here))
        normed_ref[here, :] = normed
        inverse_ref[here, :] = jnp.broadcast_to(inverse, (BLOCK_ROWS, inverse_ref.shape[1]))
        keep_parts(here, normed)
    for at in range(0, features, width):
        dsilu_ref[:, at : at + width] = times_parts(at, at + width)
        for here in blocks:
            for first in range(at, at + width, BLOCK_COLUMNS):
                columns = slice(first, first + BLOCK_COLUMNS)
                projected = dsilu_ref[here, columns]
                logistic = sigmoid(projected)
                active = projected * logistic
                dsilu_ref[here, columns] = logistic + active * (1.0 - logistic)
                if at < width:
                    gate_ref[here, columns] = active
                else:
                    heads_ref[here, first - width : first - width + BLOCK_COLUMNS] = active.astype(bf16)
    nt_ref[...] = jnp.transpose(normed_ref[...]).astype(bf16)

    pair_width = 2 * head_width
    low = lax.broadcasted_iota(jnp.int32, (slot_rows, pair_width), 1) < head_width
    row_at = lax.broadcasted_iota(jnp.int32, (slot_rows, slot_rows), 0)
    col_at = lax.broadcasted_iota(jnp.int32, (slot_rows, slot_rows), 1)

    def split(value):
        zero = jnp.zeros_like(value)
        return jnp.concatenate([jnp.where(low, value, zero), jnp.where(low, zero, value)], axis=0)

    def side_by_side(value):
        return jnp.concatenate([value[:slot_rows], value[slot_rows:]], axis=1)

    def part_of(slot, pair, which):
        first = which * width + pair * pair_width
        return heads_ref[slot * slot_rows : (slot + 1) * slot_rows, first : first + pair_width]

    pairs = HEADS // 2
    for slot in range(slots):
        live = (col_at <= row_at) & (row_at < lengths[slot])
        allowed = jnp.where(live, 1.0 / slot_rows, 0.0)
        slot_here = slice(slot * slot_rows, (slot + 1) * slot_rows)
        for pair in range(pairs):
            value, query, key = (part_of(slot, pair, which) for which in range(3))
            scores = matmul_nt(split(query), key) * score_scale
            both = []
            for head in range(2):
                half = slice(head * slot_rows, (head + 1) * slot_rows)
                q = sigmoid(scores[half])
                sq = scores[half] * q
                both.append((sq * allowed).astype(bf16))
                weights_ref[slot * pairs + pair, half, :] = both[-1]
                slope_ref[slot * pairs + pair, half, :] = allowed * (q + sq * (1.0 - q))
            lanes = slice(pair * pair_width, (pair + 1) * pair_width)
            out_ref[slot_here, lanes] = matmul(jnp.concatenate(both, axis=1), split(value))

    cot = cot_ref[...].astype(bf16)
    mixed_ref[...] = times_parts_nt(cot, weight_refs, features, features + width, bal, wide_ref)
    for here in blocks:
        normed, inverse = norm(out_ref[here, :])
        gate = gate_ref[here, :]
        grad_mixed = mixed_ref[here, :]
        back_ref[here, :] = norm_back(grad_mixed * gate, normed, inverse).astype(bf16)
        grads_ref[here, :width] = (grad_mixed * normed * dsilu_ref[here, :width]).astype(bf16)
        mixed = normed * gate
        mixed_ref[here, :] = mixed
        keep_mixed_ref[here, :] = mixed.astype(bf16)
    mt_ref[...] = jnp.transpose(mixed_ref[...]).astype(bf16)

    def owner_order(ref, turn):
        start = (bal ^ turn) * part
        if part != groups * tables * unit:
            return ref[pl.ds(pl.multiple_of(start, part), part), :]
        found = []
        for group_step in range(groups):
            for table_step in range(tables):
                owner = (group_here ^ group_step) * tables + (table_here ^ table_step)
                at = pl.multiple_of(start + owner * unit, unit)
                found.append(ref[pl.ds(at, unit), :])
        return jnp.concatenate(found, axis=0)

    def emit_terms(ref, right, first):
        left = jnp.concatenate([owner_order(ref, turn) for turn in range(bals)], axis=0)
        found = matmul(left, right).astype(bf16)
        for turn in range(bals):
            rows_here = slice(turn * part, (turn + 1) * part)
            term_refs[turn][:, first : first + right.shape[1]] = found[rows_here]

    emit_terms(mt_ref, cot, features)

    for slot in range(slots):
        here = slice(slot * slot_rows, (slot + 1) * slot_rows)
        for pair in range(pairs):
            value, query, key = (part_of(slot, pair, which) for which in range(3))
            lanes = slice(pair * pair_width, (pair + 1) * pair_width)
            upper = split(back_ref[here, lanes])
            grad_weights = matmul_nt(upper, value)
            grad_scores = (grad_weights * slope_ref[slot * pairs + pair]).astype(bf16)
            grad_value = matmul_tn(weights_ref[slot * pairs + pair], upper)
            grad_query = matmul(side_by_side(grad_scores), split(key)) * score_scale
            grad_key = matmul_tn(grad_scores, split(query)) * score_scale
            for which, found in enumerate((grad_value, grad_query, grad_key)):
                first = (1 + which) * width + pair * pair_width
                at = slice(first, first + pair_width)
                grads_ref[here, at] = (found * dsilu_ref[here, at]).astype(bf16)

    emit_terms(nt_ref, grads_ref[...], 0)


def rows_kernel(groups, slots, bals, scalar_ref, *refs):
    refs = list(refs)
    take = lambda count: [refs.pop(0) for _ in range(count)]
    grads_ref, normed_ref, inverse_ref, mixed_ref, cot_ref = take(5)
    weight_refs, block_refs = take(bals), take(groups)
    (layer_ref,) = take(1)
    grad_refs = take(groups)
    x_ref, wide_ref, halves_ref = refs
    bal, group_here, _ = Scalars(scalar_ref, 0, bals, slots).place()
    features = grads_ref.shape[1]
    piece = grad_refs[0].shape[1]
    part = weight_refs[0].shape[0]
    for step in range(groups):
        x_ref[group_here ^ step] = block_refs[step][...]
    x = jnp.concatenate([x_ref[group] for group in range(groups)], axis=1).astype(f32)
    for index in range(bals):
        halves_ref[index] = mixed_ref[:, index * part : (index + 1) * part]
    for turn in range(bals):
        x = x + matmul(halves_ref[bal ^ turn], weight_refs[turn][:, features:])
    layer_ref[...] = x.astype(bf16)
    grad_normed = times_parts_nt(grads_ref[...], weight_refs, 0, features, bal, wide_ref)
    back = norm_back(grad_normed, normed_ref[...], inverse_ref[:, :1])
    grad_rows = (cot_ref[...] + back).astype(bf16)
    for group in range(groups):
        x_ref[group] = grad_rows[:, group * piece : (group + 1) * piece]
    for step in range(groups):
        grad_refs[step][...] = x_ref[group_here ^ step]


def pieces_kernel(bals, *refs):
    count = len(refs) - bals
    groups = (count + 1) // 2
    term_refs, grad_refs = refs[:bals], refs[bals : bals + groups - 1]
    out_refs = refs[bals + groups - 1 :]
    height, width = out_refs[0].shape
    for step, out in enumerate(out_refs):
        rows = slice(step * height, (step + 1) * height)
        total = term_refs[0][rows, :].astype(f32)
        for ref in term_refs[1:]:
            total = total + ref[rows, :].astype(f32)
        out[:, :width] = total.astype(bf16)
        if step:
            grad = grad_refs[step - 1]
            columns = grad.shape[1]
            for index in range(grad.shape[0] // height):
                at = width + index * columns
                out[:, at : at + columns] = grad[index * height : (index + 1) * height, :]


def place_kernel(scale, steps, slots, tables, bals, unit, table_scale, scalar_ref, *refs):
    pieces = refs[: len(steps)]
    *refs, scaled_ref, sems = refs[len(steps) :]
    if table_scale is None:
        in_ref, out_ref = refs[-2:]
    else:
        in_ref, out_ref, sum_ref = refs[-3:]
    _, group_here, table_here = Scalars(scalar_ref, 0, bals, slots).place()
    features = in_ref.shape[1]
    copies = []
    height = tables * unit
    for number, (group_step, piece) in enumerate(zip(steps, pieces)):
        for table_step in range(tables):
            to = pl.multiple_of(number * height + (table_here ^ table_step) * unit, unit)
            value = piece[table_step * unit : (table_step + 1) * unit, :]
            scaled_ref[pl.ds(to, unit), :] = value.astype(f32) * scale
        from_rows = scaled_ref.at[pl.ds(number * height, height), :]
        to = pl.ds(pl.multiple_of((group_here ^ group_step) * height, height), height)
        for index, (first, out) in enumerate(((0, in_ref), (features, out_ref))):
            copies.append(
                pltpu.make_async_copy(
                    from_rows.at[:, pl.ds(first, out.shape[1])], out.at[to, :], sems.at[number, index]
                )
            )
            copies[-1].start()
    if table_scale is not None:
        total = refs[0][0].astype(f32)
        for ref in refs[1:tables]:
            total = total + ref[...].astype(f32)
        sum_ref[...] = total * table_scale
    for copy in copies:
        copy.wait()


def sum_rounded(terms):
    total = terms[0].astype(f32)
    for term in terms[1:]:
        total = total + term.astype(f32)
    return total.astype(bf16)


def after(value, *others):
    return lax.optimization_barrier((value,) + others)[0]


def on_device(
    item_ids, seq_lengths, surplus_slot, helper_map, embed_tables, weight_in, weight_out, cotangent
):
    bal = lax.axis_index("bal")
    emb = lax.axis_index("emb")
    bals = lax.axis_size("bal")
    embs = lax.axis_size("emb")
    tables = item_ids.shape[2]
    groups = embs // tables
    _, rows, width = cotangent.shape
    slots = seq_lengths.shape[2]
    slot_rows = rows // slots
    distinct, columns = embed_tables.shape[1:]
    part = distinct // bals
    weight_part = weight_in.shape[0]
    table_here = emb // groups
    group_here = emb % groups
    width, features = weight_out.shape[1], weight_in.shape[1]
    unit = weight_part // embs
    owned = unit % 16 == 0
    unit = unit if owned else 0
    first = bals * (2 + slots)
    lane = lax.broadcasted_iota(jnp.int32, (1, LANES), 1)
    scalars = jnp.where(lane == first, bal, 0)
    scalars = jnp.where(lane == first + 1, group_here, scalars)
    scalars = jnp.where(lane == first + 2, table_here, scalars)
    fields = [surplus_slot.T, helper_map.T] + [seq_lengths[index] for index in range(bals)]
    at = 0
    for field in fields:
        width_here = field.shape[1]
        scalars = scalars + jnp.pad(field, ((0, 0), (at, LANES - at - width_here)))
        at += width_here

    share = lax.dynamic_slice_in_dim(embed_tables[0], bal * part, part, 0)
    fetched = [emb_swap(share, step * groups, embs) for step in range(1, tables)]

    ids = lax.dynamic_slice_in_dim(
        jnp.transpose(after(item_ids[0], share)), table_here * groups * rows, groups * rows, 1
    )
    plane_ids = with_swapped(ids.reshape(tables, groups * slots, 1, slot_rows), bals)
    wide_cot = cotangent[0].astype(f32)
    scalars = after(scalars, share)
    for bit in range((groups - 1).bit_length()):
        scalars = jnp.concatenate([scalars, emb_swap(scalars, 1 << bit, embs)], axis=0)
        scalars = after(scalars, wide_cot)

    fetched[0] = after(fetched[0], scalars)
    pieces = [piece for one in [share] + fetched for piece in with_swapped(one, bals)]

    found = pl.pallas_call(
        functools.partial(lookup_kernel, groups, slots, tables, bals),
        out_shape=[jax.ShapeDtypeStruct((rows, columns), bf16)] * groups,
        in_specs=[SMEM] + [VMEM] * (bals + len(pieces)),
        out_specs=[VMEM] * groups,
        cost_estimate=estimate(3),
        compiler_params=room(16),
    )(scalars, *plane_ids, *pieces)
    weights = jnp.concatenate([weight_in, weight_out], axis=1)
    weights = with_swapped(after(weights, found[0]), bals)
    block = [found[0]] + [emb_swap(found[step], step, embs) for step in range(1, groups)]

    pairs = slots * HEADS // 2
    terms = jax.ShapeDtypeStruct((weight_part, features + width), bf16)
    results = pl.pallas_call(
        functools.partial(layer_kernel, groups, slots, tables, bals, unit),
        out_shape=[jax.ShapeDtypeStruct((rows, features), bf16)]
        + [jax.ShapeDtypeStruct((rows, columns_here), f32) for columns_here in (width, LANES)]
        + [jax.ShapeDtypeStruct((rows, width), bf16)]
        + [terms] * bals,
        in_specs=[SMEM] + [VMEM] * (groups + bals + 1),
        out_specs=[VMEM] * (4 + bals),
        scratch_shapes=[
            pltpu.VMEM((groups, rows, columns), bf16),
            pltpu.VMEM((bals, rows, weight_part), bf16),
            pltpu.VMEM((bals, rows, weight_part), f32),
            pltpu.VMEM((width, rows), bf16),
            pltpu.VMEM((width, rows), bf16),
            pltpu.VMEM((pairs, 2 * slot_rows, slot_rows), bf16),
            pltpu.VMEM((pairs, 2 * slot_rows, slot_rows), f32),
            pltpu.VMEM((rows, width), f32),
            pltpu.VMEM((rows, features - width), bf16),
            pltpu.VMEM((rows, features), f32),
            pltpu.VMEM((rows, width), f32),
            pltpu.VMEM((rows, width), f32),
            pltpu.VMEM((rows, width), bf16),
        ],
        cost_estimate=estimate(7),
        compiler_params=room(36),
    )(scalars, *block[::-1], *weights, wide_cot)
    for_rows, results = results[:4], results[4:]
    layer_out, *grads = pl.pallas_call(
        functools.partial(rows_kernel, groups, slots, bals),
        out_shape=[jax.ShapeDtypeStruct((rows, width), bf16)]
        + [jax.ShapeDtypeStruct((rows, columns), bf16)] * groups,
        in_specs=[SMEM] + [VMEM] * (5 + bals + groups),
        out_specs=[VMEM] * (1 + groups),
        scratch_shapes=[
            pltpu.VMEM((groups, rows, columns), bf16),
            pltpu.VMEM((bals, rows, weight_part), f32),
            pltpu.VMEM((bals, rows, weight_part), bf16),
        ],
        cost_estimate=estimate(2),
        compiler_params=room(16),
    )(scalars, *for_rows, wide_cot, *weights, *block)

    def over_cores(parts):
        return sum_rounded([parts[0]] + [bal_swap(parts[turn], turn, bals) for turn in range(1, bals)])

    def to_plane(value):
        return [value] + [emb_swap(value, step, embs) for step in range(1, groups)]

    def table_sums(plane_grads):
        return pl.pallas_call(
            functools.partial(scatter_kernel, groups, slots, bals),
            out_shape=[jax.ShapeDtypeStruct((tables, part, columns), bf16)] * bals,
            in_specs=[SMEM] + [VMEM] * (bals + groups),
            out_specs=[VMEM] * bals,
            cost_estimate=estimate(3),
            compiler_params=room(16),
        )(scalars, *plane_ids, *plane_grads[::-1])

    grad_scale = (rows * embs * bals) ** -0.5
    if owned:
        height, wide = weight_part // groups, features + width
        terms = [results[0]] + [bal_swap(results[turn], turn, bals) for turn in range(1, bals)]
        pieces = pl.pallas_call(
            functools.partial(pieces_kernel, bals),
            out_shape=[jax.ShapeDtypeStruct((height, wide), bf16)]
            + [jax.ShapeDtypeStruct((height, wide + rows // height * columns), bf16)] * (groups - 1),
            in_specs=[VMEM] * (bals + groups - 1),
            out_specs=[VMEM] * groups,
            compiler_params=room(12),
        )(*terms, *grads[1:])
        came = [emb_swap(pieces[step], step, embs) for step in range(1, groups)]
        mine = sum_rounded([value[:, :wide] for value in came[::-1]] + [pieces[0]])
        mine = mine.reshape(tables, unit, wide)
        sums = table_sums([grads[0]] + came)
        own_sums = over_cores(sums)
        came = [emb_swap(mine[step], step * groups, embs) for step in range(1, tables)]
        final = sum_rounded(came[-1:] + came[:-1] + [mine[0]])
        gathered = [final] + [emb_swap(final, step * groups, embs) for step in range(1, tables)]
        back = to_plane(jnp.concatenate(gathered, axis=0))
        later = after(own_sums, *gathered[1:])
        swapped = [emb_swap(later[step], step * groups, embs) for step in range(1, tables)]
        swapped = [after(value, *back[1:]) for value in swapped]
    else:
        sums = table_sums([grads[0]] + [emb_swap(grads[step], step, embs) for step in range(1, groups)])
        own_sums = over_cores(sums)
        swapped = [emb_swap(own_sums[step], step * groups, embs) for step in range(1, tables)]
    table_scale = (distinct / (bals * item_ids.shape[1])) ** 0.5

    if owned:
        totals = []
        for steps in ([0] + list(range(groups - 1, 1, -1))[: groups // 2 - 1], None):
            steps = steps or [step for step in range(1, groups) if step not in done]
            done = steps
            extra = [own_sums] + swapped if totals else []
            sum_shape = [jax.ShapeDtypeStruct((part, columns), f32)] if totals else []
            sum_scale = table_scale if totals else None
            totals = pl.pallas_call(
                functools.partial(place_kernel, grad_scale, steps, slots, tables, bals, unit, sum_scale),
                out_shape=[
                    jax.ShapeDtypeStruct((weight_part, features), f32),
                    jax.ShapeDtypeStruct((weight_part, width), f32),
                ]
                + sum_shape,
                in_specs=[SMEM] + [VMEM] * (len(steps) + len(extra)) + [HBM] * len(totals),
                out_specs=[HBM] * 2 + [VMEM] * len(sum_shape),
                scratch_shapes=[
                    pltpu.VMEM((len(steps) * tables * unit, features + width), f32),
                    pltpu.SemaphoreType.DMA((len(steps), 2)),
                ],
                input_output_aliases={
                    1 + len(steps) + len(extra) + index: index for index in range(len(totals))
                },
                cost_estimate=estimate(1),
                compiler_params=room(12),
            )(scalars, *[back[step] for step in steps], *extra, *totals)
        total_in, total_out, table_sum = totals
    else:
        total = lax.psum(over_cores(results).astype(f32), "emb") * grad_scale
        total_in, total_out = total[:, :features], total[:, features:]
        table_sum = own_sums[0].astype(f32)
        for value in swapped:
            table_sum = table_sum + value.astype(f32)
        table_sum = table_sum * table_scale

    return layer_out[None], table_sum[None], total_in, total_out


def solution(mesh):
    placed = (
        P("bal", None, None),
        P(None, "emb", None),
        P(None, "emb"),
        P(None, "emb"),
        P("emb", None, None),
        P("bal", None),
        P("bal", None),
        P("bal", "emb", None),
    )
    return jax.shard_map(
        on_device,
        mesh=mesh,
        in_specs=placed,
        out_specs=(P("bal", "emb", None), P("emb", "bal", None), P("bal", None), P("bal", None)),
        check_vma=False,
    )
```
